32 devices in a mesh: dp: 4 (over y, x), context: 2 (over core), tensor: 4 (over z).
Axes of the slice: x: 2, y: 2, z: 4, core: 2. Of those that a mesh axis runs over, the one named last changes fastest.
Arguments:
- tokens: bfloat16 [4, 1024, 2048], P('dp', 'context'), may hold values from -6 to 6
- teacher: bfloat16 [4, 1024, 2048], P('dp', 'context'), may hold values from -6 to 6
- lengths: int32 [4], P('dp'), may hold values from 256 to 1024, as said below
- loss_mask: int32 [4, 1024], P('dp', 'context'), may hold values 0 or 1
- stretch_order: int32 [4, 4], P('dp'), may hold values from 0 to 3, each once within a row
- attn_gain: bfloat16 [2048], P(('dp', 'context')), may hold values from 0.099609375 to 1.8984375
- w_query: bfloat16 [2048, 2048], P(('dp', 'context'), 'tensor'), may hold values from -0.125 to 0.125
- w_key: bfloat16 [2048, 512], P(('dp', 'context'), 'tensor'), may hold values from -0.125 to 0.125
- w_value: bfloat16 [2048, 512], P(('dp', 'context'), 'tensor'), may hold values from -0.125 to 0.125
- w_out: bfloat16 [2048, 2048], P(('dp', 'context'), 'tensor'), may hold values from -2 to 2
- mlp_gain: bfloat16 [2048], P(('dp', 'context')), may hold values from 0.099609375 to 1.8984375
- w_gate: bfloat16 [2048, 8192], P(('dp', 'context'), 'tensor'), may hold values from -0.125 to 0.125
- w_up: bfloat16 [2048, 8192], P(('dp', 'context'), 'tensor'), may hold values from -0.125 to 0.125
- w_down: bfloat16 [2048, 8192], P(('dp', 'context'), 'tensor'), may hold values from -0.125 to 0.125
- first_moment: float32 [2048, 29696], P(('dp', 'context'), 'tensor'), may hold values from -0.0007324219 to 0.0007324219
- second_moment: float32 [2048, 29696], P(('dp', 'context'), 'tensor'), may hold values from 4.932466e-09 to 4.9324658e-08
- gain_first: float32 [2, 2048], P(None, ('dp', 'context')), may hold values from -0.0007324219 to 0.0007324219
- gain_second: float32 [2, 2048], P(None, ('dp', 'context')), may hold values from 4.932466e-09 to 4.9324658e-08
Outputs:
- block_out: bfloat16 [4, 1024, 2048], P('dp', 'context')
- grad_tokens: bfloat16 [4, 1024, 2048], P('dp', 'context')
- grad_attn_gain: float32 [2048], P(('dp', 'context'))
- grad_query: float32 [2048, 2048], P(('dp', 'context'), 'tensor')
- grad_key: float32 [2048, 512], P(('dp', 'context'), 'tensor')
- grad_value: float32 [2048, 512], P(('dp', 'context'), 'tensor')
- grad_out: float32 [2048, 2048], P(('dp', 'context'), 'tensor')
- grad_mlp_gain: float32 [2048], P(('dp', 'context'))
- grad_gate: float32 [2048, 8192], P(('dp', 'context'), 'tensor')
- grad_up: float32 [2048, 8192], P(('dp', 'context'), 'tensor')
- grad_down: float32 [2048, 8192], P(('dp', 'context'), 'tensor')
- adam_step: float32 [2048, 29696], P(('dp', 'context'), 'tensor')
- gain_step: float32 [2, 2048], P(None, ('dp', 'context'))
The draws below stay inside these ranges and needn't reach their ends.
Inputs may be any that keep to these rules, and one draw needn't show every extreme that they name: `lengths`: positions at or past a slot's length are padding: no query attends to them and they are not counted. One slot is full and another holds exactly 256 tokens. Each row orders the 4 stretches of 256 positions of its slot; stored rows b * 256 to (b + 1) * 256 - 1 hold positions stretch_order[s, b] * 256 onwards.
All inputs are finite; a program needn't handle non-finite values. No bound on the sum of `loss_mask` on one device may be relied on, other than what follows from the above.
Results may differ from the reference program's by a relative error of at most 0.0085.
The reference program's roundings to bfloat16 on the way count: a program that leaves them out, or rounds other values in their place, can miss the bound.
Values may be sent and summed in bfloat16 or wider, within the bound.
A program may use at most 320 MiB of HBM per device.

```python
import functools
import math
import jax
import jax.numpy as jnp
from jax import lax

D = 2048
H = 32
KVH = 8
HD = 64
FF = 8192
STEP = 10
SLOTS = 4
SLOT_LEN = 1024
STRETCHES = 4
PACK = 29696
PARAMS = 60821504
N_CONTEXT = 2
N_TENSOR = 4


def draw_lengths(key, part):
    key_values, key_order = jax.random.split(jax.random.fold_in(key, 11))
    drawn_lengths = jax.random.randint(key_values, (SLOTS,), SLOT_LEN // 4, SLOT_LEN + 1)
    slot_order = jax.random.permutation(key_order, SLOTS)
    slot_index = jnp.arange(SLOTS)
    drawn_lengths = jnp.where(slot_index == slot_order[0], SLOT_LEN, drawn_lengths)
    drawn_lengths = jnp.where(slot_index == slot_order[1], SLOT_LEN // 4, drawn_lengths)
    return drawn_lengths.astype(jnp.int32)


def place_ends(array, key, smallest, high):
    extent = array.shape
    place = [jax.random.randint(jax.random.fold_in(key, axis), (), 0, extent[axis]) for axis in range(len(extent))]
    array = array.at[tuple(place)].set(smallest)
    longest = extent.index(max(extent))
    place[longest] = (place[longest] + 1) % extent[longest]
    return array.at[tuple(place)].set(high)


def block_scale(key, extent, shards, low, high):
    level, own = 1.0, jax.random.fold_in(key, 6)
    for dim, shards_of in shards:
        steps = jnp.exp(jax.random.uniform(jax.random.fold_in(own, dim), (shards_of,), jnp.float32, low / len(shards), high / len(shards)))
        level = level * jnp.repeat(steps, extent[dim] // shards_of).reshape([-1 if axis == dim else 1 for axis in range(len(extent))])
    return level


def gaussian(key, dims, deviation, bound, cuts=(), kind=jnp.bfloat16):
    array = deviation * jax.random.normal(key, dims, jnp.float32)
    if cuts:
        array = array * block_scale(key, dims, cuts, -0.22, 0.18)
    return jnp.clip(array, -bound, bound).astype(kind)


def setup_inputs(seed: int = 0) -> dict:
    seeds = jax.random.split(jax.random.key(seed), 19)
    return {
        "tokens": gaussian(seeds[0], (SLOTS, SLOT_LEN, D), 1.0, 6.0, ((0, 4), (1, 2))),
        "teacher": gaussian(seeds[1], (SLOTS, SLOT_LEN, D), 1.0, 6.0, ((0, 4), (1, 2))),
        "lengths": draw_lengths(jax.random.fold_in(seeds[18], 71), 0),
        "loss_mask": place_ends((jax.random.randint(seeds[3], (SLOTS, SLOT_LEN), 0, 8) < 7).astype(jnp.int32), jax.random.fold_in(seeds[3], 1), 0, 1),
        "stretch_order": jax.vmap(lambda own: jax.random.permutation(own, STRETCHES))(jax.random.split(seeds[4], SLOTS)).reshape((SLOTS, STRETCHES)).astype(jnp.int32),
        "attn_gain": jnp.clip(1.0 + 0.18 * jax.random.normal(seeds[5], (D,), jnp.float32), 0.099609375, 1.8984375).astype(jnp.bfloat16),
        "w_query": gaussian(seeds[6], (D, H * HD), D ** -0.5, 0.125, ((0, 8), (1, 4))),
        "w_key": gaussian(seeds[7], (D, KVH * HD), D ** -0.5, 0.125, ((0, 8), (1, 4))),
        "w_value": gaussian(seeds[8], (D, KVH * HD), D ** -0.5, 0.125, ((0, 8), (1, 4))),
        "w_out": gaussian(seeds[9], (D, H * HD), (max(H * HD // 256, 2)) ** -0.5, 2.0, ((0, 8), (1, 4))),
        "mlp_gain": jnp.clip(1.0 + 0.18 * jax.random.normal(seeds[10], (D,), jnp.float32), 0.099609375, 1.8984375).astype(jnp.bfloat16),
        "w_gate": gaussian(seeds[11], (D, FF), D ** -0.5, 0.125, ((0, 8), (1, 4))),
        "w_up": gaussian(seeds[12], (D, FF), D ** -0.5, 0.125, ((0, 8), (1, 4))),
        "w_down": gaussian(seeds[13], (D, FF), (FF // 4) ** -0.5, 0.125, ((0, 8), (1, 4))),
        "first_moment": gaussian(seeds[14], (D, PACK), (PARAMS ** -0.5), 0.0007324219, ((0, 8), (1, 4)), jnp.float32),
        "second_moment": jnp.clip(jnp.exp(math.log(4.9324658135674326e-08) - 2.3025851 * jax.random.uniform(seeds[15], (D, PACK), jnp.float32) ** block_scale(seeds[15], (D, PACK), ((0, 8), (1, 4)), -0.2, 0.2)), 4.9324659912031166e-09, 4.9324658135674326e-08),
        "gain_first": gaussian(seeds[16], (2, D), (PARAMS ** -0.5), 0.0007324219, ((1, 8),), jnp.float32),
        "gain_second": jnp.clip(jnp.exp(math.log(4.9324658135674326e-08) - 2.3025851 * jax.random.uniform(seeds[17], (2, D), jnp.float32) ** block_scale(seeds[17], (2, D), ((1, 8),), -0.2, 0.2)), 4.9324659912031166e-09, 4.9324658135674326e-08),
    }


@jax.custom_vjp
def low(v):
    return lax.optimization_barrier(v.astype(jnp.bfloat16)).astype(jnp.float32)

@jax.custom_vjp
def low_back(v):
    return v

def low_keep(v):
    return (low(v), None)

def low_pass(kept, grad):
    return (grad,)

def back_keep(v):
    return (v, None)

def back_low(kept, grad):
    return (low(grad),)
low.defvjp(low_keep, low_pass)
low_back.defvjp(back_keep, back_low)
EPS_NORM = 1e-05
ROPE_BASE = 500000.0
OLD_CONTEXT = 8192.0
SCALE_FACTOR = 32.0
LOW_FACTOR = 1.0
HIGH_FACTOR = 4.0
LOG2E = 1.4426950408889634
NEG_FILL = -1e+30
BETA_ONE = 0.9
BETA_TWO = 0.95
ADAM_EPS = 1e-08
CLIP_NORM = 1.0

def frequencies():
    channel = jnp.arange(HD // 2, dtype=jnp.float32)
    base_freq = jnp.power(jnp.float32(ROPE_BASE), -2.0 * channel / HD)
    wavelength = 2.0 * math.pi / base_freq
    smooth = (OLD_CONTEXT / wavelength - LOW_FACTOR) / (HIGH_FACTOR - LOW_FACTOR)
    blended = (1.0 - smooth) * base_freq / SCALE_FACTOR + smooth * base_freq
    slow_freq = jnp.where(wavelength > OLD_CONTEXT / LOW_FACTOR, base_freq / SCALE_FACTOR, blended)
    return jnp.where(wavelength < OLD_CONTEXT / HIGH_FACTOR, base_freq, slow_freq)

def rotate(values, cosine, sine_table):
    middle = values.shape[-1] // 2
    first_half = values[..., :middle]
    second_half = values[..., middle:]
    return jnp.concatenate([first_half * cosine - second_half * sine_table, second_half * cosine + first_half * sine_table], axis=-1)

def normalize(values, gain):
    factor = lax.rsqrt(lax.optimization_barrier(jnp.mean(values * values, axis=-1, keepdims=True)) + EPS_NORM)
    return values * factor * gain.astype(jnp.float32)

def head_block(allowed, score_scale, head_inputs):
    head_query, head_key, head_value = head_inputs
    highest = lax.Precision.HIGHEST
    scores = low_back(jnp.einsum('qgd,nd->gqn', head_query, head_key, precision=highest) * score_scale)
    lifted = jnp.where(allowed[None], scores * LOG2E, NEG_FILL)
    ceiling = jnp.floor(lax.optimization_barrier(jnp.max(lifted, axis=-1, keepdims=True)))
    expo_all = jnp.where(allowed[None], jnp.exp2(lifted - ceiling), 0.0)
    weight_sum = lax.optimization_barrier(jnp.sum(expo_all, axis=-1))
    mixed = jnp.einsum('gqn,nd->gqd', low(expo_all), head_value, precision=highest)
    return mixed / weight_sum[..., None]

def layer_forward(params, inputs, positions, slot_length):
    gain_one, weight_query, weight_key, weight_value, weight_out, gain_two, weight_gate, weight_up, weight_down = params
    highest = lax.Precision.HIGHEST
    seq_len = inputs.shape[0]
    group_size = H // KVH
    score_scale = float(HD) ** (-0.5)
    angles = positions.astype(jnp.float32)[:, None] * frequencies()[None, :]
    cosine = jnp.cos(angles)[:, None, :]
    sine_table = jnp.sin(angles)[:, None, :]
    allowed = (positions[None, :] <= positions[:, None]) & (positions < slot_length)[None, :]
    normed = low(normalize(inputs, gain_one))
    query_lin = low_back(jnp.dot(normed, weight_query, precision=highest))
    key_lin = low_back(jnp.dot(normed, weight_key, precision=highest))
    value_lin = low(low_back(jnp.dot(normed, weight_value, precision=highest)))
    query_rot = low(rotate(query_lin.reshape(seq_len, H, HD), cosine, sine_table))
    key_rot = low(rotate(key_lin.reshape(seq_len, KVH, HD), cosine, sine_table))
    query_heads = jnp.transpose(query_rot.reshape(seq_len, KVH, group_size, HD), (1, 0, 2, 3))
    key_heads = jnp.transpose(key_rot, (1, 0, 2))
    value_heads = jnp.transpose(value_lin.reshape(seq_len, KVH, HD), (1, 0, 2))
    mixed = lax.map(jax.checkpoint(functools.partial(head_block, allowed, score_scale)), (query_heads, key_heads, value_heads))
    attended = low(low_back(jnp.transpose(mixed, (2, 0, 1, 3)).reshape(seq_len, H * HD)))
    branch = low_back(jnp.dot(attended, weight_out.T, precision=highest))
    state = inputs + branch
    normed_two = low(normalize(state, gain_two))
    gate_proj = low_back(jnp.dot(normed_two, weight_gate, precision=highest))
    up_proj = low_back(jnp.dot(normed_two, weight_up, precision=highest))
    product = low(jax.nn.silu(gate_proj) * up_proj)
    ffn = low_back(jnp.dot(product, weight_down.T, precision=highest))
    return state + ffn

def pack_columns(matrices):
    pieces = [matrix.reshape(D, N_TENSOR, matrix.shape[1] // N_TENSOR) for matrix in matrices]
    return jnp.concatenate(pieces, axis=2).reshape(D, PACK)

def adam_direction(gradient, first, second, clip_factor):
    clipped = gradient * clip_factor
    first_new = BETA_ONE * first + (1.0 - BETA_ONE) * clipped
    second_new = BETA_TWO * second + (1.0 - BETA_TWO) * clipped * clipped
    return first_new / (1.0 - BETA_ONE ** STEP) / (jnp.sqrt(second_new / (1.0 - BETA_TWO ** STEP)) + ADAM_EPS)

def reference(tokens, teacher, lengths, loss_mask, stretch_order, attn_gain, w_query, w_key, w_value, w_out, mlp_gain, w_gate, w_up, w_down, first_moment, second_moment, gain_first, gain_second):
    half_len = SLOT_LEN // (2 * N_CONTEXT)
    row_index = jnp.arange(SLOT_LEN, dtype=jnp.int32)
    stretch_ids = jnp.take(stretch_order, row_index // half_len, axis=1)
    positions = (stretch_ids * half_len + row_index % half_len).astype(jnp.int32)
    valid = ((loss_mask == 1) & (positions < lengths[:, None])).astype(jnp.float32)
    valid_count = jnp.sum(valid)
    loss_scale = jnp.float32(SLOTS * SLOT_LEN) / valid_count
    params = tuple((weight_arg.astype(jnp.float32) for weight_arg in (attn_gain, w_query, w_key, w_value, w_out, mlp_gain, w_gate, w_up, w_down)))

    def slot_step(totals, slot_data):
        inputs, target, slot_pos, slot_length, slot_valid = slot_data

        def loss_fn(layer_input, weights):
            output = layer_forward(weights, layer_input, slot_pos, slot_length)
            residual_gap = output - target
            return (loss_scale * 0.5 * jnp.sum(slot_valid[:, None] * residual_gap * residual_gap), output)
        loss_value, pullback, output = jax.vjp(loss_fn, inputs, params, has_aux=True)
        grad_inputs, grad_weights = pullback(jnp.ones_like(loss_value))
        totals = tuple((total_now + grad_now for total_now, grad_now in zip(totals, grad_weights)))
        return (totals, (output.astype(jnp.bfloat16), grad_inputs.astype(jnp.bfloat16)))
    start_totals = tuple((jnp.zeros_like(weight_arg) for weight_arg in params))
    grad_totals, (block_out, grad_tokens) = lax.scan(slot_step, start_totals, (tokens.astype(jnp.float32), teacher.astype(jnp.float32), positions, lengths, valid))
    square_sum = sum((jnp.sum(grad_now * grad_now) for grad_now in grad_totals))
    clip_factor = CLIP_NORM / jnp.maximum(jnp.sqrt(square_sum), CLIP_NORM)
    grad_attn_gain, grad_query, grad_key, grad_value, grad_out, grad_mlp_gain, grad_gate, grad_up, grad_down = grad_totals
    packed = pack_columns((grad_query, grad_key, grad_value, grad_out, grad_gate, grad_up, grad_down))
    adam_step = adam_direction(packed, first_moment, second_moment, clip_factor)
    gain_step = adam_direction(jnp.stack([grad_attn_gain, grad_mlp_gain]), gain_first, gain_second, clip_factor)
    return (block_out, grad_tokens, grad_attn_gain, grad_query, grad_key, grad_value, grad_out, grad_mlp_gain, grad_gate, grad_up, grad_down, adam_step, gain_step)
```

```python
import functools
import math

import jax
import jax.numpy as jnp
from jax import lax
from jax.experimental import pallas as pl
from jax.experimental.pallas import tpu as pltpu
from jax.sharding import PartitionSpec as P

HD = 64
STEP = 10


EPS_NORM = 1e-05
ROPE_BASE = 500000.0
OLD_CONTEXT = 8192.0
SCALE_FACTOR = 32.0
LOW_FACTOR = 1.0
HIGH_FACTOR = 4.0
LOG2E = 1.4426950408889634
NEG_FILL = -1e30
BETA_ONE = 0.9
BETA_TWO = 0.95
ADAM_EPS = 1e-08
CLIP_NORM = 1.0


def frequencies():
    channel = jnp.arange(HD // 2, dtype=jnp.float32)
    base_freq = jnp.power(jnp.float32(ROPE_BASE), -2.0 * channel / HD)
    wavelength = 2.0 * math.pi / base_freq
    smooth = (OLD_CONTEXT / wavelength - LOW_FACTOR) / (HIGH_FACTOR - LOW_FACTOR)
    blended = (1.0 - smooth) * base_freq / SCALE_FACTOR + smooth * base_freq
    slow_freq = jnp.where(wavelength > OLD_CONTEXT / LOW_FACTOR, base_freq / SCALE_FACTOR, blended)
    return jnp.where(wavelength < OLD_CONTEXT / HIGH_FACTOR, base_freq, slow_freq)


def rotate(values, cosine, sine_table):
    middle = values.shape[-1] // 2
    first_half = values[..., :middle]
    second_half = values[..., middle:]
    return jnp.concatenate(
        [
            first_half * cosine - second_half * sine_table,
            second_half * cosine + first_half * sine_table,
        ],
        axis=-1,
    )


def normalize(values, gain):
    factor = lax.rsqrt(jnp.mean(values * values, axis=-1, keepdims=True) + EPS_NORM)
    return values * factor * gain.astype(jnp.float32)


def normalize_back(values, gain, upstream):
    factor = lax.rsqrt(jnp.mean(values * values, axis=-1, keepdims=True) + EPS_NORM)
    unit_rows = values * factor
    gain_grad = jnp.sum(upstream * unit_rows, axis=0)
    scaled_up = upstream * gain.astype(jnp.float32)
    input_grad = factor * (
        scaled_up - unit_rows * jnp.mean(scaled_up * unit_rows, axis=-1, keepdims=True)
    )
    return (input_grad, gain_grad)


def positions_of(order_table, row_index, half_len):
    stretch_slot = row_index // half_len
    matches = stretch_slot[:, None] == jnp.arange(order_table.shape[1], dtype=jnp.int32)[None, :]
    stretch_ids = jnp.sum(jnp.where(matches[None, :, :], order_table[:, None, :], 0), axis=-1)
    return stretch_ids * half_len + row_index % half_len


def allowed_mask(query_pos, key_pos, lengths):
    causal = key_pos[:, None, :] <= query_pos[:, :, None]
    inside = (key_pos < lengths[:, None])[:, None, :]
    return (causal & inside)[:, None, None, :, :]


def add_rows(target_rows, term, position):
    current_rows = lax.dynamic_slice_in_dim(target_rows, position, term.shape[1], 1)
    return lax.dynamic_update_slice_in_dim(target_rows, current_rows + term, position, 1)


def times_transpose(left, right):
    return lax.dot_general(
        left, right, (((1,), (1,)), ((), ())), preferred_element_type=jnp.float32
    )


def column_term(left, right):
    return lax.dot_general(
        left, right, (((0,), (0,)), ((), ())), preferred_element_type=jnp.float32
    )


def adam_direction(gradient, first, second, clip_factor):
    clipped = gradient * clip_factor
    first_new = BETA_ONE * first + (1.0 - BETA_ONE) * clipped
    second_new = BETA_TWO * second + (1.0 - BETA_TWO) * clipped * clipped
    return (
        first_new
        / (1.0 - BETA_ONE**STEP)
        / (jnp.sqrt(second_new / (1.0 - BETA_TWO**STEP)) + ADAM_EPS)
    )


def forward_fold(query_blocks, query_pos, lengths, stretch_order, half_len, score_scale):

    def forward_fold_keys(state_now, shard_piece, start_row):
        key_piece, value_piece = shard_piece
        piece_len = key_piece.shape[1]
        block_len = math.gcd(piece_len, 512)
        key_pos = positions_of(stretch_order, jnp.arange(piece_len, dtype=jnp.int32), half_len)

        def forward_inner_step(block_index, state_in):
            first_row = block_index * block_len
            block_keys = lax.dynamic_slice_in_dim(key_piece, first_row, block_len, 1)
            block_values = lax.dynamic_slice_in_dim(value_piece, first_row, block_len, 1)
            allowed = allowed_mask(
                query_pos, lax.dynamic_slice_in_dim(key_pos, first_row, block_len, 1), lengths
            )
            totals, weights, ceiling = state_in
            scores = (
                jnp.einsum(
                    "sqkgd,snkd->skgqn",
                    query_blocks,
                    block_keys,
                    preferred_element_type=jnp.float32,
                )
                * score_scale
            )
            lifted = jnp.where(allowed, scores * LOG2E, NEG_FILL)
            new_ceiling = jnp.maximum(ceiling, jnp.floor(jnp.max(lifted, axis=-1)))
            expo_block = jnp.where(allowed, jnp.exp2(lifted - new_ceiling[..., None]), 0.0)
            shrink = jnp.exp2(ceiling - new_ceiling)
            weights_next = weights * shrink + jnp.sum(expo_block, axis=-1)
            totals_next = totals * shrink[..., None] + jnp.einsum(
                "skgqn,snkd->skgqd",
                expo_block.astype(jnp.bfloat16),
                block_values,
                preferred_element_type=jnp.float32,
            )
            return (totals_next, weights_next, new_ceiling)

        return lax.fori_loop(0, piece_len // block_len, forward_inner_step, state_now)

    return forward_fold_keys


def backward_fold(
    query_blocks,
    grad_heads,
    scaled_grad,
    delta,
    ceiling,
    weights,
    query_pos,
    lengths,
    stretch_order,
    half_len,
    score_scale,
):

    def backward_fold_keys(state_now, shard_piece, start_row):
        key_piece, value_piece = shard_piece
        piece_len = key_piece.shape[1]
        block_len = math.gcd(piece_len, 512)
        key_pos = positions_of(stretch_order, jnp.arange(piece_len, dtype=jnp.int32), half_len)

        def backward_inner_step(block_index, state_in):
            first_row = block_index * block_len
            block_keys = lax.dynamic_slice_in_dim(key_piece, first_row, block_len, 1)
            block_values = lax.dynamic_slice_in_dim(value_piece, first_row, block_len, 1)
            allowed = allowed_mask(
                query_pos, lax.dynamic_slice_in_dim(key_pos, first_row, block_len, 1), lengths
            )
            grad_query, grad_keys, grad_values = state_in
            scores = (
                jnp.einsum(
                    "sqkgd,snkd->skgqn",
                    query_blocks,
                    block_keys,
                    preferred_element_type=jnp.float32,
                )
                * score_scale
            )
            lifted = jnp.where(allowed, scores * LOG2E, NEG_FILL)
            expo_block = jnp.where(allowed, jnp.exp2(lifted - ceiling[..., None]), 0.0)
            probs = expo_block / weights[..., None]
            grad_probs = jnp.einsum(
                "sqkgd,snkd->skgqn", grad_heads, block_values, preferred_element_type=jnp.float32
            )
            grad_scores = (probs * (grad_probs - delta[..., None])).astype(jnp.bfloat16)
            grad_query = (
                grad_query
                + jnp.einsum(
                    "skgqn,snkd->sqkgd", grad_scores, block_keys, preferred_element_type=jnp.float32
                )
                * score_scale
            )
            key_term = (
                jnp.einsum(
                    "skgqn,sqkgd->snkd",
                    grad_scores,
                    query_blocks,
                    preferred_element_type=jnp.float32,
                )
                * score_scale
            )
            value_term = jnp.einsum(
                "skgqn,skgqd->snkd",
                expo_block.astype(jnp.bfloat16).astype(jnp.float32),
                scaled_grad,
                preferred_element_type=jnp.float32,
                precision=lax.Precision.HIGHEST,
            )
            return (
                grad_query,
                add_rows(grad_keys, key_term, first_row),
                add_rows(grad_values, value_term, first_row),
            )

        return lax.fori_loop(0, piece_len // block_len, backward_inner_step, state_now)

    return backward_fold_keys


MESH_ID = pl.DeviceIdType.MESH


def row_mean(values):
    return jnp.mean(values, axis=-1, keepdims=True)


def line_body(n_line, steps, finish, extra_count, kept_count, *refs):
    part = refs[0]
    extra = refs[1 : 1 + extra_count]
    out = refs[1 + extra_count]
    kept = refs[2 + extra_count : 2 + extra_count + kept_count]
    (
        from_left,
        from_right,
        total,
        done,
        sum_send_right,
        sum_send_left,
        sum_recv_left,
        sum_recv_right,
        out_send_right,
        out_send_left,
        out_recv,
        own_sem,
    ) = refs[2 + extra_count + kept_count :]
    place = lax.axis_index("tensor")
    last = n_line - 1
    right = {"tensor": jnp.minimum(place + 1, last)}
    left = {"tensor": jnp.maximum(place - 1, 0)}
    share = part.shape[0] // n_line
    rows = share // steps
    has_left = place > 0
    has_right = place < last

    def span(owner, step):
        return pl.ds(pl.multiple_of(owner * share + step * rows, rows), rows)

    barrier = pltpu.get_barrier_semaphore()

    @pl.when(has_left)
    def _():
        pl.semaphore_signal(barrier, inc=1, device_id=left, device_id_type=MESH_ID)

    @pl.when(has_right)
    def _():
        pl.semaphore_signal(barrier, inc=1, device_id=right, device_id_type=MESH_ID)

    pl.semaphore_wait(barrier, has_left.astype(jnp.int32) + has_right.astype(jnp.int32))

    def sum_right(src, owner, step):
        return pltpu.make_async_remote_copy(
            src_ref=src,
            dst_ref=from_left.at[owner, step],
            send_sem=sum_send_right.at[owner, step],
            recv_sem=sum_recv_left.at[owner, step],
            device_id=right,
            device_id_type=MESH_ID,
        )

    def sum_left(src, owner, step):
        return pltpu.make_async_remote_copy(
            src_ref=src,
            dst_ref=from_right.at[owner, step],
            send_sem=sum_send_left.at[owner, step],
            recv_sem=sum_recv_right.at[owner, step],
            device_id=left,
            device_id_type=MESH_ID,
        )

    def hand(src, owner, step, sems, hop, target):
        return pltpu.make_async_remote_copy(
            src_ref=src,
            dst_ref=out.at[span(owner, step)],
            send_sem=sems.at[hop, step],
            recv_sem=out_recv.at[owner, step],
            device_id=target,
            device_id_type=MESH_ID,
        )

    def pass_on(step):
        for hop in range(1, n_line):

            @pl.when(place >= hop)
            def _():
                owner = place - hop
                hand(
                    out.at[span(owner, step)], owner, step, out_send_right, hop, right
                ).wait_recv()

                @pl.when(has_right)
                def _():
                    hand(
                        out.at[span(owner, step)], owner, step, out_send_right, hop, right
                    ).start()

            @pl.when(place + hop <= last)
            def _():
                owner = place + hop
                hand(
                    out.at[span(owner, step)], owner, step, out_send_left, hop, left
                ).wait_recv()

                @pl.when(has_left)
                def _():
                    hand(
                        out.at[span(owner, step)], owner, step, out_send_left, hop, left
                    ).start()

    for step in range(steps):
        for hop in range(last):

            @pl.when(place == 0)
            def _():
                sum_right(part.at[span(last - hop, step)], last - hop, step).start()

            @pl.when(place == last)
            def _():
                sum_left(part.at[span(hop, step)], hop, step).start()

    for step in range(steps):
        for hop in range(last):
            far_right, far_left = last - hop, hop

            @pl.when((place > 0) & (place < far_right))
            def _():
                slot = from_left.at[far_right, step]
                sum_right(slot, far_right, step).wait_recv()
                slot[...] = (
                    slot[...].astype(jnp.float32)
                    + part[span(far_right, step), :].astype(jnp.float32)
                ).astype(jnp.bfloat16)
                sum_right(slot, far_right, step).start()

            @pl.when((place < last) & (place > far_left))
            def _():
                slot = from_right.at[far_left, step]
                sum_left(slot, far_left, step).wait_recv()
                slot[...] = (
                    slot[...].astype(jnp.float32)
                    + part[span(far_left, step), :].astype(jnp.float32)
                ).astype(jnp.bfloat16)
                sum_left(slot, far_left, step).start()

        own = span(place, step)
        total[...] = part[own, :].astype(jnp.float32)

        @pl.when(has_left)
        def _():
            slot = from_left.at[place, step]
            sum_right(slot, place, step).wait_recv()
            total[...] += slot[...].astype(jnp.float32)

        @pl.when(has_right)
        def _():
            slot = from_right.at[place, step]
            sum_left(slot, place, step).wait_recv()
            total[...] += slot[...].astype(jnp.float32)

        finish(total[...], own, pl.ds(step * rows, rows), step, done, extra, kept)
        pltpu.make_async_copy(done.at[step], out.at[own], own_sem.at[step]).start()

        @pl.when(has_right)
        def _():
            hand(done.at[step], place, step, out_send_right, 0, right).start()

        @pl.when(has_left)
        def _():
            hand(done.at[step], place, step, out_send_left, 0, left).start()

        if step > 0:
            pass_on(step - 1)
    pass_on(steps - 1)

    for step in range(steps):
        pltpu.make_async_copy(done.at[step], out.at[span(place, step)], own_sem.at[step]).wait()
        for owner in range(n_line):

            @pl.when(place < owner)
            def _():
                sum_right(from_left.at[owner, step], owner, step).wait_send()

            @pl.when(place > owner)
            def _():
                sum_left(from_right.at[owner, step], owner, step).wait_send()

        for hop in range(n_line):

            @pl.when((place >= hop) & has_right)
            def _():
                hand(done.at[step], place, step, out_send_right, hop, right).wait_send()

            @pl.when((place + hop <= last) & has_left)
            def _():
                hand(done.at[step], place, step, out_send_left, hop, left).wait_send()


def line_sum(finish, part, extra, kept, which, n_line, steps=2):
    total_rows, width = part.shape
    rows = total_rows // n_line // steps
    in_vmem = pl.BlockSpec(memory_space=pltpu.VMEM)
    return pl.pallas_call(
        functools.partial(line_body, n_line, steps, finish, len(extra), len(kept)),
        out_shape=[jax.ShapeDtypeStruct((total_rows, width), jnp.bfloat16)] + kept,
        in_specs=[in_vmem] * (1 + len(extra)),
        out_specs=[pl.BlockSpec(memory_space=pl.ANY)] + [in_vmem] * len(kept),
        scratch_shapes=[
            pltpu.VMEM((n_line, steps, rows, width), jnp.bfloat16),
            pltpu.VMEM((n_line, steps, rows, width), jnp.bfloat16),
            pltpu.VMEM((rows, width), jnp.float32),
            pltpu.VMEM((steps, rows, width), jnp.bfloat16),
        ]
        + [pltpu.SemaphoreType.DMA((n_line, steps))] * 7
        + [pltpu.SemaphoreType.DMA((steps,))],
        compiler_params=pltpu.CompilerParams(
            collective_id=which, has_side_effects=True, vmem_limit_bytes=48 << 20
        ),
        cost_estimate=pl.CostEstimate(
            flops=20 * total_rows * width,
            bytes_accessed=30 * total_rows * width,
            transcendentals=total_rows,
        ),
    )(part, *extra)


def finish_branch(total, own, local, step, done, extra, kept):
    tokens, gain = extra
    (state,) = kept
    rows_now = tokens[own, :].astype(jnp.float32) + total
    state[local, :] = rows_now
    done[step] = normalize(rows_now, gain[...]).astype(jnp.bfloat16)


def finish_output(total, own, local, step, done, extra, kept):
    state, teacher, factor = extra
    output_low, grad_output = kept
    output = state[local, :] + total
    output_low[local, :] = output.astype(jnp.bfloat16)
    grad_now = factor[own, :] * (output - teacher[own, :].astype(jnp.float32))
    grad_output[local, :] = grad_now
    done[step] = grad_now.astype(jnp.bfloat16)


def finish_ffn_back(total, own, local, step, done, extra, kept):
    state, grad_output, gain = extra
    grad_state, gain_grad = kept
    input_grad, gain_now = normalize_back(state[local, :], gain[...], total)
    grad_now = grad_output[local, :] + input_grad
    grad_state[local, :] = grad_now
    gain_grad[step : step + 1, :] = gain_now[None, :]
    done[step] = grad_now.astype(jnp.bfloat16)


def finish_attn_back(total, own, local, step, done, extra, kept):
    tokens, grad_state, gain = extra
    (gain_grad,) = kept
    input_grad, gain_now = normalize_back(tokens[own, :].astype(jnp.float32), gain[...], total)
    gain_grad[step : step + 1, :] = gain_now[None, :]
    done[step] = (grad_state[local, :] + input_grad).astype(jnp.bfloat16)


def on_device(
    tokens,
    teacher,
    lengths,
    loss_mask,
    stretch_order,
    attn_gain,
    w_query,
    w_key,
    w_value,
    w_out,
    mlp_gain,
    w_gate,
    w_up,
    w_down,
    first_moment,
    second_moment,
    gain_first,
    gain_second,
):
    slot_count, stretch_len, model_width = tokens.shape
    token_rows = slot_count * stretch_len
    half_len = stretch_len // 2
    slot_len = stretch_len * lax.axis_size("context")
    all_rows = slot_count * lax.axis_size("dp") * slot_len
    n_line = lax.axis_size("tensor")
    steps = 2
    share_rows = token_rows // n_line
    local_index = stretch_len * lax.axis_index("context") + jnp.arange(stretch_len, dtype=jnp.int32)
    query_pos = positions_of(stretch_order, local_index, half_len)
    valid = ((loss_mask == 1) & (query_pos < lengths[:, None])).astype(jnp.float32)
    valid_here = jnp.sum(valid)
    count_high = jnp.floor(valid_here / 64.0)
    count_low = valid_here - 64.0 * count_high
    shard_rows = attn_gain.shape[0]
    side = jnp.concatenate(
        [
            attn_gain[:, None],
            mlp_gain[:, None],
            jnp.full((shard_rows, 1), count_high, jnp.bfloat16),
            jnp.full((shard_rows, 1), count_low, jnp.bfloat16),
            jnp.zeros((shard_rows, 124), jnp.bfloat16),
        ],
        axis=1,
    )
    whole = functools.partial(lax.all_gather, axis_name=("dp", "context"), axis=0, tiled=True)
    q_cols, k_cols = w_query.shape[1], w_key.shape[1]
    first_pack = whole(jnp.concatenate([w_query, w_key, w_value, side], axis=1))
    full_out = whole(w_out)
    full_gate = whole(w_gate)
    full_up = whole(w_up)
    full_down = whole(w_down)
    full_qkv = first_pack[:, : q_cols + 2 * k_cols]
    gain_one = first_pack[:, q_cols + 2 * k_cols]
    gain_two = first_pack[:, q_cols + 2 * k_cols + 1]
    counts = first_pack[::shard_rows, q_cols + 2 * k_cols + 2 : q_cols + 2 * k_cols + 4]
    counts = counts.astype(jnp.float32)
    valid_count = jnp.sum(counts[:, 0] * 64.0 + counts[:, 1])
    head_count = q_cols // HD
    kv_count = k_cols // HD
    group_size = head_count // kv_count
    score_scale = float(HD) ** (-0.5)
    angles = query_pos.reshape(token_rows).astype(jnp.float32)[:, None] * frequencies()[None, :]
    cosine = jnp.cos(angles)[:, None, :]
    sine_table = jnp.sin(angles)[:, None, :]
    token_rows_low = tokens.reshape(token_rows, model_width)
    inputs = token_rows_low.astype(jnp.float32)
    normed = normalize(inputs, gain_one).astype(jnp.bfloat16)
    lin = jnp.dot(normed, full_qkv, preferred_element_type=jnp.float32)
    query_lin = lin[:, :q_cols]
    key_lin = lin[:, q_cols : q_cols + k_cols]
    value_low = lin[:, q_cols + k_cols :].astype(jnp.bfloat16)
    query_low = rotate(query_lin.reshape(token_rows, head_count, HD), cosine, sine_table).astype(
        jnp.bfloat16
    )
    key_low = rotate(key_lin.reshape(token_rows, kv_count, HD), cosine, sine_table).astype(
        jnp.bfloat16
    )
    query_blocks = query_low.reshape(slot_count, stretch_len, kv_count, group_size, HD)
    key_blocks = key_low.reshape(slot_count, stretch_len, kv_count, HD)
    value_blocks = value_low.reshape(slot_count, stretch_len, kv_count, HD)
    pairs = lax.all_gather(
        jnp.concatenate([key_blocks, value_blocks], axis=2), "context", axis=1, tiled=True
    )
    all_keys, all_values = pairs[:, :, :kv_count], pairs[:, :, kv_count:]
    stat_shape = (slot_count, kv_count, group_size, stretch_len)
    start_state = (
        jnp.zeros(stat_shape + (HD,), jnp.float32),
        jnp.zeros(stat_shape, jnp.float32),
        jnp.full(stat_shape, NEG_FILL, jnp.float32),
    )
    fold_forward = forward_fold(
        query_blocks, query_pos, lengths, stretch_order, half_len, score_scale
    )
    totals, weights, ceiling = fold_forward(start_state, (all_keys, all_values), jnp.int32(0))
    mixed_heads = totals / weights[..., None]
    mixed_low = (
        jnp.transpose(mixed_heads, (0, 3, 1, 2, 4))
        .reshape(token_rows, head_count * HD)
        .astype(jnp.bfloat16)
    )
    shard_f32 = jax.ShapeDtypeStruct((share_rows, model_width), jnp.float32)
    shard_low = jax.ShapeDtypeStruct((share_rows, model_width), jnp.bfloat16)
    gain_parts = jax.ShapeDtypeStruct((steps, model_width), jnp.float32)
    line = functools.partial(line_sum, n_line=n_line, steps=steps)
    normed_two, state = line(
        finish_branch,
        times_transpose(mixed_low, full_out).astype(jnp.bfloat16),
        (token_rows_low, gain_two[None, :]),
        [shard_f32],
        0,
    )
    gate_proj = jnp.dot(normed_two, full_gate, preferred_element_type=jnp.float32)
    up_proj = jnp.dot(normed_two, full_up, preferred_element_type=jnp.float32)
    sigmoid_gate = jax.nn.sigmoid(gate_proj)
    activated = gate_proj * sigmoid_gate
    product = (activated * up_proj).astype(jnp.bfloat16)
    factor = jnp.float32(all_rows) / valid_count * valid.reshape(token_rows, 1)
    grad_ffn, output_low, grad_output = line(
        finish_output,
        times_transpose(product, full_down).astype(jnp.bfloat16),
        (state, teacher.reshape(token_rows, model_width), factor),
        [shard_low, shard_f32],
        1,
    )
    block_out = lax.all_gather(output_low, "tensor", axis=0, tiled=True)
    grad_product = jnp.dot(grad_ffn, full_down, preferred_element_type=jnp.float32)
    grad_gate = (
        grad_product * up_proj * sigmoid_gate * (1.0 + gate_proj * (1.0 - sigmoid_gate))
    ).astype(jnp.bfloat16)
    grad_up = (grad_product * activated).astype(jnp.bfloat16)
    owner_sum = functools.partial(
        lax.psum_scatter, axis_name=("dp", "context"), scatter_dimension=0, tiled=True
    )

    def owned(left, right):
        return owner_sum(column_term(left, right).astype(jnp.bfloat16)).astype(jnp.float32)

    owned_down = owned(grad_ffn, product)
    owned_gate = owned(normed_two, grad_gate)
    owned_up = owned(normed_two, grad_up)
    grad_branch, grad_state, gain_two_parts = line(
        finish_ffn_back,
        (times_transpose(grad_gate, full_gate) + times_transpose(grad_up, full_up)).astype(
            jnp.bfloat16
        ),
        (state, grad_output, gain_two[None, :]),
        [shard_f32, gain_parts],
        2,
    )
    grad_mixed_low = jnp.dot(grad_branch, full_out, preferred_element_type=jnp.float32).astype(
        jnp.bfloat16
    )
    owned_out = owned(grad_branch, mixed_low)
    grad_heads = grad_mixed_low.reshape(slot_count, stretch_len, kv_count, group_size, HD)
    grad_heads_f = jnp.transpose(grad_heads.astype(jnp.float32), (0, 2, 3, 1, 4))
    delta = jnp.sum(grad_heads_f * mixed_heads, axis=-1)
    scaled_grad = grad_heads_f / weights[..., None]
    back_state = (
        jnp.zeros((slot_count, stretch_len, kv_count, group_size, HD), jnp.float32),
        jnp.zeros((slot_count, slot_len, kv_count, HD), jnp.float32),
        jnp.zeros((slot_count, slot_len, kv_count, HD), jnp.float32),
    )
    fold_backward = backward_fold(
        query_blocks,
        grad_heads,
        scaled_grad,
        delta,
        ceiling,
        weights,
        query_pos,
        lengths,
        stretch_order,
        half_len,
        score_scale,
    )
    grad_query_rot, grad_keys_all, grad_values_all = fold_backward(
        back_state, (all_keys, all_values), jnp.int32(0)
    )
    pair_grads = lax.psum_scatter(
        jnp.concatenate([grad_keys_all, grad_values_all], axis=2),
        "context",
        scatter_dimension=1,
        tiled=True,
    )
    grad_keys_own, grad_values_own = pair_grads[:, :, :kv_count], pair_grads[:, :, kv_count:]
    grad_query_lin = (
        rotate(grad_query_rot.reshape(token_rows, head_count, HD), cosine, -sine_table)
        .reshape(token_rows, head_count * HD)
        .astype(jnp.bfloat16)
    )
    grad_key_lin = (
        rotate(grad_keys_own.reshape(token_rows, kv_count, HD), cosine, -sine_table)
        .reshape(token_rows, kv_count * HD)
        .astype(jnp.bfloat16)
    )
    grad_value_lin = grad_values_own.reshape(token_rows, kv_count * HD).astype(jnp.bfloat16)
    grad_lin = jnp.concatenate([grad_query_lin, grad_key_lin, grad_value_lin], axis=1)
    owned_qkv = owned(normed, grad_lin)
    grad_tokens, gain_one_parts = line(
        finish_attn_back,
        times_transpose(grad_lin, full_qkv).astype(jnp.bfloat16),
        (token_rows_low, grad_state, gain_one[None, :]),
        [gain_parts],
        3,
    )
    gains_here = jnp.stack([jnp.sum(gain_one_parts, axis=0), jnp.sum(gain_two_parts, axis=0)])
    gains_all = lax.psum(gains_here, ("dp", "context", "tensor"))
    gains_owned = lax.dynamic_slice_in_dim(
        gains_all, lax.axis_index(("dp", "context")) * shard_rows, shard_rows, 1
    )
    matrices = [
        owned_qkv[:, :q_cols],
        owned_qkv[:, q_cols : q_cols + k_cols],
        owned_qkv[:, q_cols + k_cols :],
        owned_out,
        owned_gate,
        owned_up,
        owned_down,
    ]
    square_local = sum(jnp.sum(part * part) for part in (owned_qkv, owned_out, owned_gate, owned_up, owned_down))
    square_all = lax.psum(square_local, ("dp", "context", "tensor")) + jnp.sum(gains_all * gains_all)
    clip_factor = CLIP_NORM / jnp.maximum(jnp.sqrt(square_all), CLIP_NORM)
    packed = jnp.concatenate(matrices, axis=1)
    adam_step = adam_direction(packed, first_moment, second_moment, clip_factor)
    gain_step = adam_direction(gains_owned, gain_first, gain_second, clip_factor)
    return (
        block_out.reshape(slot_count, stretch_len, model_width),
        grad_tokens.reshape(slot_count, stretch_len, model_width),
        gains_owned[0],
        matrices[0],
        matrices[1],
        matrices[2],
        matrices[3],
        gains_owned[1],
        matrices[4],
        matrices[5],
        matrices[6],
        adam_step,
        gain_step,
    )


def solution(mesh):
    in_specs = (
        P("dp", "context", None),
        P("dp", "context", None),
        P("dp"),
        P("dp", "context"),
        P("dp", None),
        P(("dp", "context")),
        P(("dp", "context"), "tensor"),
        P(("dp", "context"), "tensor"),
        P(("dp", "context"), "tensor"),
        P(("dp", "context"), "tensor"),
        P(("dp", "context")),
        P(("dp", "context"), "tensor"),
        P(("dp", "context"), "tensor"),
        P(("dp", "context"), "tensor"),
        P(("dp", "context"), "tensor"),
        P(("dp", "context"), "tensor"),
        P(None, ("dp", "context")),
        P(None, ("dp", "context")),
    )
    out_specs = (
        P("dp", "context", None),
        P("dp", "context", None),
        P(("dp", "context")),
        P(("dp", "context"), "tensor"),
        P(("dp", "context"), "tensor"),
        P(("dp", "context"), "tensor"),
        P(("dp", "context"), "tensor"),
        P(("dp", "context")),
        P(("dp", "context"), "tensor"),
        P(("dp", "context"), "tensor"),
        P(("dp", "context"), "tensor"),
        P(("dp", "context"), "tensor"),
        P(None, ("dp", "context")),
    )
    return jax.shard_map(
        on_device, mesh=mesh, in_specs=in_specs, out_specs=out_specs, check_vma=False
    )
```

```python
import functools
import math

import jax
import jax.numpy as jnp
from jax import lax
from jax.experimental import pallas as pl
from jax.experimental.pallas import tpu as pltpu
from jax.sharding import PartitionSpec as P

HD = 64
STEP = 10


EPS_NORM = 1e-05
ROPE_BASE = 500000.0
OLD_CONTEXT = 8192.0
SCALE_FACTOR = 32.0
LOW_FACTOR = 1.0
HIGH_FACTOR = 4.0
LOG2E = 1.4426950408889634
NEG_FILL = -1e30
BETA_ONE = 0.9
BETA_TWO = 0.95
ADAM_EPS = 1e-08
CLIP_NORM = 1.0


def frequencies():
    channel = jnp.arange(HD // 2, dtype=jnp.float32)
    base_freq = jnp.power(jnp.float32(ROPE_BASE), -2.0 * channel / HD)
    wavelength = 2.0 * math.pi / base_freq
    smooth = (OLD_CONTEXT / wavelength - LOW_FACTOR) / (HIGH_FACTOR - LOW_FACTOR)
    blended = (1.0 - smooth) * base_freq / SCALE_FACTOR + smooth * base_freq
    slow_freq = jnp.where(wavelength > OLD_CONTEXT / LOW_FACTOR, base_freq / SCALE_FACTOR, blended)
    return jnp.where(wavelength < OLD_CONTEXT / HIGH_FACTOR, base_freq, slow_freq)


def normalize(values, gain):
    factor = lax.rsqrt(jnp.mean(values * values, axis=-1, keepdims=True) + EPS_NORM)
    return values * factor * gain.astype(jnp.float32)


def normalize_back(values, gain, upstream):
    factor = lax.rsqrt(jnp.mean(values * values, axis=-1, keepdims=True) + EPS_NORM)
    unit_rows = values * factor
    gain_grad = jnp.sum(upstream * unit_rows, axis=0)
    scaled_up = upstream * gain.astype(jnp.float32)
    input_grad = factor * (
        scaled_up - unit_rows * jnp.mean(scaled_up * unit_rows, axis=-1, keepdims=True)
    )
    return (input_grad, gain_grad)


def positions_of(order_table, row_index, half_len):
    stretch_slot = row_index // half_len
    matches = stretch_slot[:, None] == jnp.arange(order_table.shape[1], dtype=jnp.int32)[None, :]
    stretch_ids = jnp.sum(jnp.where(matches[None, :, :], order_table[:, None, :], 0), axis=-1)
    return stretch_ids * half_len + row_index % half_len


def times_transpose(left, right):
    return lax.dot_general(
        left, right, (((1,), (1,)), ((), ())), preferred_element_type=jnp.float32
    )


def column_term(left, right):
    return lax.dot_general(
        left, right, (((0,), (0,)), ((), ())), preferred_element_type=jnp.float32
    )


def adam_direction(gradient, first, second, clip_factor):
    clipped = gradient * clip_factor
    first_new = BETA_ONE * first + (1.0 - BETA_ONE) * clipped
    second_new = BETA_TWO * second + (1.0 - BETA_TWO) * clipped * clipped
    return (
        first_new
        / (1.0 - BETA_ONE**STEP)
        / (jnp.sqrt(second_new / (1.0 - BETA_TWO**STEP)) + ADAM_EPS)
    )


MESH_ID = pl.DeviceIdType.MESH


def row_mean(values):
    return jnp.mean(values, axis=-1, keepdims=True)


def line_place():
    place = lax.axis_index("tensor")
    side = place // 2
    inner = place + 1 - 2 * side
    outer = jnp.clip(place - 1 + 2 * side, 0, 3)
    return (place == 0) | (place == 3), side, {"tensor": inner}, {"tensor": outer}


def square_peers():
    ring, core = lax.axis_index("dp"), lax.axis_index("context")
    across = ring + 1 - 2 * (ring % 2)
    along = (ring + 2) % 4
    first = across * (1 - core) + along * core
    second = along * (1 - core) + across * core
    return ring, core, first, second, 3 - ring


def meet(with_line, with_square, with_all=False):
    barrier = pltpu.get_barrier_semaphore()
    expected = jnp.int32(0)
    if with_all:
        place = lax.axis_index("tensor")
        for hop in (1, 2, 3):
            pl.semaphore_signal(
                barrier,
                inc=1,
                device_id={"tensor": (place + hop) % 4},
                device_id_type=MESH_ID,
            )
        expected = expected + 3
    elif with_line:
        at_end, side, inner, outer = line_place()
        pl.semaphore_signal(barrier, inc=1, device_id=inner, device_id_type=MESH_ID)

        @pl.when(jnp.logical_not(at_end))
        def _():
            pl.semaphore_signal(barrier, inc=1, device_id=outer, device_id_type=MESH_ID)

        expected = expected + 2 - at_end.astype(jnp.int32)
    if with_square:
        ring, core, first, second, far = square_peers()
        for target in ({"dp": first}, {"dp": second}, {"context": 1 - core}):
            pl.semaphore_signal(barrier, inc=1, device_id=target, device_id_type=MESH_ID)
        expected = expected + 3
    pl.semaphore_wait(barrier, expected)


def line_scratch(steps, total_rows, width):
    rows = total_rows // 2 // steps
    return [
        pltpu.VMEM((2, steps, rows, width), jnp.bfloat16),
        pltpu.VMEM((steps, rows, width), jnp.bfloat16),
        pltpu.VMEM((steps, rows, width), jnp.bfloat16),
        pltpu.SemaphoreType.DMA((12, steps)),
    ]


def line_events(steps, finish, part, extra, out, kept, scratch):
    outer_in, cross_in, done, sems = scratch
    at_end, side, inner, outer = line_place()
    in_middle = jnp.logical_not(at_end)
    half = part.shape[0] // 2
    rows = half // steps

    def near(step):
        return pl.ds(pl.multiple_of(side * half + step * rows, rows), rows)

    def far(step):
        return pl.ds(pl.multiple_of((1 - side) * half + step * rows, rows), rows)

    def remote(src, dst, send, recv, step, target):
        return pltpu.make_async_remote_copy(
            src_ref=src,
            dst_ref=dst,
            send_sem=sems.at[send, step],
            recv_sem=sems.at[recv, step],
            device_id=target,
            device_id_type=MESH_ID,
        )

    def inward(kind, step):
        span = near(step) if kind else far(step)
        return remote(part.at[span], outer_in.at[kind, step], kind, 2 + kind, step, inner)

    def across(step):
        return remote(outer_in.at[0, step], cross_in.at[step], 4, 5, step, inner)

    def hand_outer(step):
        return remote(done.at[step], out.at[near(step)], 6, 9, step, outer)

    def hand_inner(step):
        return remote(done.at[step], out.at[near(step)], 7, 10, step, inner)

    def hand_on(step):
        return remote(out.at[far(step)], out.at[far(step)], 8, 10, step, outer)

    def keep(step):
        return pltpu.make_async_copy(done.at[step], out.at[near(step)], sems.at[11, step])

    def feed(index):
        step, kind = divmod(index, 2)
        if index >= 2:
            inward(kind, step - 1).wait_send()
        inward(kind, step).start()

    def pass_on(step):
        hand_inner(step).wait_recv()
        hand_on(step).start()

    @pl.when(at_end)
    def _():
        feed(0)
        feed(1)

    for item in kept:
        if item.shape[0] == steps:
            item[...] = jnp.zeros_like(item)
    yield
    for step in range(steps):

        @pl.when(at_end)
        def _():
            if step + 1 < steps:
                feed(2 * step + 2)

        @pl.when(in_middle)
        def _():
            inward(0, step).wait_recv()
            outer_in[0, step] = (
                outer_in[0, step].astype(jnp.float32) + part[far(step), :].astype(jnp.float32)
            ).astype(jnp.bfloat16)
            across(step).start()

        yield

        @pl.when(at_end)
        def _():
            if step + 1 < steps:
                feed(2 * step + 3)

        @pl.when(in_middle)
        def _():
            inward(1, step).wait_recv()
            across(step).wait_recv()
            total = (
                part[near(step), :].astype(jnp.float32)
                + outer_in[1, step].astype(jnp.float32)
                + cross_in[step].astype(jnp.float32)
            )
            finish(total, near(step), pl.ds(step * rows, rows), step, done, extra, kept)
            hand_outer(step).start()
            hand_inner(step).start()
            keep(step).start()
            if step > 0:
                pass_on(step - 1)

        yield

    @pl.when(in_middle)
    def _():
        pass_on(steps - 1)
        for step in range(steps):
            across(step).wait_send()
            hand_outer(step).wait_send()
            hand_inner(step).wait_send()
            hand_on(step).wait_send()
            keep(step).wait()

    @pl.when(at_end)
    def _():
        for kind in range(2):
            inward(kind, steps - 1).wait_send()
        for step in range(steps):
            hand_outer(step).wait_recv()
            remote(out.at[far(step)], out.at[far(step)], 8, 10, step, outer).wait_recv()

    yield


def gather_events(src, dst, sems):
    rows = src.shape[0]
    ring, core, first, second, far = square_peers()
    to_first, to_second, to_twin = {"dp": first}, {"dp": second}, {"context": 1 - core}

    def span(owner_ring, owner_core):
        return pl.ds(pl.multiple_of((owner_ring * 2 + owner_core) * rows, rows), rows)

    def copy(source, owner_ring, owner_core, slot, target):
        return pltpu.make_async_remote_copy(
            src_ref=source,
            dst_ref=dst.at[span(owner_ring, owner_core)],
            send_sem=sems.at[slot],
            recv_sem=sems.at[8 + owner_ring * 2 + owner_core],
            device_id=target,
            device_id_type=MESH_ID,
        )

    own = pltpu.make_async_copy(src, dst.at[span(ring, core)], sems.at[7])
    copy(src, ring, core, 0, to_first).start()
    copy(src, ring, core, 1, to_second).start()
    copy(src, ring, core, 2, to_twin).start()
    own.start()
    yield
    block = dst.at[span(first, core)]
    copy(block, first, core, 3, to_second).wait_recv()
    copy(block, first, core, 3, to_second).start()
    copy(block, first, core, 4, to_twin).start()
    yield
    block = dst.at[span(second, core)]
    copy(block, second, core, 5, to_twin).wait_recv()
    copy(block, second, core, 5, to_twin).start()
    yield
    block = dst.at[span(far, core)]
    copy(block, far, core, 6, to_twin).wait_recv()
    copy(block, far, core, 6, to_twin).start()
    yield
    for owner_ring in (ring, first, second, far):
        block = dst.at[span(owner_ring, 1 - core)]
        copy(block, owner_ring, 1 - core, 2, to_twin).wait_recv()
    for slot in range(7):
        copy(src, ring, core, slot, to_twin).wait_send()
    own.wait()
    yield


def lane_sums(item):
    sums = jnp.sum(item[...] * item[...], axis=0, keepdims=True)
    return sum(sums[:, first : first + 128] for first in range(0, sums.shape[1], 128))


def scatter_scratch(rows, cols):
    return [
        pltpu.VMEM((4, rows, cols), jnp.bfloat16),
        pltpu.VMEM((4, rows, cols), jnp.bfloat16),
        pltpu.VMEM((2, rows, cols), jnp.bfloat16),
        pltpu.VMEM((1, rows, cols), jnp.bfloat16),
        pltpu.SemaphoreType.DMA((14,)),
    ]


def scatter_events(left, right, out, square, scratch):
    twin_out, twin_in, first_in, second_in, sems = scratch
    rows = out.shape[0]
    ring, core, first, second, far = square_peers()
    to_first, to_second, to_twin = {"dp": first}, {"dp": second}, {"context": 1 - core}
    own_order = (far, first, second, ring)
    twin_order = (far, second, first, ring)

    def block(owner_ring, owner_core):
        span = pl.ds(pl.multiple_of((owner_ring * 2 + owner_core) * rows, rows), rows)
        return column_term(left[:, span], right[...])

    def remote(src, dst, slot, target):
        return pltpu.make_async_remote_copy(
            src_ref=src,
            dst_ref=dst,
            send_sem=sems.at[slot],
            recv_sem=sems.at[7 + slot],
            device_id=target,
            device_id_type=MESH_ID,
        )

    def swap(role):
        return remote(twin_out.at[role], twin_in.at[role], role, to_twin)

    def over_first(role):
        return remote(twin_in.at[role], first_in.at[role], 4 + role, to_first)

    over_second = remote(twin_in.at[2], second_in.at[0], 6, to_second)

    def for_twin(role):
        twin_out[role] = block(twin_order[role], 1 - core).astype(jnp.bfloat16)
        swap(role).start()

    for role in range(2):
        for_twin(role)
        yield
    for role in range(2):
        term = block(own_order[role], core)
        swap(role).wait_recv()
        twin_in[role] = (term + twin_in[role].astype(jnp.float32)).astype(jnp.bfloat16)
        over_first(role).start()
        yield
    for_twin(2)
    yield
    for_twin(3)
    yield
    term = block(second, core)
    swap(2).wait_recv()
    over_first(0).wait_recv()
    twin_in[2] = (
        term + twin_in[2].astype(jnp.float32) + first_in[0].astype(jnp.float32)
    ).astype(jnp.bfloat16)
    over_second.start()
    yield
    term = block(ring, core)
    swap(3).wait_recv()
    over_first(1).wait_recv()
    out[...] = term + twin_in[3].astype(jnp.float32) + first_in[1].astype(jnp.float32)
    yield
    over_second.wait_recv()
    out[...] += second_in[0].astype(jnp.float32)
    square[...] = lane_sums(out)
    for role in range(4):
        swap(role).wait_send()
    over_first(0).wait_send()
    over_first(1).wait_send()
    over_second.wait_send()
    yield


def total_scratch(width):
    return [
        pltpu.VMEM((7, 1, width), jnp.float32),
        pltpu.VMEM((4, 1, width), jnp.float32),
        pltpu.SemaphoreType.DMA((13,)),
    ]


def total_everywhere(out, taken, line_in, sems):
    ring, core, first, second, far = square_peers()
    place = lax.axis_index("tensor")
    across = ring + 1 - 2 * (ring % 2)
    along = (ring + 2) % 4
    others = [{"tensor": (place + hop) % 4} for hop in (1, 2, 3)]
    for stage, target in enumerate(({"context": 1 - core}, {"dp": across}, {"dp": along})):
        copy = pltpu.make_async_remote_copy(
            src_ref=taken.at[2 * stage],
            dst_ref=taken.at[2 * stage + 1],
            send_sem=sems.at[stage],
            recv_sem=sems.at[3 + stage],
            device_id=target,
            device_id_type=MESH_ID,
        )
        copy.start()
        copy.wait()
        taken[2 * stage + 2] = taken[2 * stage] + taken[2 * stage + 1]

    def along_line(hop, owner):
        return pltpu.make_async_remote_copy(
            src_ref=taken.at[6],
            dst_ref=line_in.at[owner],
            send_sem=sems.at[6 + hop],
            recv_sem=sems.at[9 + owner],
            device_id=others[hop],
            device_id_type=MESH_ID,
        )

    for hop in range(3):
        along_line(hop, place).start()
    line_in[place] = taken[6]
    for hop in range(3):
        along_line(hop, (place + hop + 1) % 4).wait_recv()
    out[...] = (line_in[0] + line_in[1]) + (line_in[2] + line_in[3])
    for hop in range(3):
        along_line(hop, place).wait_send()


def clip_of(totals, gain_cols):
    gains, squares = totals[:, :gain_cols], totals[:, gain_cols:]
    square_all = jnp.sum(squares) + jnp.sum(gains * gains)
    return CLIP_NORM / jnp.maximum(jnp.sqrt(square_all), CLIP_NORM)


def update_body(widths, gain_cols, totals, *refs):
    owned, (first, second), outs = refs[:5], refs[5:7], refs[7:]
    clip_factor = clip_of(totals[...], gain_cols)
    bounds = [0, widths[0], widths[0] + widths[1], sum(widths[:3])]
    grads = [owned[0][:, bounds[place] : bounds[place + 1]] for place in range(3)]
    grads += [item[...] for item in owned[1:]]
    start = 0
    for grad, grad_out in zip(grads, outs[:7]):
        grad_out[...] = grad
        span = slice(start, start + grad.shape[1])
        outs[7][:, span] = adam_direction(grad, first[:, span], second[:, span], clip_factor)
        start = start + grad.shape[1]


def update_rows(owned, first, second, totals, gain_cols, widths):
    shard_rows, pack_cols = first.shape
    rows = min(32, shard_rows)

    def block(width):
        return pl.BlockSpec((rows, width), lambda row: (row, 0))

    return pl.pallas_call(
        functools.partial(update_body, widths, gain_cols),
        grid=(shard_rows // rows,),
        out_shape=[jax.ShapeDtypeStruct((shard_rows, width), jnp.float32) for width in widths]
        + [jax.ShapeDtypeStruct((shard_rows, pack_cols), jnp.float32)],
        in_specs=[pl.BlockSpec(totals.shape, lambda row: (0, 0))]
        + [block(item.shape[1]) for item in owned]
        + [block(pack_cols)] * 2,
        out_specs=[block(width) for width in widths] + [block(pack_cols)],
        compiler_params=pltpu.CompilerParams(vmem_limit_bytes=48 << 20),
        cost_estimate=busy(15),
    )(totals, *owned, first, second)


def busy(microseconds):
    return pl.CostEstimate(
        flops=microseconds * 10**9, bytes_accessed=1 << 20, transcendentals=0
    )


def weave(order):
    for events in order:
        next(events, None)
    for events in order:
        for _ in events:
            pass


def line_body(steps, finish, counts, order, *refs):
    extra_count, kept_count, gather_count, scatter_count, pooled_count = counts
    refs = list(refs)

    def take(count):
        taken = refs[:count]
        del refs[:count]
        return taken

    (part,) = take(1)
    extra = take(extra_count)
    shards = take(gather_count)
    factors = take(2 * scatter_count)
    pooled = take(pooled_count)
    (out,) = take(1)
    kept = take(kept_count)
    wholes = take(gather_count)
    owned = take(scatter_count)
    squares = take(scatter_count)
    totals = take(min(pooled_count, 1))
    line_refs = take(4)
    total_refs = take(3 if pooled else 0)
    gather_sems = take(gather_count)
    meet(True, bool(gather_count or scatter_count), bool(pooled))
    lists = {"line": line_events(steps, finish, part, extra, out, kept, line_refs)}
    for place in range(gather_count):
        lists[f"g{place}"] = gather_events(shards[place], wholes[place], gather_sems[place])
    for place in range(scatter_count):
        lists[f"s{place}"] = scatter_events(
            factors[2 * place], factors[2 * place + 1], owned[place], squares[place], take(5)
        )
    weave([lists[name] for name in order + tuple(sorted(lists))])
    if pooled:
        own_row = total_refs[0].at[0]
        width = kept[-1].shape[1]
        own_row[:, :width] = jnp.sum(kept[-1][...], axis=0, keepdims=True)
        own_row[:, width : 2 * width] = jnp.sum(pooled[0][...], axis=0, keepdims=True)
        own_row[:, 2 * width :] = sum(item[...] for item in (*pooled[1:], *squares))
        total_everywhere(totals[0], *total_refs)


def line_sum(finish, part, extra, kept, which, steps, shards=(), factors=(), pooled=(), order=()):
    total_rows, width = part.shape
    in_vmem = pl.BlockSpec(memory_space=pltpu.VMEM)
    anywhere = pl.BlockSpec(memory_space=pl.ANY)
    wholes = [jax.ShapeDtypeStruct((8 * item.shape[0], item.shape[1]), item.dtype) for item in shards]
    owned = [
        jax.ShapeDtypeStruct((left.shape[1] // 8, right.shape[1]), jnp.float32)
        for left, right in factors
    ]
    squares = [jax.ShapeDtypeStruct((1, 128), jnp.float32) for item in owned]
    pool_width = 2 * width + 128
    totals = [jax.ShapeDtypeStruct((1, pool_width), jnp.float32)] if pooled else []
    scratch = line_scratch(steps, total_rows, width)
    scratch += total_scratch(pool_width) if pooled else []
    scratch += [pltpu.SemaphoreType.DMA((16,))] * len(shards)
    for item in owned:
        scratch += scatter_scratch(*item.shape)
    counts = (len(extra), len(kept), len(shards), len(factors), len(pooled))
    return pl.pallas_call(
        functools.partial(line_body, steps, finish, counts, order),
        out_shape=[jax.ShapeDtypeStruct((total_rows, width), jnp.bfloat16)] + kept + wholes + owned + squares + totals,
        in_specs=[in_vmem] * (1 + len(extra)) + [anywhere] * len(shards) + [in_vmem] * (2 * len(factors) + len(pooled)),
        out_specs=[anywhere] + [in_vmem] * len(kept) + [anywhere] * len(shards) + [in_vmem] * (2 * len(owned) + len(totals)),
        scratch_shapes=scratch,
        compiler_params=pltpu.CompilerParams(
            collective_id=which, has_side_effects=True, vmem_limit_bytes=60 << 20
        ),
        cost_estimate=busy(70),
    )(part, *extra, *shards, *[item for pair in factors for item in pair], *pooled)


def join_halves(held, own, crossed, other):
    place = lax.axis_index("tensor")
    at_end = (place == 0) | (place == 3)
    own = jnp.where(at_end, own, held)
    other = jnp.where(at_end, other, crossed)
    low_side = place < 2
    return jnp.concatenate(
        [jnp.where(low_side, own, other), jnp.where(low_side, other, own)], axis=0
    )


FFN_BACK_ORDER = (
    "line", "s0", "s0", "s0", "s0", "s1", "s1", "s1", "line", "s1",
    "s0", "s0", "s1", "s1", "line", "line", "line", "line", "line", "line",
    "s0", "s0", "line", "s1", "s1",
)


def finish_branch(total, own, local, step, done, extra, kept):
    tokens, gain = extra
    (state,) = kept
    rows_now = tokens[own, :].astype(jnp.float32) + total
    state[local, :] = rows_now
    done[step] = normalize(rows_now, gain[...]).astype(jnp.bfloat16)


def finish_output(total, own, local, step, done, extra, kept):
    state, teacher, factor = extra
    output_low, grad_output = kept
    output = state[local, :] + total
    output_low[local, :] = output.astype(jnp.bfloat16)
    grad_now = factor[own, :] * (output - teacher[own, :].astype(jnp.float32))
    grad_output[local, :] = grad_now
    done[step] = grad_now.astype(jnp.bfloat16)


def finish_ffn_back(total, own, local, step, done, extra, kept):
    state, grad_output, gain = extra
    grad_state, gain_grad = kept
    input_grad, gain_now = normalize_back(state[local, :], gain[...], total)
    grad_now = grad_output[local, :] + input_grad
    grad_state[local, :] = grad_now
    gain_grad[step : step + 1, :] = gain_now[None, :]
    done[step] = grad_now.astype(jnp.bfloat16)


def finish_attn_back(total, own, local, step, done, extra, kept):
    tokens, grad_state, gain = extra
    (gain_grad,) = kept
    input_grad, gain_now = normalize_back(tokens[own, :].astype(jnp.float32), gain[...], total)
    gain_grad[step : step + 1, :] = gain_now[None, :]
    done[step] = (grad_state[local, :] + input_grad).astype(jnp.bfloat16)


def local_call(body, time, outs, operands, scratch=(), vmem=60):
    in_vmem = pl.BlockSpec(memory_space=pltpu.VMEM)
    return pl.pallas_call(
        body,
        out_shape=outs,
        in_specs=[in_vmem] * len(operands),
        out_specs=[in_vmem] * len(outs),
        scratch_shapes=list(scratch),
        compiler_params=pltpu.CompilerParams(vmem_limit_bytes=vmem << 20),
        cost_estimate=busy(time),
    )(*operands)


def ffn_body(normed, w_gate, w_up, w_down, gate, up, product, part, total):
    step = pl.program_id(0)
    gate_now = jnp.dot(normed[...], w_gate[...], preferred_element_type=jnp.float32)
    up_now = jnp.dot(normed[...], w_up[...], preferred_element_type=jnp.float32)
    gate[...] = gate_now
    up[...] = up_now
    product_now = (gate_now * jax.nn.sigmoid(gate_now) * up_now).astype(jnp.bfloat16)
    product[...] = product_now
    accumulate(step, total, part, times_transpose(product_now, w_down[...]))


def ffn_back_body(
    grad_rows, w_gate, w_up, w_down, gate, up, grad_gate, grad_up, part, total
):
    step = pl.program_id(0)
    grad_product = jnp.dot(grad_rows[...], w_down[...], preferred_element_type=jnp.float32)
    gate_now = gate[...]
    sigmoid_gate = jax.nn.sigmoid(gate_now)
    gate_low = (
        grad_product * up[...] * sigmoid_gate * (1.0 + gate_now * (1.0 - sigmoid_gate))
    ).astype(jnp.bfloat16)
    up_low = (grad_product * (gate_now * sigmoid_gate)).astype(jnp.bfloat16)
    grad_gate[...] = gate_low
    grad_up[...] = up_low
    accumulate(
        step,
        total,
        part,
        times_transpose(gate_low, w_gate[...]) + times_transpose(up_low, w_up[...]),
    )


def accumulate(step, total, part, term):
    last = pl.num_programs(0) - 1

    @pl.when(step == 0)
    def _():
        total[...] = term

    @pl.when((step > 0) & (step < last))
    def _():
        total[...] += term

    @pl.when(step == last)
    def _():
        part[...] = (total[...] + term).astype(jnp.bfloat16)


def by_units(body, rows_in, weights, by_columns, outs, time):
    rows, width = rows_in.shape
    units = weights[0].shape[1]
    block = min(UNIT_BLOCK, units)

    def columns(depth):
        return pl.BlockSpec((depth, block), lambda step: (0, step))

    whole = pl.BlockSpec((rows, width), lambda step: (0, 0))
    return pl.pallas_call(
        body,
        grid=(units // block,),
        out_shape=[jax.ShapeDtypeStruct((rows, units), kind) for kind in outs]
        + [jax.ShapeDtypeStruct((rows, width), jnp.bfloat16)],
        in_specs=[whole]
        + [columns(item.shape[0]) for item in weights]
        + [columns(rows) for _ in by_columns],
        out_specs=[columns(rows) for _ in outs] + [whole],
        scratch_shapes=[pltpu.VMEM((rows, width), jnp.float32)],
        compiler_params=pltpu.CompilerParams(vmem_limit_bytes=56 << 20),
        cost_estimate=busy(time),
    )(rows_in, *weights, *by_columns)


UNIT_BLOCK = 512


def turn(head_rows, cosine, sine_table):
    middle = head_rows.shape[0] // 2
    upper, lower = head_rows[:middle], head_rows[middle:]
    return jnp.concatenate(
        [upper * cosine - lower * sine_table, lower * cosine + upper * sine_table], axis=0
    )


def normalize_rows(tokens, gain, normed):
    @pl.loop(0, tokens.shape[0] // 64)
    def _(block):
        span = pl.ds(pl.multiple_of(block * 64, 64), 64)
        normed[span, :] = normalize(tokens[span, :].astype(jnp.float32), gain[...]).astype(
            jnp.bfloat16
        )


def project_rows(normed, weights, cosine, sine_table, query_t, pairs):
    q_cols = query_t.shape[0]
    k_cols = pairs.shape[1] // 2
    lin_t = jnp.dot(
        normed[...], weights[:, : q_cols + k_cols], preferred_element_type=jnp.float32
    ).T
    for first in range(0, q_cols, HD):
        query_t[first : first + HD, :] = turn(
            lin_t[first : first + HD], cosine[...], sine_table[...]
        ).astype(jnp.bfloat16)
    keys = [
        turn(lin_t[first : first + HD], cosine[...], sine_table[...])
        for first in range(q_cols, q_cols + k_cols, HD)
    ]
    pairs[:, :k_cols] = jnp.concatenate(keys, axis=0).T.astype(jnp.bfloat16)
    pairs[:, k_cols:] = jnp.dot(
        normed[...],
        weights[:, q_cols + k_cols : q_cols + 2 * k_cols],
        preferred_element_type=jnp.float32,
    ).astype(jnp.bfloat16)


def project_body(tokens, gain, weights, cosine, sine_table, normed, query_t, pairs):
    normalize_rows(tokens, gain, normed)
    project_rows(normed, weights, cosine, sine_table, query_t, pairs)


def split_pairs(pairs, keys, keys_t, values, values_t):
    heads = pairs.shape[1] // (2 * HD)
    for head in range(heads):
        part = pairs[:, head * HD : (head + 1) * HD]
        if keys is not None:
            keys[head] = part
        if keys_t is not None:
            keys_t[head] = part.astype(jnp.float32).T.astype(jnp.bfloat16)
        part = pairs[:, (heads + head) * HD : (heads + head + 1) * HD]
        if values is not None:
            values[head] = part
        if values_t is not None:
            values_t[head] = part.astype(jnp.float32).T.astype(jnp.bfloat16)


SCORE_FACTOR = float(HD) ** (-0.5) * LOG2E
KEY_BLOCK = 256


def lifted_scores(key_block, query_head, query_pos, key_pos):
    scores = jnp.dot(key_block, query_head, preferred_element_type=jnp.float32)
    return jnp.where(key_pos <= query_pos, scores * SCORE_FACTOR, NEG_FILL)


def attend_heads(
    heads, group, query_t, query_pos, key_pos, keys, values_t, lifted, mixed_t, low_t, stats
):
    rows = query_t.shape[1]
    blocks = keys.shape[1] // KEY_BLOCK

    @pl.loop(*heads)
    def _(head):
        span = pl.ds(pl.multiple_of(head * HD, HD), HD)
        shared = head // group
        query_head = query_t[span, :]

        def scan_scores(block, highest):
            keys_now = pl.ds(pl.multiple_of(block * KEY_BLOCK, KEY_BLOCK), KEY_BLOCK)
            scores = lifted_scores(
                keys[shared, keys_now, :], query_head, query_pos[...], key_pos[keys_now, :]
            )
            lifted[keys_now, :] = scores
            return jnp.maximum(highest, jnp.max(scores, axis=0, keepdims=True))

        highest = lax.fori_loop(
            0, blocks, scan_scores, jnp.full((1, rows), NEG_FILL, jnp.float32)
        )
        ceiling = jnp.floor(highest)

        def scan_values(block, state):
            weight_sum, mixed = state
            keys_now = pl.ds(pl.multiple_of(block * KEY_BLOCK, KEY_BLOCK), KEY_BLOCK)
            expo = jnp.exp2(lifted[keys_now, :] - ceiling)
            mixed = mixed + jnp.dot(
                values_t[shared, :, keys_now],
                expo.astype(jnp.bfloat16),
                preferred_element_type=jnp.float32,
            )
            return weight_sum + jnp.sum(expo, axis=0, keepdims=True), mixed

        weight_sum, mixed = lax.fori_loop(
            0,
            blocks,
            scan_values,
            (jnp.zeros((1, rows), jnp.float32), jnp.zeros((HD, rows), jnp.float32)),
        )
        mixed = mixed / weight_sum
        mixed_t[span, :] = mixed
        low_t[span, :] = mixed.astype(jnp.bfloat16).astype(jnp.float32)
        stats[head] = jnp.concatenate([ceiling, weight_sum], axis=0)


def branch_rows(low_t, w_out, mixed_low, part):
    mixed_low[...] = low_t[...].T.astype(jnp.bfloat16)

    @pl.loop(0, part.shape[1] // 512)
    def _(block):
        span = pl.ds(pl.multiple_of(block * 512, 512), 512)
        part[:, span] = times_transpose(mixed_low[...], w_out[span, :]).astype(jnp.bfloat16)


def attend_body(
    group, query_t, pairs, query_pos, key_pos, w_out, mixed_t, mixed_low, stats, part,
    keys, values_t, lifted, low_t,
):
    split_pairs(pairs, keys, None, None, values_t)
    attend_heads(
        (0, query_t.shape[0] // HD), group, query_t, query_pos, key_pos, keys, values_t,
        lifted, mixed_t, low_t, stats,
    )
    branch_rows(low_t, w_out, mixed_low, part)


FRONT_ORDER = (
    "gs", "gq", "gk", "gv", "gs", "gs", "gs", "gs", "c", "gq",
    "gk", "gv", "go", "gq", "gk", "gv", "gz", "gq", "gk", "gv",
    "gq", "gk", "gv", "c", "go", "c", "ga", "go", "c", "go",
    "c", "c", "gu", "go", "c", "line", "line", "line", "line", "gz",
    "gz", "line", "gd", "line", "ga", "gu", "ga", "gu", "line", "line",
    "line", "gz", "line", "gd", "gz", "gd", "ga", "gu", "gd",
)


def front_body(steps, group, order, *refs):
    refs = list(refs)

    def take(count):
        taken = refs[:count]
        del refs[:count]
        return taken

    tokens, cosine, sine_table, query_pos, key_pos = take(5)
    shards = take(9)
    normed, query_t, pairs_out, mixed_t, mixed_low, stats, gains, state = take(8)
    normed_two, pack_out, out_whole, gate, up, down, counts = take(7)
    pack, w_out, gain_tiles, pairs, keys, values_t, lifted, low_t, part = take(9)
    line_refs = take(4)
    gather_sems = take(9)
    (own_sems,) = take(1)
    ring, core, first, second, far = square_peers()
    rows, width = tokens.shape
    q_cols, k_cols = query_t.shape[0], pairs.shape[1] // 2
    heads = q_cols // HD
    shard_rows = width // 8
    meet(True, True)

    def pair_rows(which):
        return pl.ds(pl.multiple_of(which * rows, rows), rows)

    def swap_pairs(which):
        return pltpu.make_async_remote_copy(
            src_ref=pairs.at[pair_rows(which)],
            dst_ref=pairs.at[pair_rows(which)],
            send_sem=own_sems.at[0],
            recv_sem=own_sems.at[1],
            device_id={"context": 1 - core},
            device_id_type=MESH_ID,
        )

    keep_pack = pltpu.make_async_copy(pack, pack_out, own_sems.at[2])
    keep_out = pltpu.make_async_copy(w_out, out_whole, own_sems.at[3])

    def compute():
        for row in range(2):
            gains[row : row + 1, :] = jnp.concatenate(
                [
                    gain_tiles[32 * owner + 16 * row : 32 * owner + 16 * row + 16, :].astype(
                        jnp.float32
                    )[:1]
                    for owner in range(8)
                ],
                axis=1,
            )
        normalize_rows(tokens, gains.at[0:1], normed)
        yield
        project_rows(normed, pack, cosine, sine_table, query_t, pairs.at[pair_rows(core)])
        swap_pairs(core).start()
        keep_pack.start()
        yield
        swap_pairs(1 - core).wait_recv()
        split_pairs(pairs, keys, None, None, values_t)
        pairs_out[...] = pairs[...]
        for chunk in range(4):
            attend_heads(
                (chunk * heads // 4, (chunk + 1) * heads // 4), group, query_t, query_pos,
                key_pos, keys, values_t, lifted, mixed_t, low_t, stats,
            )
            yield
        keep_out.start()
        branch_rows(low_t, w_out, mixed_low, part)
        yield
        swap_pairs(core).wait_send()
        keep_pack.wait()
        keep_out.wait()
        yield

    targets = [
        pack.at[:, pl.ds(0, q_cols)],
        pack.at[:, pl.ds(q_cols, k_cols)],
        pack.at[:, pl.ds(q_cols + k_cols, k_cols)],
        w_out,
        gain_tiles,
        gate,
        up,
        down,
        counts,
    ]
    lists = {
        name: gather_events(source, target, sems)
        for name, source, target, sems in zip(
            ("gq", "gk", "gv", "go", "gs", "ga", "gu", "gd", "gz"), shards, targets, gather_sems
        )
    }
    lists["c"] = compute()
    lists["line"] = line_events(
        steps, finish_branch, part, (tokens, gains.at[1:2]), normed_two, (state,), line_refs
    )
    weave([lists[name] for name in order + tuple(sorted(lists))])


def front(tokens, tables, shards, group, steps, which):
    rows, width = tokens.shape
    cosine, sine_table, query_pos, key_pos = tables
    slot_len = key_pos.shape[0]
    q_cols, k_cols = shards[0].shape[1], shards[1].shape[1]
    heads, kv_heads = q_cols // HD, k_cols // HD
    low = functools.partial(jax.ShapeDtypeStruct, dtype=jnp.bfloat16)
    full = functools.partial(jax.ShapeDtypeStruct, dtype=jnp.float32)
    in_vmem = pl.BlockSpec(memory_space=pltpu.VMEM)
    anywhere = pl.BlockSpec(memory_space=pl.ANY)
    pack_cols = q_cols + 2 * k_cols
    held = [
        low((rows, width)),
        low((q_cols, rows)),
        low((slot_len, 2 * k_cols)),
        full((q_cols, rows)),
        low((rows, q_cols)),
        full((heads, 2, rows)),
        full((2, width)),
        full((rows // 2, width)),
    ]
    far = [low((rows, width)), low((width, pack_cols)), low((width, q_cols))]
    far += [low((8 * item.shape[0], item.shape[1])) for item in shards[5:]]
    return pl.pallas_call(
        functools.partial(front_body, steps, group, FRONT_ORDER),
        out_shape=held + far,
        in_specs=[in_vmem] * 5 + [anywhere] * 9,
        out_specs=[in_vmem] * len(held) + [anywhere] * len(far),
        scratch_shapes=[
            pltpu.VMEM((width, pack_cols), jnp.bfloat16),
            pltpu.VMEM((width, q_cols), jnp.bfloat16),
            pltpu.VMEM((8 * shards[4].shape[0], shards[4].shape[1]), jnp.bfloat16),
            pltpu.VMEM((slot_len, 2 * k_cols), jnp.bfloat16),
            pltpu.VMEM((kv_heads, slot_len, HD), jnp.bfloat16),
            pltpu.VMEM((kv_heads, HD, slot_len), jnp.bfloat16),
            pltpu.VMEM((slot_len, rows), jnp.float32),
            pltpu.VMEM((q_cols, rows), jnp.float32),
            pltpu.VMEM((rows, width), jnp.bfloat16),
        ]
        + line_scratch(steps, rows, width)
        + [pltpu.SemaphoreType.DMA((16,))] * 9
        + [pltpu.SemaphoreType.DMA((4,))],
        compiler_params=pltpu.CompilerParams(
            collective_id=which, has_side_effects=True, vmem_limit_bytes=60 << 20
        ),
        cost_estimate=busy(130),
    )(tokens, cosine, sine_table, query_pos, key_pos, *shards)


def prepare_back(grad_branch, w_out, query_t, queries, grad_t):
    queries_f = query_t[...].astype(jnp.float32).T
    for head in range(queries.shape[0]):
        queries[head] = queries_f[:, head * HD : (head + 1) * HD].astype(jnp.bfloat16)
    grad_t[...] = (
        jnp.dot(grad_branch[...], w_out[...], preferred_element_type=jnp.float32)
        .astype(jnp.bfloat16)
        .astype(jnp.float32)
        .T
    )


def attend_back_heads(
    heads, group, query_t, mixed_t, stats, query_pos, key_pos, cosine, sine_table, grad_pairs,
    keys, keys_t, values, queries, grad_t, turned,
):
    rows = query_t.shape[1]
    blocks = keys.shape[1] // KEY_BLOCK
    score_scale = float(HD) ** (-0.5)

    @pl.loop(*heads)
    def _(head):
        span = pl.ds(pl.multiple_of(head * HD, HD), HD)
        shared = head // group
        query_head = query_t[span, :]
        query_rows = queries[head]
        ceiling = stats[head, 0:1, :]
        inverse = 1.0 / stats[head, 1:2, :]
        grad_head = grad_t[span, :]
        delta = jnp.sum(grad_head * mixed_t[span, :], axis=0, keepdims=True)
        scaled = grad_head * inverse
        scaled_high = scaled.astype(jnp.bfloat16)
        scaled_low = (scaled - scaled_high.astype(jnp.float32)).astype(jnp.bfloat16)
        scaled_both = jnp.concatenate([scaled_high, scaled_low], axis=0)
        grad_head_low = grad_head.astype(jnp.bfloat16)

        def scan_keys(block, grad_query_t):
            keys_now = pl.ds(pl.multiple_of(block * KEY_BLOCK, KEY_BLOCK), KEY_BLOCK)
            scores = lifted_scores(
                keys[shared, keys_now, :], query_head, query_pos[...], key_pos[keys_now, :]
            )
            expo = jnp.exp2(scores - ceiling)
            value_term = times_transpose(expo.astype(jnp.bfloat16), scaled_both)
            grad_probs = jnp.dot(
                values[shared, keys_now, :], grad_head_low, preferred_element_type=jnp.float32
            )
            grad_scores = (expo * inverse * (grad_probs - delta)).astype(jnp.bfloat16)
            key_term = jnp.dot(grad_scores, query_rows, preferred_element_type=jnp.float32)
            grad_pairs[shared, keys_now, :] += jnp.concatenate(
                [key_term * score_scale, value_term[:, :HD] + value_term[:, HD:]], axis=1
            )
            return grad_query_t + jnp.dot(
                keys_t[shared, :, keys_now], grad_scores, preferred_element_type=jnp.float32
            )

        grad_query_t = lax.fori_loop(
            0, blocks, scan_keys, jnp.zeros((HD, rows), jnp.float32)
        )
        turned[span, :] = turn(grad_query_t * score_scale, cosine[...], -sine_table[...])


def attend_back_body(
    group, grad_branch, w_out, query_t, pairs, mixed_t, stats, query_pos, key_pos, cosine,
    sine_table, grad_query, grad_pairs, keys, keys_t, values, queries, grad_t, turned,
):
    split_pairs(pairs, keys, keys_t, values, None)
    prepare_back(grad_branch, w_out, query_t, queries, grad_t)
    grad_pairs[...] = jnp.zeros_like(grad_pairs)
    attend_back_heads(
        (0, queries.shape[0]), group, query_t, mixed_t, stats, query_pos, key_pos, cosine,
        sine_table, grad_pairs, keys, keys_t, values, queries, grad_t, turned,
    )
    grad_query[...] = turned[...].T.astype(jnp.bfloat16)


def join_rows(grad_query, pair_grads, cosine, sine_table, weights, grad_lin, part):
    q_cols = grad_query.shape[1]
    k_cols = HD * len(pair_grads)
    grad_lin[:, :q_cols] = grad_query
    keys = [turn(item.T[:HD], cosine[...], -sine_table[...]) for item in pair_grads]
    grad_lin[:, q_cols : q_cols + k_cols] = jnp.concatenate(keys, axis=0).T.astype(jnp.bfloat16)
    grad_lin[:, q_cols + k_cols :] = jnp.concatenate(
        [item[:, HD:] for item in pair_grads], axis=1
    ).astype(jnp.bfloat16)

    @pl.loop(0, part.shape[1] // 512)
    def _(block):
        span = pl.ds(pl.multiple_of(block * 512, 512), 512)
        part[:, span] = times_transpose(
            grad_lin[...], weights[span, : q_cols + 2 * k_cols]
        ).astype(jnp.bfloat16)


def join_body(grad_query, grad_pairs, cosine, sine_table, weights, grad_lin, part):
    pair_grads = [grad_pairs[head] for head in range(grad_pairs.shape[0])]
    join_rows(grad_query[...], pair_grads, cosine, sine_table, weights, grad_lin, part)


BACK_ORDER = (
    "s0", "s0", "s0", "s0", "s0", "s0", "c", "s1", "s1", "s1",
    "s1", "s1", "s1", "c", "c", "c", "s0", "s0", "c", "s1",
    "s1", "c", "line", "s2", "s2", "s2", "s2", "line", "s2", "s2",
    "line", "line", "s2", "s2", "line", "line", "line", "line", "line",
)


def back_body(steps, group, order, *refs):
    refs = list(refs)

    def take(count):
        taken = refs[:count]
        del refs[:count]
        return taken

    cosine, sine_table, query_pos, key_pos = take(4)
    grad_branch, w_out, query_t, pairs, mixed_t, stats, gains = take(7)
    normed_two, grad_up, mixed_low = take(3)
    pooled = take(3)
    later = take(4)
    owned = take(3)
    (totals,) = take(1)
    (out,) = take(1)
    keys, keys_t, values, queries, grad_t, turned, grad_pairs, pairs_in, grad_lin, part = take(10)
    gain_parts = take(1)
    loaded = take(4)
    squares = take(3)
    line_refs = take(4)
    total_refs = take(3)
    scatter_refs = [take(5) for _ in range(3)]
    (own_sems,) = take(1)
    weights, tokens, grad_state, normed = loaded
    ring, core, first, second, far = square_peers()
    rows = query_t.shape[1]
    heads = queries.shape[0]
    meet(True, True, True)
    loads = [
        pltpu.make_async_copy(source, target, own_sems.at[2 + place])
        for place, (source, target) in enumerate(zip(later, loaded))
    ]
    for load in loads:
        load.start()

    def own_rows(which):
        return pl.ds(pl.multiple_of(which * rows, rows), rows)

    swap = pltpu.make_async_remote_copy(
        src_ref=grad_pairs.at[:, own_rows(1 - core)],
        dst_ref=pairs_in,
        send_sem=own_sems.at[0],
        recv_sem=own_sems.at[1],
        device_id={"context": 1 - core},
        device_id_type=MESH_ID,
    )

    def compute():
        split_pairs(pairs, keys, keys_t, values, None)
        prepare_back(grad_branch, w_out, query_t, queries, grad_t)
        grad_pairs[...] = jnp.zeros_like(grad_pairs)
        yield
        for chunk in range(4):
            attend_back_heads(
                (chunk * heads // 4, (chunk + 1) * heads // 4), group, query_t, mixed_t, stats,
                query_pos, key_pos, cosine, sine_table, grad_pairs, keys, keys_t, values,
                queries, grad_t, turned,
            )
            yield
        swap.start()
        for load in loads:
            load.wait()
        grad_query = turned[...].T.astype(jnp.bfloat16)
        swap.wait_recv()
        pair_grads = [
            grad_pairs[head, own_rows(core), :] + pairs_in[head] for head in range(keys.shape[0])
        ]
        join_rows(grad_query, pair_grads, cosine, sine_table, weights, grad_lin, part)
        yield
        swap.wait_send()
        yield

    pairs_of = ((normed_two, grad_up), (grad_branch, mixed_low), (normed, grad_lin))
    lists = {
        f"s{place}": scatter_events(left, right, owned[place], squares[place], scatter_refs[place])
        for place, (left, right) in enumerate(pairs_of)
    }
    lists["c"] = compute()
    lists["line"] = line_events(
        steps, finish_attn_back, part, (tokens, grad_state, gains.at[0:1]), out, gain_parts,
        line_refs,
    )
    weave([lists[name] for name in order + tuple(sorted(lists))])
    own_row = total_refs[0].at[0]
    width = gains.shape[1]
    own_row[:, :width] = jnp.sum(gain_parts[0][...], axis=0, keepdims=True)
    own_row[:, width : 2 * width] = jnp.sum(pooled[0][...], axis=0, keepdims=True)
    own_row[:, 2 * width :] = sum(item[...] for item in (*pooled[1:], *squares))
    total_everywhere(totals, *total_refs)


def back(tables, held, factors, pooled, later, group, steps, which):
    query_t, pairs = held[2], held[3]
    q_cols, rows = query_t.shape
    slot_len, k_cols = pairs.shape[0], pairs.shape[1] // 2
    kv_heads, heads = k_cols // HD, q_cols // HD
    width = held[0].shape[1]
    pack_cols = q_cols + 2 * k_cols
    full = functools.partial(jax.ShapeDtypeStruct, dtype=jnp.float32)
    in_vmem = pl.BlockSpec(memory_space=pltpu.VMEM)
    anywhere = pl.BlockSpec(memory_space=pl.ANY)
    shard_rows = width // 8
    owned = [full((shard_rows, cols)) for cols in (factors[1].shape[1], q_cols, pack_cols)]
    pool_width = 2 * width + 128
    near = (*tables, *held, *factors, *pooled)
    scratch = [
        pltpu.VMEM((kv_heads, slot_len, HD), jnp.bfloat16),
        pltpu.VMEM((kv_heads, HD, slot_len), jnp.bfloat16),
        pltpu.VMEM((kv_heads, slot_len, HD), jnp.bfloat16),
        pltpu.VMEM((heads, rows, HD), jnp.bfloat16),
        pltpu.VMEM((q_cols, rows), jnp.float32),
        pltpu.VMEM((q_cols, rows), jnp.float32),
        pltpu.VMEM((kv_heads, slot_len, 2 * HD), jnp.float32),
        pltpu.VMEM((kv_heads, rows, 2 * HD), jnp.float32),
        pltpu.VMEM((rows, pack_cols), jnp.bfloat16),
        pltpu.VMEM((rows, width), jnp.bfloat16),
        pltpu.VMEM((steps, width), jnp.float32),
    ]
    scratch += [pltpu.VMEM(item.shape, item.dtype) for item in later]
    scratch += [pltpu.VMEM((1, 128), jnp.float32)] * 3
    scratch += line_scratch(steps, rows, width) + total_scratch(pool_width)
    for item in owned:
        scratch += scatter_scratch(*item.shape)
    return pl.pallas_call(
        functools.partial(back_body, steps, group, BACK_ORDER),
        out_shape=owned + [full((1, pool_width)), jax.ShapeDtypeStruct((rows, width), jnp.bfloat16)],
        in_specs=[in_vmem] * len(near) + [anywhere] * len(later),
        out_specs=[in_vmem] * 4 + [anywhere],
        scratch_shapes=scratch + [pltpu.SemaphoreType.DMA((6,))],
        compiler_params=pltpu.CompilerParams(
            collective_id=which, has_side_effects=True, vmem_limit_bytes=62 << 20
        ),
        cost_estimate=busy(110),
    )(*near, *later)


def on_device(
    tokens,
    teacher,
    lengths,
    loss_mask,
    stretch_order,
    attn_gain,
    w_query,
    w_key,
    w_value,
    w_out,
    mlp_gain,
    w_gate,
    w_up,
    w_down,
    first_moment,
    second_moment,
    gain_first,
    gain_second,
):
    slot_count, stretch_len, model_width = tokens.shape
    token_rows = slot_count * stretch_len
    half_len = stretch_len // 2
    slot_len = stretch_len * lax.axis_size("context")
    all_rows = slot_count * lax.axis_size("dp") * slot_len
    steps = 4
    share_rows = token_rows // 2
    local_index = stretch_len * lax.axis_index("context") + jnp.arange(stretch_len, dtype=jnp.int32)
    query_pos = positions_of(stretch_order, local_index, half_len)
    valid = ((loss_mask == 1) & (query_pos < lengths[:, None])).astype(jnp.float32)
    valid_here = jnp.sum(valid)
    shard_rows = attn_gain.shape[0]
    q_cols, k_cols = w_query.shape[1], w_key.shape[1]
    square = lax.axis_size("dp") == 4 and lax.axis_size("context") == 2
    head_count = q_cols // HD
    kv_count = k_cols // HD
    group_size = head_count // kv_count
    angles = frequencies()[:, None] * query_pos.reshape(1, token_rows).astype(jnp.float32)
    cosine, sine_table = jnp.cos(angles), jnp.sin(angles)
    token_rows_low = tokens.reshape(token_rows, model_width)
    low = functools.partial(jax.ShapeDtypeStruct, dtype=jnp.bfloat16)
    full = functools.partial(jax.ShapeDtypeStruct, dtype=jnp.float32)
    shard_f32 = full((share_rows, model_width))
    shard_low = low((share_rows, model_width))
    gain_parts = full((steps, model_width))
    line = functools.partial(line_sum, steps=steps)
    key_pos = positions_of(stretch_order, jnp.arange(slot_len, dtype=jnp.int32), half_len)
    key_pos = jnp.where(key_pos < lengths[:, None], key_pos, slot_len).reshape(slot_len, 1)
    query_row = query_pos.reshape(1, token_rows)
    if square:
        both_gains = jnp.stack([attn_gain, mlp_gain])
        gain_tiles = jnp.broadcast_to(both_gains[:, None, :], (2, 16, shard_rows))
        count_high = jnp.floor(valid_here / 64.0)
        count_low = valid_here - 64.0 * count_high
        count_tile = jnp.broadcast_to(
            jnp.where(jnp.arange(256)[None, :] < 128, count_high, count_low), (16, 256)
        ).astype(jnp.bfloat16)
        (
            normed, query_t, pairs, mixed_t, mixed_low, stats, gains, state, normed_two,
            first_pack, full_out, full_gate, full_up, full_down, count_whole,
        ) = front(
            token_rows_low,
            (cosine, sine_table, query_row, key_pos),
            (
                w_query, w_key, w_value, w_out, gain_tiles.reshape(32, shard_rows),
                w_gate, w_up, w_down, count_tile,
            ),
            group_size,
            steps,
            0,
        )
        gain_one, gain_two = gains[:1], gains[1:]
        counts = count_whole.reshape(8, 16, 256)[:, 0].astype(jnp.float32)
        valid_count = jnp.sum(64.0 * counts[:, 0] + counts[:, 128])
    else:
        whole = functools.partial(
            lax.all_gather, axis_name=("dp", "context"), axis=0, tiled=True
        )
        first_pack = whole(jnp.concatenate([w_query, w_key, w_value], axis=1))
        full_out, full_gate, full_up, full_down = (
            whole(item) for item in (w_out, w_gate, w_up, w_down)
        )
        gain_one, gain_two = (
            whole(item)[None, :].astype(jnp.float32) for item in (attn_gain, mlp_gain)
        )
        valid_count = lax.psum(valid_here, ("dp", "context"))
        normed, query_t, pairs_here = local_call(
            project_body,
            8,
            [
                low((token_rows, model_width)),
                low((q_cols, token_rows)),
                low((token_rows, 2 * k_cols)),
            ],
            [token_rows_low, gain_one, first_pack, cosine, sine_table],
        )
        pairs = lax.all_gather(pairs_here, "context", axis=0, tiled=True)
        mixed_t, mixed_low, stats, branch_part = local_call(
            functools.partial(attend_body, group_size),
            20,
            [
                full((q_cols, token_rows)),
                low((token_rows, q_cols)),
                full((head_count, 2, token_rows)),
                low((token_rows, model_width)),
            ],
            [query_t, pairs, query_row, key_pos, full_out],
            [
                pltpu.VMEM((kv_count, slot_len, HD), jnp.bfloat16),
                pltpu.VMEM((kv_count, HD, slot_len), jnp.bfloat16),
                pltpu.VMEM((slot_len, token_rows), jnp.float32),
                pltpu.VMEM((q_cols, token_rows), jnp.float32),
            ],
        )
        normed_two, state = line(
            finish_branch, branch_part, (token_rows_low, gain_two), [shard_f32], 0
        )
    gate, up, product, output_part = by_units(
        ffn_body,
        normed_two,
        [full_gate, full_up, full_down],
        [],
        [jnp.float32, jnp.float32, jnp.bfloat16],
        18,
    )
    factor = jnp.float32(all_rows) / valid_count * valid.reshape(token_rows, 1)
    grad_ffn, output_low, grad_output = line(
        finish_output,
        output_part,
        (state, teacher.reshape(token_rows, model_width), factor),
        [shard_low, shard_f32],
        1,
    )
    own_half = lax.ppermute(output_low, "tensor", [(1, 0), (2, 3)])
    crossed_half = lax.ppermute(output_low, "tensor", [(1, 2), (2, 1)])
    grad_gate, grad_up, normed_part = by_units(
        ffn_back_body,
        grad_ffn,
        [full_gate, full_up, full_down],
        [gate, up],
        [jnp.bfloat16, jnp.bfloat16],
        18,
    )
    normed_part, own_half, crossed_half = lax.optimization_barrier(
        (normed_part, own_half, crossed_half)
    )
    other_half = lax.ppermute(crossed_half, "tensor", [(1, 0), (2, 3)])
    owner_sum = functools.partial(
        lax.psum_scatter, axis_name=("dp", "context"), scatter_dimension=0, tiled=True
    )

    def owned(left, right):
        return owner_sum(column_term(left, right).astype(jnp.bfloat16)).astype(jnp.float32)

    if not square:
        owned_down = owned(grad_ffn, product)
        owned_gate = owned(normed_two, grad_gate)
        owned_up = owned(normed_two, grad_up)
    grad_branch, grad_state, gain_two_parts, *late = line(
        finish_ffn_back,
        normed_part,
        (state, grad_output, gain_two),
        [shard_f32, gain_parts],
        2,
        factors=((grad_ffn, product), (normed_two, grad_gate)) if square else (),
        order=FFN_BACK_ORDER if square else (),
    )
    if square:
        owned_down, owned_gate, squares_down, squares_gate = late
    if not square:
        owned_out = owned(grad_branch, mixed_low)
    grad_branch, other_half = lax.optimization_barrier((grad_branch, other_half))
    block_out = join_halves(output_low, own_half, crossed_half, other_half)
    if square:
        owned_up, owned_out, owned_qkv, totals, grad_tokens = back(
            (cosine, sine_table, query_row, key_pos),
            (grad_branch, full_out, query_t, pairs, mixed_t, stats, gains),
            (normed_two, grad_up, mixed_low),
            (gain_two_parts, squares_down, squares_gate),
            (first_pack, token_rows_low, grad_state, normed),
            group_size,
            steps,
            3,
        )
    else:
        grad_query, grad_pairs = local_call(
            functools.partial(attend_back_body, group_size),
            24,
            [low((token_rows, q_cols)), full((kv_count, slot_len, 2 * HD))],
            [
                grad_branch, full_out, query_t, pairs, mixed_t, stats, query_row, key_pos,
                cosine, sine_table,
            ],
            [
                pltpu.VMEM((kv_count, slot_len, HD), jnp.bfloat16),
                pltpu.VMEM((kv_count, HD, slot_len), jnp.bfloat16),
                pltpu.VMEM((kv_count, slot_len, HD), jnp.bfloat16),
                pltpu.VMEM((head_count, token_rows, HD), jnp.bfloat16),
                pltpu.VMEM((q_cols, token_rows), jnp.float32),
                pltpu.VMEM((q_cols, token_rows), jnp.float32),
            ],
        )
        grad_pairs_own = lax.psum_scatter(
            grad_pairs, "context", scatter_dimension=1, tiled=True
        )
        grad_lin, inputs_part = local_call(
            join_body,
            6,
            [low((token_rows, q_cols + 2 * k_cols)), low((token_rows, model_width))],
            [grad_query, grad_pairs_own, cosine, sine_table, first_pack],
        )
        owned_qkv = owned(normed, grad_lin)
        grad_tokens, gain_one_parts = line(
            finish_attn_back, inputs_part, (token_rows_low, grad_state, gain_one), [gain_parts], 3
        )
    owned_all = [owned_qkv, owned_out, owned_gate, owned_up, owned_down]
    gain_cols = 2 * model_width
    if not square:
        square_local = sum(jnp.sum(part * part) for part in owned_all)
        totals = lax.psum(
            jnp.concatenate(
                [
                    jnp.sum(gain_one_parts, axis=0),
                    jnp.sum(gain_two_parts, axis=0),
                    jnp.full((128,), square_local / 128.0),
                ]
            )[None, :],
            ("dp", "context", "tensor"),
        )
    gains_owned = lax.dynamic_slice_in_dim(
        totals[0, :gain_cols].reshape(2, model_width),
        lax.axis_index(("dp", "context")) * shard_rows,
        shard_rows,
        1,
    )
    widths = (q_cols, k_cols, k_cols) + tuple(item.shape[1] for item in owned_all[1:])
    *matrices, adam_step = update_rows(
        owned_all, first_moment, second_moment, totals, gain_cols, widths
    )
    gain_step = adam_direction(
        gains_owned, gain_first, gain_second, clip_of(totals, gain_cols)
    )
    return (
        block_out.reshape(slot_count, stretch_len, model_width),
        grad_tokens.reshape(slot_count, stretch_len, model_width),
        gains_owned[0],
        matrices[0],
        matrices[1],
        matrices[2],
        matrices[3],
        gains_owned[1],
        matrices[4],
        matrices[5],
        matrices[6],
        adam_step,
        gain_step,
    )


def solution(mesh):
    in_specs = (
        P("dp", "context", None),
        P("dp", "context", None),
        P("dp"),
        P("dp", "context"),
        P("dp", None),
        P(("dp", "context")),
        P(("dp", "context"), "tensor"),
        P(("dp", "context"), "tensor"),
        P(("dp", "context"), "tensor"),
        P(("dp", "context"), "tensor"),
        P(("dp", "context")),
        P(("dp", "context"), "tensor"),
        P(("dp", "context"), "tensor"),
        P(("dp", "context"), "tensor"),
        P(("dp", "context"), "tensor"),
        P(("dp", "context"), "tensor"),
        P(None, ("dp", "context")),
        P(None, ("dp", "context")),
    )
    out_specs = (
        P("dp", "context", None),
        P("dp", "context", None),
        P(("dp", "context")),
        P(("dp", "context"), "tensor"),
        P(("dp", "context"), "tensor"),
        P(("dp", "context"), "tensor"),
        P(("dp", "context"), "tensor"),
        P(("dp", "context")),
        P(("dp", "context"), "tensor"),
        P(("dp", "context"), "tensor"),
        P(("dp", "context"), "tensor"),
        P(("dp", "context"), "tensor"),
        P(None, ("dp", "context")),
    )
    return jax.shard_map(
        on_device, mesh=mesh, in_specs=in_specs, out_specs=out_specs, check_vma=False
    )
```

```python
import functools
import math

import jax
import jax.numpy as jnp
from jax import lax
from jax.experimental import pallas as pl
from jax.experimental.pallas import tpu as pltpu
from jax.sharding import PartitionSpec as P

HD = 64
STEP = 10


EPS_NORM = 1e-05
ROPE_BASE = 500000.0
OLD_CONTEXT = 8192.0
SCALE_FACTOR = 32.0
LOW_FACTOR = 1.0
HIGH_FACTOR = 4.0
LOG2E = 1.4426950408889634
NEG_FILL = -1e30
BETA_ONE = 0.9
BETA_TWO = 0.95
ADAM_EPS = 1e-08
CLIP_NORM = 1.0


def frequencies():
    channel = jnp.arange(HD // 2, dtype=jnp.float32)
    base_freq = jnp.power(jnp.float32(ROPE_BASE), -2.0 * channel / HD)
    wavelength = 2.0 * math.pi / base_freq
    smooth = (OLD_CONTEXT / wavelength - LOW_FACTOR) / (HIGH_FACTOR - LOW_FACTOR)
    blended = (1.0 - smooth) * base_freq / SCALE_FACTOR + smooth * base_freq
    slow_freq = jnp.where(wavelength > OLD_CONTEXT / LOW_FACTOR, base_freq / SCALE_FACTOR, blended)
    return jnp.where(wavelength < OLD_CONTEXT / HIGH_FACTOR, base_freq, slow_freq)


def normalize(values, gain):
    factor = lax.rsqrt(jnp.mean(values * values, axis=-1, keepdims=True) + EPS_NORM)
    return values * factor * gain.astype(jnp.float32)


def normalize_back(values, gain, upstream):
    factor = lax.rsqrt(jnp.mean(values * values, axis=-1, keepdims=True) + EPS_NORM)
    unit_rows = values * factor
    gain_grad = jnp.sum(upstream * unit_rows, axis=0)
    scaled_up = upstream * gain.astype(jnp.float32)
    input_grad = factor * (
        scaled_up - unit_rows * jnp.mean(scaled_up * unit_rows, axis=-1, keepdims=True)
    )
    return (input_grad, gain_grad)


def positions_of(order_table, row_index, half_len):
    stretch_slot = row_index // half_len
    matches = stretch_slot[:, None] == jnp.arange(order_table.shape[1], dtype=jnp.int32)[None, :]
    stretch_ids = jnp.sum(jnp.where(matches[None, :, :], order_table[:, None, :], 0), axis=-1)
    return stretch_ids * half_len + row_index % half_len


def times_transpose(left, right):
    return lax.dot_general(
        left, right, (((1,), (1,)), ((), ())), preferred_element_type=jnp.float32
    )


def column_term(left, right):
    return lax.dot_general(
        left, right, (((0,), (0,)), ((), ())), preferred_element_type=jnp.float32
    )


def adam_direction(gradient, first, second, clip_factor):
    clipped = gradient * clip_factor
    first_new = BETA_ONE * first + (1.0 - BETA_ONE) * clipped
    second_new = BETA_TWO * second + (1.0 - BETA_TWO) * clipped * clipped
    return (
        first_new
        / (1.0 - BETA_ONE**STEP)
        / (jnp.sqrt(second_new / (1.0 - BETA_TWO**STEP)) + ADAM_EPS)
    )


MESH_ID = pl.DeviceIdType.MESH


def row_mean(values):
    return jnp.mean(values, axis=-1, keepdims=True)


def line_place():
    place = lax.axis_index("tensor")
    side = place // 2
    inner = place + 1 - 2 * side
    outer = jnp.clip(place - 1 + 2 * side, 0, 3)
    return (place == 0) | (place == 3), side, {"tensor": inner}, {"tensor": outer}


def square_peers():
    ring, core = lax.axis_index("dp"), lax.axis_index("context")
    across = ring + 1 - 2 * (ring % 2)
    along = (ring + 2) % 4
    first = across * (1 - core) + along * core
    second = along * (1 - core) + across * core
    return ring, core, first, second, 3 - ring


def meet(with_line, with_square, with_all=False):
    barrier = pltpu.get_barrier_semaphore()
    expected = jnp.int32(0)
    if with_all:
        place = lax.axis_index("tensor")
        for hop in (1, 2, 3):
            pl.semaphore_signal(
                barrier,
                inc=1,
                device_id={"tensor": (place + hop) % 4},
                device_id_type=MESH_ID,
            )
        expected = expected + 3
    elif with_line:
        at_end, side, inner, outer = line_place()
        pl.semaphore_signal(barrier, inc=1, device_id=inner, device_id_type=MESH_ID)

        @pl.when(jnp.logical_not(at_end))
        def _():
            pl.semaphore_signal(barrier, inc=1, device_id=outer, device_id_type=MESH_ID)

        expected = expected + 2 - at_end.astype(jnp.int32)
    if with_square:
        ring, core, first, second, far = square_peers()
        for target in ({"dp": first}, {"dp": second}, {"context": 1 - core}):
            pl.semaphore_signal(barrier, inc=1, device_id=target, device_id_type=MESH_ID)
        expected = expected + 3
    pl.semaphore_wait(barrier, expected)


def line_scratch(steps, total_rows, width):
    rows = total_rows // 2 // steps
    return [
        pltpu.VMEM((2, steps, rows, width), jnp.bfloat16),
        pltpu.VMEM((steps, rows, width), jnp.bfloat16),
        pltpu.VMEM((steps, rows, width), jnp.bfloat16),
        pltpu.SemaphoreType.DMA((12, steps)),
    ]


def line_events(steps, finish, part, extra, out, kept, scratch, watch=False):
    outer_in, cross_in, done, sems = scratch
    at_end, side, inner, outer = line_place()
    in_middle = jnp.logical_not(at_end)
    half = part.shape[0] // 2
    rows = half // steps

    def near(step):
        return pl.ds(pl.multiple_of(side * half + step * rows, rows), rows)

    def far(step):
        return pl.ds(pl.multiple_of((1 - side) * half + step * rows, rows), rows)

    def remote(src, dst, send, recv, step, target):
        return pltpu.make_async_remote_copy(
            src_ref=src,
            dst_ref=dst,
            send_sem=sems.at[send, step],
            recv_sem=sems.at[recv, step],
            device_id=target,
            device_id_type=MESH_ID,
        )

    def inward(kind, step):
        span = near(step) if kind else far(step)
        return remote(part.at[span], outer_in.at[kind, step], kind, 2 + kind, step, inner)

    def across(step):
        return remote(outer_in.at[0, step], cross_in.at[step], 4, 5, step, inner)

    def hand_outer(step):
        return remote(done.at[step], out.at[near(step)], 6, 9, step, outer)

    def hand_inner(step):
        return remote(done.at[step], out.at[near(step)], 7, 10, step, inner)

    def hand_on(step):
        return remote(out.at[far(step)], out.at[far(step)], 8, 10, step, outer)

    def keep(step):
        return pltpu.make_async_copy(done.at[step], out.at[near(step)], sems.at[11, step])

    def feed(index):
        step, kind = divmod(index, 2)
        if index >= 2:
            inward(kind, step - 1).wait_send()
        inward(kind, step).start()

    def pass_on(step):
        hand_inner(step).wait_recv()
        hand_on(step).start()

    def arrive(step):
        @pl.when(in_middle)
        def _():
            keep(step).wait()

        @pl.when(at_end)
        def _():
            hand_outer(step).wait_recv()
            hand_on(step).wait_recv()

    @pl.when(at_end)
    def _():
        feed(0)
        feed(1)

    for item in kept:
        if item.shape[0] == steps:
            item[...] = jnp.zeros_like(item)
    yield
    for step in range(steps):

        @pl.when(at_end)
        def _():
            if step + 1 < steps:
                feed(2 * step + 2)

        @pl.when(in_middle)
        def _():
            inward(0, step).wait_recv()
            outer_in[0, step] = (
                outer_in[0, step].astype(jnp.float32) + part[far(step), :].astype(jnp.float32)
            ).astype(jnp.bfloat16)
            across(step).start()

        yield

        @pl.when(at_end)
        def _():
            if step + 1 < steps:
                feed(2 * step + 3)

        @pl.when(in_middle)
        def _():
            inward(1, step).wait_recv()
            across(step).wait_recv()
            total = (
                part[near(step), :].astype(jnp.float32)
                + outer_in[1, step].astype(jnp.float32)
                + cross_in[step].astype(jnp.float32)
            )
            finish(total, near(step), pl.ds(step * rows, rows), step, done, extra, kept)
            hand_outer(step).start()
            hand_inner(step).start()
            keep(step).start()
            if step > 0:
                pass_on(step - 1)

        yield
        if watch and step >= 2:
            arrive(step - 2)
            yield

    @pl.when(in_middle)
    def _():
        pass_on(steps - 1)

    @pl.when(at_end)
    def _():
        for kind in range(2):
            inward(kind, steps - 1).wait_send()

    if watch:
        yield
    for step in range(steps - 2 if watch else 0, steps):
        arrive(step)
        if watch:
            yield

    @pl.when(in_middle)
    def _():
        for step in range(steps):
            across(step).wait_send()
            hand_outer(step).wait_send()
            hand_inner(step).wait_send()
            hand_on(step).wait_send()

    yield


def gather_events(src, dst, sems):
    rows = src.shape[0]
    ring, core, first, second, far = square_peers()
    to_first, to_second, to_twin = {"dp": first}, {"dp": second}, {"context": 1 - core}

    def span(owner_ring, owner_core):
        return pl.ds(pl.multiple_of((owner_ring * 2 + owner_core) * rows, rows), rows)

    def copy(source, owner_ring, owner_core, slot, target):
        return pltpu.make_async_remote_copy(
            src_ref=source,
            dst_ref=dst.at[span(owner_ring, owner_core)],
            send_sem=sems.at[slot],
            recv_sem=sems.at[8 + owner_ring * 2 + owner_core],
            device_id=target,
            device_id_type=MESH_ID,
        )

    own = pltpu.make_async_copy(src, dst.at[span(ring, core)], sems.at[7])
    copy(src, ring, core, 0, to_first).start()
    copy(src, ring, core, 1, to_second).start()
    copy(src, ring, core, 2, to_twin).start()
    own.start()
    yield
    block = dst.at[span(first, core)]
    copy(block, first, core, 3, to_second).wait_recv()
    copy(block, first, core, 3, to_second).start()
    copy(block, first, core, 4, to_twin).start()
    yield
    block = dst.at[span(second, core)]
    copy(block, second, core, 5, to_twin).wait_recv()
    copy(block, second, core, 5, to_twin).start()
    yield
    block = dst.at[span(far, core)]
    copy(block, far, core, 6, to_twin).wait_recv()
    copy(block, far, core, 6, to_twin).start()
    yield
    for owner_ring in (ring, first, second, far):
        block = dst.at[span(owner_ring, 1 - core)]
        copy(block, owner_ring, 1 - core, 2, to_twin).wait_recv()
    for slot in range(7):
        copy(src, ring, core, slot, to_twin).wait_send()
    own.wait()
    yield


def lane_sums(item):
    sums = jnp.sum(item[...] * item[...], axis=0, keepdims=True)
    return sum(sums[:, first : first + 128] for first in range(0, sums.shape[1], 128))


def scatter_scratch(rows, cols):
    return [
        pltpu.VMEM((2, rows, cols), jnp.bfloat16),
        pltpu.VMEM((4, rows, cols), jnp.bfloat16),
        pltpu.VMEM((2, rows, cols), jnp.bfloat16),
        pltpu.VMEM((1, rows, cols), jnp.bfloat16),
        pltpu.SemaphoreType.DMA((14,)),
    ]


def scatter_events(left, right, out, square, scratch):
    twin_out, twin_in, first_in, second_in, sems = scratch
    rows = out.shape[0]
    ring, core, first, second, far = square_peers()
    to_first, to_second, to_twin = {"dp": first}, {"dp": second}, {"context": 1 - core}
    own_order = (far, first, second, ring)
    twin_order = (far, second, first, ring)

    def block(owner_ring, owner_core):
        span = pl.ds(pl.multiple_of((owner_ring * 2 + owner_core) * rows, rows), rows)
        return column_term(left[:, span], right[...])

    def remote(src, dst, slot, target):
        return pltpu.make_async_remote_copy(
            src_ref=src,
            dst_ref=dst,
            send_sem=sems.at[slot],
            recv_sem=sems.at[7 + slot],
            device_id=target,
            device_id_type=MESH_ID,
        )

    def swap(role):
        return remote(twin_out.at[role % 2], twin_in.at[role], role, to_twin)

    def over_first(role):
        return remote(twin_in.at[role], first_in.at[role], 4 + role, to_first)

    over_second = remote(twin_in.at[2], second_in.at[0], 6, to_second)

    def for_twin(role):
        if role >= 2:
            swap(role - 2).wait_send()
        twin_out[role % 2] = block(twin_order[role], 1 - core).astype(jnp.bfloat16)
        swap(role).start()

    for role in range(2):
        for_twin(role)
        yield
    for role in range(2):
        term = block(own_order[role], core)
        swap(role).wait_recv()
        twin_in[role] = (term + twin_in[role].astype(jnp.float32)).astype(jnp.bfloat16)
        over_first(role).start()
        yield
    for_twin(2)
    yield
    for_twin(3)
    yield
    term = block(second, core)
    swap(2).wait_recv()
    over_first(0).wait_recv()
    twin_in[2] = (
        term + twin_in[2].astype(jnp.float32) + first_in[0].astype(jnp.float32)
    ).astype(jnp.bfloat16)
    over_second.start()
    yield
    term = block(ring, core)
    swap(3).wait_recv()
    over_first(1).wait_recv()
    out[...] = term + twin_in[3].astype(jnp.float32) + first_in[1].astype(jnp.float32)
    yield
    over_second.wait_recv()
    out[...] += second_in[0].astype(jnp.float32)
    square[...] = lane_sums(out)
    swap(2).wait_send()
    swap(3).wait_send()
    over_first(0).wait_send()
    over_first(1).wait_send()
    over_second.wait_send()
    yield


def total_scratch(width):
    return [
        pltpu.VMEM((7, 1, width), jnp.float32),
        pltpu.VMEM((4, 1, width), jnp.float32),
        pltpu.SemaphoreType.DMA((13,)),
    ]


def total_everywhere(out, taken, line_in, sems):
    ring, core, first, second, far = square_peers()
    place = lax.axis_index("tensor")
    across = ring + 1 - 2 * (ring % 2)
    along = (ring + 2) % 4
    others = [{"tensor": (place + hop) % 4} for hop in (1, 2, 3)]
    for stage, target in enumerate(({"context": 1 - core}, {"dp": across}, {"dp": along})):
        copy = pltpu.make_async_remote_copy(
            src_ref=taken.at[2 * stage],
            dst_ref=taken.at[2 * stage + 1],
            send_sem=sems.at[stage],
            recv_sem=sems.at[3 + stage],
            device_id=target,
            device_id_type=MESH_ID,
        )
        copy.start()
        copy.wait()
        taken[2 * stage + 2] = taken[2 * stage] + taken[2 * stage + 1]

    def along_line(hop, owner):
        return pltpu.make_async_remote_copy(
            src_ref=taken.at[6],
            dst_ref=line_in.at[owner],
            send_sem=sems.at[6 + hop],
            recv_sem=sems.at[9 + owner],
            device_id=others[hop],
            device_id_type=MESH_ID,
        )

    for hop in range(3):
        along_line(hop, place).start()
    line_in[place] = taken[6]
    for hop in range(3):
        along_line(hop, (place + hop + 1) % 4).wait_recv()
    out[...] = (line_in[0] + line_in[1]) + (line_in[2] + line_in[3])
    for hop in range(3):
        along_line(hop, place).wait_send()


def clip_of(totals, gain_cols):
    gains, squares = totals[:, :gain_cols], totals[:, gain_cols:]
    square_all = jnp.sum(squares) + jnp.sum(gains * gains)
    return CLIP_NORM / jnp.maximum(jnp.sqrt(square_all), CLIP_NORM)


def update_body(widths, gain_cols, totals, *refs):
    owned, (first, second), outs = refs[:5], refs[5:7], refs[7:]
    clip_factor = clip_of(totals[...], gain_cols)
    bounds = [0, widths[0], widths[0] + widths[1], sum(widths[:3])]
    grads = [owned[0][:, bounds[place] : bounds[place + 1]] for place in range(3)]
    grads += [item[...] for item in owned[1:]]
    start = 0
    for grad, grad_out in zip(grads, outs[:7]):
        grad_out[...] = grad
        span = slice(start, start + grad.shape[1])
        outs[7][:, span] = adam_direction(grad, first[:, span], second[:, span], clip_factor)
        start = start + grad.shape[1]


def update_rows(owned, first, second, totals, gain_cols, widths):
    shard_rows, pack_cols = first.shape
    rows = min(32, shard_rows)

    def block(width):
        return pl.BlockSpec((rows, width), lambda row: (row, 0))

    return pl.pallas_call(
        functools.partial(update_body, widths, gain_cols),
        grid=(shard_rows // rows,),
        out_shape=[jax.ShapeDtypeStruct((shard_rows, width), jnp.float32) for width in widths]
        + [jax.ShapeDtypeStruct((shard_rows, pack_cols), jnp.float32)],
        in_specs=[pl.BlockSpec(totals.shape, lambda row: (0, 0))]
        + [block(item.shape[1]) for item in owned]
        + [block(pack_cols)] * 2,
        out_specs=[block(width) for width in widths] + [block(pack_cols)],
        compiler_params=pltpu.CompilerParams(vmem_limit_bytes=48 << 20),
        cost_estimate=busy(15),
    )(totals, *owned, first, second)


def busy(microseconds):
    return pl.CostEstimate(
        flops=microseconds * 10**9, bytes_accessed=1 << 20, transcendentals=0
    )


def weave(order):
    for events in order:
        next(events, None)
    for events in order:
        for _ in events:
            pass


def line_body(steps, finish, extra_count, kept_count, *refs):
    part, extra, out = refs[0], refs[1 : 1 + extra_count], refs[1 + extra_count]
    kept, scratch = refs[2 + extra_count : 2 + extra_count + kept_count], refs[-4:]
    meet(True, False)
    weave([line_events(steps, finish, part, extra, out, kept, scratch)])


def line_sum(finish, part, extra, kept, which, steps):
    total_rows, width = part.shape
    in_vmem = pl.BlockSpec(memory_space=pltpu.VMEM)
    return pl.pallas_call(
        functools.partial(line_body, steps, finish, len(extra), len(kept)),
        out_shape=[jax.ShapeDtypeStruct((total_rows, width), jnp.bfloat16)] + kept,
        in_specs=[in_vmem] * (1 + len(extra)),
        out_specs=[pl.BlockSpec(memory_space=pl.ANY)] + [in_vmem] * len(kept),
        scratch_shapes=line_scratch(steps, total_rows, width),
        compiler_params=pltpu.CompilerParams(
            collective_id=which, has_side_effects=True, vmem_limit_bytes=60 << 20
        ),
        cost_estimate=busy(70),
    )(part, *extra)


def join_halves(held, own, crossed, other):
    place = lax.axis_index("tensor")
    at_end = (place == 0) | (place == 3)
    own = jnp.where(at_end, own, held)
    other = jnp.where(at_end, other, crossed)
    low_side = place < 2
    return jnp.concatenate(
        [jnp.where(low_side, own, other), jnp.where(low_side, other, own)], axis=0
    )


def finish_branch(total, own, local, step, done, extra, kept):
    tokens, gain = extra
    (state,) = kept
    rows_now = tokens[own, :].astype(jnp.float32) + total
    state[local, :] = rows_now
    done[step] = normalize(rows_now, gain[...]).astype(jnp.bfloat16)


def finish_output(total, own, local, step, done, extra, kept):
    state, teacher, factor = extra
    output_low, grad_output = kept
    output = state[local, :] + total
    output_low[local, :] = output.astype(jnp.bfloat16)
    grad_now = factor[own, :] * (output - teacher[own, :].astype(jnp.float32))
    grad_output[local, :] = grad_now
    done[step] = grad_now.astype(jnp.bfloat16)


def finish_ffn_back(total, own, local, step, done, extra, kept):
    state, grad_output, gain = extra
    grad_state, gain_grad = kept
    input_grad, gain_now = normalize_back(state[local, :], gain[...], total)
    grad_now = grad_output[local, :] + input_grad
    grad_state[local, :] = grad_now
    gain_grad[step : step + 1, :] = gain_now[None, :]
    done[step] = grad_now.astype(jnp.bfloat16)


def finish_attn_back(total, own, local, step, done, extra, kept):
    tokens, grad_state, gain = extra
    (gain_grad,) = kept
    input_grad, gain_now = normalize_back(tokens[own, :].astype(jnp.float32), gain[...], total)
    gain_grad[step : step + 1, :] = gain_now[None, :]
    done[step] = (grad_state[local, :] + input_grad).astype(jnp.bfloat16)


def local_call(body, time, outs, operands, scratch=(), vmem=60):
    in_vmem = pl.BlockSpec(memory_space=pltpu.VMEM)
    return pl.pallas_call(
        body,
        out_shape=outs,
        in_specs=[in_vmem] * len(operands),
        out_specs=[in_vmem] * len(outs),
        scratch_shapes=list(scratch),
        compiler_params=pltpu.CompilerParams(vmem_limit_bytes=vmem << 20),
        cost_estimate=busy(time),
    )(*operands)


def ffn_body(normed, w_gate, w_up, w_down, gate, up, product, part, total):
    step = pl.program_id(0)
    gate_now = jnp.dot(normed[...], w_gate[...], preferred_element_type=jnp.float32)
    up_now = jnp.dot(normed[...], w_up[...], preferred_element_type=jnp.float32)
    gate[...] = gate_now
    up[...] = up_now
    product_now = (gate_now * jax.nn.sigmoid(gate_now) * up_now).astype(jnp.bfloat16)
    product[...] = product_now
    accumulate(step, total, part, times_transpose(product_now, w_down[...]))


def ffn_back_body(
    grad_rows, w_gate, w_up, w_down, gate, up, grad_gate, grad_up, part, total
):
    step = pl.program_id(0)
    grad_product = jnp.dot(grad_rows[...], w_down[...], preferred_element_type=jnp.float32)
    gate_now = gate[...]
    sigmoid_gate = jax.nn.sigmoid(gate_now)
    gate_low = (
        grad_product * up[...] * sigmoid_gate * (1.0 + gate_now * (1.0 - sigmoid_gate))
    ).astype(jnp.bfloat16)
    up_low = (grad_product * (gate_now * sigmoid_gate)).astype(jnp.bfloat16)
    grad_gate[...] = gate_low
    grad_up[...] = up_low
    accumulate(
        step,
        total,
        part,
        times_transpose(gate_low, w_gate[...]) + times_transpose(up_low, w_up[...]),
    )


def accumulate(step, total, part, term):
    last = pl.num_programs(0) - 1

    @pl.when(step == 0)
    def _():
        total[...] = term

    @pl.when((step > 0) & (step < last))
    def _():
        total[...] += term

    @pl.when(step == last)
    def _():
        part[...] = (total[...] + term).astype(jnp.bfloat16)


def by_units(body, rows_in, weights, by_columns, outs, time):
    rows, width = rows_in.shape
    units = weights[0].shape[1]
    block = min(UNIT_BLOCK, units)

    def columns(depth):
        return pl.BlockSpec((depth, block), lambda step: (0, step))

    whole = pl.BlockSpec((rows, width), lambda step: (0, 0))
    return pl.pallas_call(
        body,
        grid=(units // block,),
        out_shape=[jax.ShapeDtypeStruct((rows, units), kind) for kind in outs]
        + [jax.ShapeDtypeStruct((rows, width), jnp.bfloat16)],
        in_specs=[whole]
        + [columns(item.shape[0]) for item in weights]
        + [columns(rows) for _ in by_columns],
        out_specs=[columns(rows) for _ in outs] + [whole],
        scratch_shapes=[pltpu.VMEM((rows, width), jnp.float32)],
        compiler_params=pltpu.CompilerParams(vmem_limit_bytes=56 << 20),
        cost_estimate=busy(time),
    )(rows_in, *weights, *by_columns)


UNIT_BLOCK = 512


MIDDLE_BLOCK = 256


def finish_output_near(total, own, local, step, done, extra, kept):
    state, teacher, factor = extra
    output_low, grad_output = kept
    output = state[local, :] + total
    output_low[local, :] = output.astype(jnp.bfloat16)
    grad_now = factor[own, :] * (output - teacher[local, :].astype(jnp.float32))
    grad_output[local, :] = grad_now
    done[step] = grad_now.astype(jnp.bfloat16)


MIDDLE_ORDER = (
    "c", "c", "l1", "c", "l1", "c", "l1", "l1", "l1", "l1",
    "l1", "l1", "l1", "l1", "l1", "c", "c", "l1", "c", "l1",
    "l2", "l1", "c", "s0", "s0", "s0", "s0", "c", "l2", "c",
    "l1", "l2", "s1", "s1", "s1", "s1", "l2", "s0", "s0", "l2",
    "s1", "s1", "l2", "s0", "s0", "l2", "l2", "l2", "s1", "s1",
    "l2",
)


def middle_body(steps, order, *refs):
    refs = list(refs)

    def take(count):
        taken = refs[:count]
        del refs[:count]
        return taken

    state, factor, gains = take(3)
    normed_two, teacher, *weights = take(5)
    output_low, grad_up, grad_state, gain_parts = take(4)
    owned, squares = take(2), take(2)
    grad_ffn, grad_branch, inner_store = take(3)
    normed, product, grads_in, grad_gate, part, total, teacher_near = take(7)
    slots, kept_out, kept_in = take(3), *take(2)
    first_line, second_line = take(4), take(4)
    scatter_refs = [take(5), take(5)]
    weight_sems, store_sems, load_sems, row_sems = take(4)
    at_end, side, inner, outer = line_place()
    rows, width = normed.shape
    half, quarter = rows // 2, rows // 4
    units = weights[0].shape[1]
    block = MIDDLE_BLOCK
    blocks = units // block
    meet(True, True)

    def chunk_copy(source, target, chunk, sem):
        return [
            pltpu.make_async_copy(
                source.at[pl.ds(part_of * half + chunk * quarter, quarter)],
                target.at[pl.ds(chunk * half + part_of * quarter, quarter)],
                row_sems.at[sem + part_of],
            )
            for part_of in range(2)
        ]

    near_rows = pl.ds(pl.multiple_of(side * half, half), half)
    load_teacher = pltpu.make_async_copy(teacher.at[near_rows], teacher_near, row_sems.at[8])
    load_teacher.start()
    loads = chunk_copy(normed_two, normed, 0, 0) + chunk_copy(normed_two, normed, 1, 2)
    for load in loads:
        load.start()

    def columns(index):
        return pl.ds(pl.multiple_of(lax.rem(index, blocks) * block, block), block)

    def weight_copies(index):
        slot = lax.rem(index, 2)
        return [
            pltpu.make_async_copy(
                weight.at[:, columns(index)], item.at[slot], weight_sems.at[place, slot]
            )
            for place, (weight, item) in enumerate(zip(weights, slots))
        ]

    def store(index):
        slot = lax.rem(index, 2)
        return pltpu.make_async_copy(kept_out.at[slot], inner_store.at[index], store_sems.at[slot])

    def restore(index):
        slot = lax.rem(index, 2)
        return pltpu.make_async_copy(
            inner_store.at[index - 2 * blocks], kept_in.at[slot], load_sems.at[slot]
        )

    def fetch(index):
        for copy in weight_copies(index):
            copy.start()

        @pl.when(index >= 2 * blocks)
        def _():
            restore(index).start()

    def add_term(index, term):
        @pl.when(lax.rem(index, blocks) == 0)
        def _():
            total[...] = term

        @pl.when(lax.rem(index, blocks) > 0)
        def _():
            total[...] += term

    def put_part(chunk):
        for part_of in range(2):
            part[pl.ds(part_of * half + chunk * quarter, quarter), :] = total[
                pl.ds(part_of * quarter, quarter), :
            ].astype(jnp.bfloat16)

    def chunk_rows(chunk):
        return pl.ds(chunk * half, half)

    def forward(chunk, index):
        slot = lax.rem(index, 2)
        fetch(index + 1)
        for copy in weight_copies(index):
            copy.wait()
        gate = jnp.dot(
            normed[chunk_rows(chunk), :], slots[0][slot], preferred_element_type=jnp.float32
        )
        up = jnp.dot(
            normed[chunk_rows(chunk), :], slots[1][slot], preferred_element_type=jnp.float32
        )

        @pl.when(index >= 2)
        def _():
            store(index - 2).wait()

        kept_out[slot, 0] = gate
        kept_out[slot, 1] = up
        store(index).start()
        product_now = (gate * jax.nn.sigmoid(gate) * up).astype(jnp.bfloat16)
        product[chunk_rows(chunk), columns(index)] = product_now
        add_term(index, times_transpose(product_now, slots[2][slot]))

    def backward(chunk, index):
        slot = lax.rem(index, 2)

        @pl.when(index + 1 < 4 * blocks)
        def _():
            fetch(index + 1)

        for copy in weight_copies(index):
            copy.wait()
        restore(index).wait()
        grad_product = jnp.dot(
            grads_in[chunk_rows(chunk), :], slots[2][slot], preferred_element_type=jnp.float32
        )
        gate, up = kept_in[slot, 0], kept_in[slot, 1]
        sigmoid_gate = jax.nn.sigmoid(gate)
        gate_low = (
            grad_product * up * sigmoid_gate * (1.0 + gate * (1.0 - sigmoid_gate))
        ).astype(jnp.bfloat16)
        up_low = (grad_product * (gate * sigmoid_gate)).astype(jnp.bfloat16)
        grad_gate[chunk_rows(chunk), columns(index)] = gate_low
        for part_of in range(2):
            grad_up[pl.ds(part_of * half + chunk * quarter, quarter), columns(index)] = up_low[
                part_of * quarter : (part_of + 1) * quarter
            ]
        add_term(
            index,
            times_transpose(gate_low, slots[0][slot]) + times_transpose(up_low, slots[1][slot]),
        )

    def compute():
        fetch(jnp.int32(0))
        for load in loads:
            load.wait()
        for chunk in range(2):
            for piece in range(2):
                first = chunk * blocks + piece * blocks // 2

                @pl.loop(first, first + blocks // 2)
                def _(index):
                    forward(chunk, index)

                if piece == 1:
                    put_part(chunk)
                    if chunk == 0:
                        load_teacher.wait()
                yield
        store(jnp.int32(2 * blocks - 2)).wait()
        store(jnp.int32(2 * blocks - 1)).wait()
        for chunk in range(2):
            copies = chunk_copy(grad_ffn, grads_in, chunk, 4 + 2 * chunk)
            for copy in copies:
                copy.start()
            for copy in copies:
                copy.wait()
            yield
            for piece in range(2):
                first = (2 + chunk) * blocks + piece * blocks // 2

                @pl.loop(first, first + blocks // 2)
                def _(index):
                    backward(chunk, index)

                if piece == 1:
                    put_part(chunk)
                yield

    lists = {
        "c": compute(),
        "l1": line_events(
            steps, finish_output_near, part, (state, teacher_near, factor), grad_ffn,
            (output_low, grad_state), first_line, watch=True,
        ),
        "l2": line_events(
            steps, finish_ffn_back, part, (state, grad_state, gains.at[1:2]), grad_branch,
            (grad_state, gain_parts), second_line,
        ),
    }
    for place, (left, right) in enumerate(((grads_in, product), (normed, grad_gate))):
        lists[f"s{place}"] = scatter_events(
            left, right, owned[place], squares[place], scatter_refs[place]
        )
    weave([lists[name] for name in order + tuple(sorted(lists))])


def middle(state, factor, gains, normed_two, teacher, weights, steps, which):
    rows, width = normed_two.shape
    units = weights[0].shape[1]
    low = functools.partial(jax.ShapeDtypeStruct, dtype=jnp.bfloat16)
    full = functools.partial(jax.ShapeDtypeStruct, dtype=jnp.float32)
    in_vmem = pl.BlockSpec(memory_space=pltpu.VMEM)
    anywhere = pl.BlockSpec(memory_space=pl.ANY)
    held = [
        low((rows // 2, width)),
        low((rows, units)),
        full((rows // 2, width)),
        full((steps, width)),
    ]
    owned = [full((width // 8, units))] * 2 + [full((1, 128))] * 2
    blocks = units // MIDDLE_BLOCK
    inner = (2, rows // 2, MIDDLE_BLOCK)
    far = [low((rows, width)), low((rows, width)), full((2 * blocks,) + inner)]
    scratch = [
        pltpu.VMEM((rows, width), jnp.bfloat16),
        pltpu.VMEM((rows, units), jnp.bfloat16),
        pltpu.VMEM((rows, width), jnp.bfloat16),
        pltpu.VMEM((rows, units), jnp.bfloat16),
        pltpu.VMEM((rows, width), jnp.bfloat16),
        pltpu.VMEM((rows // 2, width), jnp.float32),
        pltpu.VMEM((rows // 2, width), jnp.bfloat16),
    ]
    scratch += [pltpu.VMEM((2, width, MIDDLE_BLOCK), jnp.bfloat16)] * 3
    scratch += [pltpu.VMEM((2,) + inner, jnp.float32)] * 2
    scratch += line_scratch(steps, rows, width) * 2
    scratch += scatter_scratch(width // 8, units) * 2
    scratch += [
        pltpu.SemaphoreType.DMA((3, 2)),
        pltpu.SemaphoreType.DMA((2,)),
        pltpu.SemaphoreType.DMA((2,)),
        pltpu.SemaphoreType.DMA((9,)),
    ]
    return pl.pallas_call(
        functools.partial(middle_body, steps, MIDDLE_ORDER),
        out_shape=held + owned + far,
        in_specs=[in_vmem] * 3 + [anywhere] * 5,
        out_specs=[in_vmem] * 8 + [anywhere] * 3,
        scratch_shapes=scratch,
        compiler_params=pltpu.CompilerParams(
            collective_id=which, has_side_effects=True, vmem_limit_bytes=63 << 20
        ),
        cost_estimate=busy(150),
    )(state, factor, gains, normed_two, teacher, *weights)


def turn(head_rows, cosine, sine_table):
    middle = head_rows.shape[0] // 2
    upper, lower = head_rows[:middle], head_rows[middle:]
    return jnp.concatenate(
        [upper * cosine - lower * sine_table, lower * cosine + upper * sine_table], axis=0
    )


def normalize_rows(tokens, gain, normed):
    @pl.loop(0, tokens.shape[0] // 64)
    def _(block):
        span = pl.ds(pl.multiple_of(block * 64, 64), 64)
        normed[span, :] = normalize(tokens[span, :].astype(jnp.float32), gain[...]).astype(
            jnp.bfloat16
        )


def project_rows(normed, weights, cosine, sine_table, query_t, pairs):
    q_cols = query_t.shape[0]
    k_cols = pairs.shape[1] // 2
    lin_t = jnp.dot(
        normed[...], weights[:, : q_cols + k_cols], preferred_element_type=jnp.float32
    ).T
    for first in range(0, q_cols, HD):
        query_t[first : first + HD, :] = turn(
            lin_t[first : first + HD], cosine[...], sine_table[...]
        ).astype(jnp.bfloat16)
    keys = [
        turn(lin_t[first : first + HD], cosine[...], sine_table[...])
        for first in range(q_cols, q_cols + k_cols, HD)
    ]
    pairs[:, :k_cols] = jnp.concatenate(keys, axis=0).T.astype(jnp.bfloat16)
    pairs[:, k_cols:] = jnp.dot(
        normed[...],
        weights[:, q_cols + k_cols : q_cols + 2 * k_cols],
        preferred_element_type=jnp.float32,
    ).astype(jnp.bfloat16)


def project_body(tokens, gain, weights, cosine, sine_table, normed, query_t, pairs):
    normalize_rows(tokens, gain, normed)
    project_rows(normed, weights, cosine, sine_table, query_t, pairs)


def split_pairs(pairs, keys, keys_t, values, values_t):
    heads = pairs.shape[1] // (2 * HD)
    for head in range(heads):
        part = pairs[:, head * HD : (head + 1) * HD]
        if keys is not None:
            keys[head] = part
        if keys_t is not None:
            keys_t[head] = part.astype(jnp.float32).T.astype(jnp.bfloat16)
        part = pairs[:, (heads + head) * HD : (heads + head + 1) * HD]
        if values is not None:
            values[head] = part
        if values_t is not None:
            values_t[head] = part.astype(jnp.float32).T.astype(jnp.bfloat16)


SCORE_FACTOR = float(HD) ** (-0.5) * LOG2E
KEY_BLOCK = 256


def lifted_scores(key_block, query_head, query_pos, key_pos):
    scores = jnp.dot(key_block, query_head, preferred_element_type=jnp.float32)
    return jnp.where(key_pos <= query_pos, scores * SCORE_FACTOR, NEG_FILL)


def attend_heads(
    heads, group, query_t, query_pos, key_pos, keys, values_t, lifted, mixed_t, low_t, stats
):
    rows = query_t.shape[1]
    blocks = keys.shape[1] // KEY_BLOCK

    @pl.loop(*heads)
    def _(head):
        span = pl.ds(pl.multiple_of(head * HD, HD), HD)
        shared = head // group
        query_head = query_t[span, :]

        def scan_scores(block, highest):
            keys_now = pl.ds(pl.multiple_of(block * KEY_BLOCK, KEY_BLOCK), KEY_BLOCK)
            scores = lifted_scores(
                keys[shared, keys_now, :], query_head, query_pos[...], key_pos[keys_now, :]
            )
            lifted[keys_now, :] = scores
            return jnp.maximum(highest, jnp.max(scores, axis=0, keepdims=True))

        highest = lax.fori_loop(
            0, blocks, scan_scores, jnp.full((1, rows), NEG_FILL, jnp.float32)
        )
        ceiling = jnp.floor(highest)

        def scan_values(block, state):
            weight_sum, mixed = state
            keys_now = pl.ds(pl.multiple_of(block * KEY_BLOCK, KEY_BLOCK), KEY_BLOCK)
            expo = jnp.exp2(lifted[keys_now, :] - ceiling)
            mixed = mixed + jnp.dot(
                values_t[shared, :, keys_now],
                expo.astype(jnp.bfloat16),
                preferred_element_type=jnp.float32,
            )
            return weight_sum + jnp.sum(expo, axis=0, keepdims=True), mixed

        weight_sum, mixed = lax.fori_loop(
            0,
            blocks,
            scan_values,
            (jnp.zeros((1, rows), jnp.float32), jnp.zeros((HD, rows), jnp.float32)),
        )
        mixed = mixed / weight_sum
        mixed_t[span, :] = mixed
        low_t[span, :] = mixed.astype(jnp.bfloat16).astype(jnp.float32)
        stats[head] = jnp.concatenate([ceiling, weight_sum], axis=0)


def branch_rows(low_t, w_out, mixed_low, part):
    mixed_low[...] = low_t[...].T.astype(jnp.bfloat16)

    @pl.loop(0, part.shape[1] // 512)
    def _(block):
        span = pl.ds(pl.multiple_of(block * 512, 512), 512)
        part[:, span] = times_transpose(mixed_low[...], w_out[span, :]).astype(jnp.bfloat16)


def attend_body(
    group, query_t, pairs, query_pos, key_pos, w_out, mixed_t, mixed_low, stats, part,
    keys, values_t, lifted, low_t,
):
    split_pairs(pairs, keys, None, None, values_t)
    attend_heads(
        (0, query_t.shape[0] // HD), group, query_t, query_pos, key_pos, keys, values_t,
        lifted, mixed_t, low_t, stats,
    )
    branch_rows(low_t, w_out, mixed_low, part)


FRONT_ORDER = (
    "gs", "gq", "gk", "gv", "gs", "gs", "gs", "gs", "c", "gq",
    "gk", "gv", "go", "gq", "gk", "gv", "gz", "gq", "gk", "gv",
    "gq", "gk", "gv", "c", "go", "c", "ga", "go", "c", "go",
    "c", "c", "gu", "go", "c", "line", "line", "line", "line", "gz",
    "gz", "line", "gd", "line", "ga", "gu", "ga", "gu", "line", "line",
    "line", "gz", "line", "gd", "gz", "gd", "ga", "gu", "gd",
)


def front_body(steps, group, order, *refs):
    refs = list(refs)

    def take(count):
        taken = refs[:count]
        del refs[:count]
        return taken

    tokens, cosine, sine_table, query_pos, key_pos = take(5)
    shards = take(9)
    normed, query_t, pairs_out, mixed_t, mixed_low, stats, gains, state = take(8)
    normed_two, pack_out, out_whole, gate, up, down, counts = take(7)
    pack, w_out, gain_tiles, pairs, keys, values_t, lifted, low_t, part = take(9)
    line_refs = take(4)
    gather_sems = take(9)
    (own_sems,) = take(1)
    ring, core, first, second, far = square_peers()
    rows, width = tokens.shape
    q_cols, k_cols = query_t.shape[0], pairs.shape[1] // 2
    heads = q_cols // HD
    shard_rows = width // 8
    meet(True, True)

    def pair_rows(which):
        return pl.ds(pl.multiple_of(which * rows, rows), rows)

    def swap_pairs(which):
        return pltpu.make_async_remote_copy(
            src_ref=pairs.at[pair_rows(which)],
            dst_ref=pairs.at[pair_rows(which)],
            send_sem=own_sems.at[0],
            recv_sem=own_sems.at[1],
            device_id={"context": 1 - core},
            device_id_type=MESH_ID,
        )

    keep_pack = pltpu.make_async_copy(pack, pack_out, own_sems.at[2])
    keep_out = pltpu.make_async_copy(w_out, out_whole, own_sems.at[3])

    def compute():
        for row in range(2):
            gains[row : row + 1, :] = jnp.concatenate(
                [
                    gain_tiles[32 * owner + 16 * row : 32 * owner + 16 * row + 16, :].astype(
                        jnp.float32
                    )[:1]
                    for owner in range(8)
                ],
                axis=1,
            )
        normalize_rows(tokens, gains.at[0:1], normed)
        yield
        project_rows(normed, pack, cosine, sine_table, query_t, pairs.at[pair_rows(core)])
        swap_pairs(core).start()
        keep_pack.start()
        yield
        swap_pairs(1 - core).wait_recv()
        split_pairs(pairs, keys, None, None, values_t)
        pairs_out[...] = pairs[...]
        for chunk in range(4):
            attend_heads(
                (chunk * heads // 4, (chunk + 1) * heads // 4), group, query_t, query_pos,
                key_pos, keys, values_t, lifted, mixed_t, low_t, stats,
            )
            yield
        keep_out.start()
        branch_rows(low_t, w_out, mixed_low, part)
        yield
        swap_pairs(core).wait_send()
        keep_pack.wait()
        keep_out.wait()
        yield

    targets = [
        pack.at[:, pl.ds(0, q_cols)],
        pack.at[:, pl.ds(q_cols, k_cols)],
        pack.at[:, pl.ds(q_cols + k_cols, k_cols)],
        w_out,
        gain_tiles,
        gate,
        up,
        down,
        counts,
    ]
    lists = {
        name: gather_events(source, target, sems)
        for name, source, target, sems in zip(
            ("gq", "gk", "gv", "go", "gs", "ga", "gu", "gd", "gz"), shards, targets, gather_sems
        )
    }
    lists["c"] = compute()
    lists["line"] = line_events(
        steps, finish_branch, part, (tokens, gains.at[1:2]), normed_two, (state,), line_refs
    )
    weave([lists[name] for name in order + tuple(sorted(lists))])


def front(tokens, tables, shards, group, steps, which):
    rows, width = tokens.shape
    cosine, sine_table, query_pos, key_pos = tables
    slot_len = key_pos.shape[0]
    q_cols, k_cols = shards[0].shape[1], shards[1].shape[1]
    heads, kv_heads = q_cols // HD, k_cols // HD
    low = functools.partial(jax.ShapeDtypeStruct, dtype=jnp.bfloat16)
    full = functools.partial(jax.ShapeDtypeStruct, dtype=jnp.float32)
    in_vmem = pl.BlockSpec(memory_space=pltpu.VMEM)
    anywhere = pl.BlockSpec(memory_space=pl.ANY)
    pack_cols = q_cols + 2 * k_cols
    held = [
        low((rows, width)),
        low((q_cols, rows)),
        low((slot_len, 2 * k_cols)),
        full((q_cols, rows)),
        low((rows, q_cols)),
        full((heads, 2, rows)),
        full((2, width)),
        full((rows // 2, width)),
    ]
    far = [low((rows, width)), low((width, pack_cols)), low((width, q_cols))]
    far += [low((8 * item.shape[0], item.shape[1])) for item in shards[5:]]
    return pl.pallas_call(
        functools.partial(front_body, steps, group, FRONT_ORDER),
        out_shape=held + far,
        in_specs=[in_vmem] * 5 + [anywhere] * 9,
        out_specs=[in_vmem] * len(held) + [anywhere] * len(far),
        scratch_shapes=[
            pltpu.VMEM((width, pack_cols), jnp.bfloat16),
            pltpu.VMEM((width, q_cols), jnp.bfloat16),
            pltpu.VMEM((8 * shards[4].shape[0], shards[4].shape[1]), jnp.bfloat16),
            pltpu.VMEM((slot_len, 2 * k_cols), jnp.bfloat16),
            pltpu.VMEM((kv_heads, slot_len, HD), jnp.bfloat16),
            pltpu.VMEM((kv_heads, HD, slot_len), jnp.bfloat16),
            pltpu.VMEM((slot_len, rows), jnp.float32),
            pltpu.VMEM((q_cols, rows), jnp.float32),
            pltpu.VMEM((rows, width), jnp.bfloat16),
        ]
        + line_scratch(steps, rows, width)
        + [pltpu.SemaphoreType.DMA((16,))] * 9
        + [pltpu.SemaphoreType.DMA((4,))],
        compiler_params=pltpu.CompilerParams(
            collective_id=which, has_side_effects=True, vmem_limit_bytes=60 << 20
        ),
        cost_estimate=busy(130),
    )(tokens, cosine, sine_table, query_pos, key_pos, *shards)


def prepare_back(grad_branch, w_out, query_t, queries, grad_t):
    queries_f = query_t[...].astype(jnp.float32).T
    for head in range(queries.shape[0]):
        queries[head] = queries_f[:, head * HD : (head + 1) * HD].astype(jnp.bfloat16)
    grad_t[...] = (
        jnp.dot(grad_branch[...], w_out[...], preferred_element_type=jnp.float32)
        .astype(jnp.bfloat16)
        .astype(jnp.float32)
        .T
    )


def attend_back_heads(
    heads, group, query_t, mixed_t, stats, query_pos, key_pos, cosine, sine_table, grad_pairs,
    keys, keys_t, values, queries, grad_t, turned,
):
    rows = query_t.shape[1]
    blocks = keys.shape[1] // KEY_BLOCK
    score_scale = float(HD) ** (-0.5)

    @pl.loop(*heads)
    def _(head):
        span = pl.ds(pl.multiple_of(head * HD, HD), HD)
        shared = head // group
        query_head = query_t[span, :]
        query_rows = queries[head]
        ceiling = stats[head, 0:1, :]
        inverse = 1.0 / stats[head, 1:2, :]
        grad_head = grad_t[span, :]
        delta = jnp.sum(grad_head * mixed_t[span, :], axis=0, keepdims=True)
        scaled = grad_head * inverse
        scaled_high = scaled.astype(jnp.bfloat16)
        scaled_low = (scaled - scaled_high.astype(jnp.float32)).astype(jnp.bfloat16)
        scaled_both = jnp.concatenate([scaled_high, scaled_low], axis=0)
        grad_head_low = grad_head.astype(jnp.bfloat16)

        def scan_keys(block, grad_query_t):
            keys_now = pl.ds(pl.multiple_of(block * KEY_BLOCK, KEY_BLOCK), KEY_BLOCK)
            scores = lifted_scores(
                keys[shared, keys_now, :], query_head, query_pos[...], key_pos[keys_now, :]
            )
            expo = jnp.exp2(scores - ceiling)
            value_term = times_transpose(expo.astype(jnp.bfloat16), scaled_both)
            grad_probs = jnp.dot(
                values[shared, keys_now, :], grad_head_low, preferred_element_type=jnp.float32
            )
            grad_scores = (expo * inverse * (grad_probs - delta)).astype(jnp.bfloat16)
            key_term = jnp.dot(grad_scores, query_rows, preferred_element_type=jnp.float32)
            grad_pairs[shared, keys_now, :] += jnp.concatenate(
                [key_term * score_scale, value_term[:, :HD] + value_term[:, HD:]], axis=1
            )
            return grad_query_t + jnp.dot(
                keys_t[shared, :, keys_now], grad_scores, preferred_element_type=jnp.float32
            )

        grad_query_t = lax.fori_loop(
            0, blocks, scan_keys, jnp.zeros((HD, rows), jnp.float32)
        )
        turned[span, :] = turn(grad_query_t * score_scale, cosine[...], -sine_table[...])


def attend_back_body(
    group, grad_branch, w_out, query_t, pairs, mixed_t, stats, query_pos, key_pos, cosine,
    sine_table, grad_query, grad_pairs, keys, keys_t, values, queries, grad_t, turned,
):
    split_pairs(pairs, keys, keys_t, values, None)
    prepare_back(grad_branch, w_out, query_t, queries, grad_t)
    grad_pairs[...] = jnp.zeros_like(grad_pairs)
    attend_back_heads(
        (0, queries.shape[0]), group, query_t, mixed_t, stats, query_pos, key_pos, cosine,
        sine_table, grad_pairs, keys, keys_t, values, queries, grad_t, turned,
    )
    grad_query[...] = turned[...].T.astype(jnp.bfloat16)


def join_rows(grad_query, pair_grads, cosine, sine_table, weights, grad_lin, part):
    q_cols = grad_query.shape[1]
    k_cols = HD * len(pair_grads)
    grad_lin[:, :q_cols] = grad_query
    keys = [turn(item.T[:HD], cosine[...], -sine_table[...]) for item in pair_grads]
    grad_lin[:, q_cols : q_cols + k_cols] = jnp.concatenate(keys, axis=0).T.astype(jnp.bfloat16)
    grad_lin[:, q_cols + k_cols :] = jnp.concatenate(
        [item[:, HD:] for item in pair_grads], axis=1
    ).astype(jnp.bfloat16)

    @pl.loop(0, part.shape[1] // 512)
    def _(block):
        span = pl.ds(pl.multiple_of(block * 512, 512), 512)
        part[:, span] = times_transpose(
            grad_lin[...], weights[span, : q_cols + 2 * k_cols]
        ).astype(jnp.bfloat16)


def join_body(grad_query, grad_pairs, cosine, sine_table, weights, grad_lin, part):
    pair_grads = [grad_pairs[head] for head in range(grad_pairs.shape[0])]
    join_rows(grad_query[...], pair_grads, cosine, sine_table, weights, grad_lin, part)


BACK_ORDER = (
    "y", "s0", "s0", "s0", "s0", "s0", "s0", "c", "s1", "s1",
    "s1", "s1", "s1", "s1", "c", "c", "c", "s0", "s0", "y",
    "c", "s1", "s1", "c", "line", "s2", "s2", "s2", "s2", "line",
    "s2", "s2", "line", "line", "s2", "s2", "line", "line", "line", "line",
    "y", "line",
)


def back_body(steps, group, order, *refs):
    refs = list(refs)

    def take(count):
        taken = refs[:count]
        del refs[:count]
        return taken

    cosine, sine_table, query_pos, key_pos = take(4)
    grad_branch, w_out, query_t, pairs, mixed_t, stats, gains = take(7)
    normed_two, grad_up, mixed_low = take(3)
    pooled = take(3)
    later = take(4)
    (half_low,) = take(1)
    owned = take(3)
    (totals,) = take(1)
    out, block_out = take(2)
    keys, keys_t, values, queries, grad_t, turned, grad_pairs, pairs_in, grad_lin, part = take(10)
    gain_parts = take(1)
    loaded = take(4)
    squares = take(3)
    line_refs = take(4)
    total_refs = take(3)
    scatter_refs = [take(5) for _ in range(3)]
    (own_sems,) = take(1)
    weights, tokens, grad_state, normed = loaded
    ring, core, first, second, far = square_peers()
    rows = query_t.shape[1]
    heads = queries.shape[0]
    meet(True, True, True)
    loads = [
        pltpu.make_async_copy(source, target, own_sems.at[2 + place])
        for place, (source, target) in enumerate(zip(later, loaded))
    ]
    for load in loads:
        load.start()

    def own_rows(which):
        return pl.ds(pl.multiple_of(which * rows, rows), rows)

    swap = pltpu.make_async_remote_copy(
        src_ref=grad_pairs.at[:, own_rows(1 - core)],
        dst_ref=pairs_in,
        send_sem=own_sems.at[0],
        recv_sem=own_sems.at[1],
        device_id={"context": 1 - core},
        device_id_type=MESH_ID,
    )

    def compute():
        split_pairs(pairs, keys, keys_t, values, None)
        prepare_back(grad_branch, w_out, query_t, queries, grad_t)
        grad_pairs[...] = jnp.zeros_like(grad_pairs)
        yield
        for chunk in range(4):
            attend_back_heads(
                (chunk * heads // 4, (chunk + 1) * heads // 4), group, query_t, mixed_t, stats,
                query_pos, key_pos, cosine, sine_table, grad_pairs, keys, keys_t, values,
                queries, grad_t, turned,
            )
            yield
        swap.start()
        for load in loads:
            load.wait()
        grad_query = turned[...].T.astype(jnp.bfloat16)
        swap.wait_recv()
        pair_grads = [
            grad_pairs[head, own_rows(core), :] + pairs_in[head] for head in range(keys.shape[0])
        ]
        join_rows(grad_query, pair_grads, cosine, sine_table, weights, grad_lin, part)
        yield
        swap.wait_send()
        yield

    at_end, side, inner, outer = line_place()
    in_middle = jnp.logical_not(at_end)

    def spread():
        half = half_low.shape[0]
        near = block_out.at[pl.ds(pl.multiple_of(side * half, half), half)]
        far = block_out.at[pl.ds(pl.multiple_of((1 - side) * half, half), half)]

        def hand(source, target, send, recv, device):
            return pltpu.make_async_remote_copy(
                src_ref=source,
                dst_ref=target,
                send_sem=own_sems.at[send],
                recv_sem=own_sems.at[recv],
                device_id=device,
                device_id_type=MESH_ID,
            )

        to_outer = hand(half_low, near, 6, 7, outer)
        to_inner = hand(half_low, near, 8, 9, inner)
        onward = hand(far, far, 10, 9, outer)
        keep = pltpu.make_async_copy(half_low, near, own_sems.at[11])

        @pl.when(in_middle)
        def _():
            to_outer.start()
            to_inner.start()
            keep.start()

        yield

        @pl.when(in_middle)
        def _():
            to_inner.wait_recv()
            onward.start()

        yield

        @pl.when(in_middle)
        def _():
            to_outer.wait_send()
            to_inner.wait_send()
            onward.wait_send()
            keep.wait()

        @pl.when(at_end)
        def _():
            to_outer.wait_recv()
            onward.wait_recv()

        yield

    pairs_of = ((normed_two, grad_up), (grad_branch, mixed_low), (normed, grad_lin))
    lists = {
        f"s{place}": scatter_events(left, right, owned[place], squares[place], scatter_refs[place])
        for place, (left, right) in enumerate(pairs_of)
    }
    lists["c"] = compute()
    lists["y"] = spread()
    lists["line"] = line_events(
        steps, finish_attn_back, part, (tokens, grad_state, gains.at[0:1]), out, gain_parts,
        line_refs,
    )
    weave([lists[name] for name in order + tuple(sorted(lists))])
    own_row = total_refs[0].at[0]
    width = gains.shape[1]
    own_row[:, :width] = jnp.sum(gain_parts[0][...], axis=0, keepdims=True)
    own_row[:, width : 2 * width] = jnp.sum(pooled[0][...], axis=0, keepdims=True)
    own_row[:, 2 * width :] = sum(item[...] for item in (*pooled[1:], *squares))
    total_everywhere(totals, *total_refs)


def back(tables, held, factors, pooled, later, half_low, group, steps, which):
    query_t, pairs = held[2], held[3]
    q_cols, rows = query_t.shape
    slot_len, k_cols = pairs.shape[0], pairs.shape[1] // 2
    kv_heads, heads = k_cols // HD, q_cols // HD
    width = held[0].shape[1]
    pack_cols = q_cols + 2 * k_cols
    full = functools.partial(jax.ShapeDtypeStruct, dtype=jnp.float32)
    in_vmem = pl.BlockSpec(memory_space=pltpu.VMEM)
    anywhere = pl.BlockSpec(memory_space=pl.ANY)
    shard_rows = width // 8
    owned = [full((shard_rows, cols)) for cols in (factors[1].shape[1], q_cols, pack_cols)]
    pool_width = 2 * width + 128
    near = (*tables, *held, *factors, *pooled)
    scratch = [
        pltpu.VMEM((kv_heads, slot_len, HD), jnp.bfloat16),
        pltpu.VMEM((kv_heads, HD, slot_len), jnp.bfloat16),
        pltpu.VMEM((kv_heads, slot_len, HD), jnp.bfloat16),
        pltpu.VMEM((heads, rows, HD), jnp.bfloat16),
        pltpu.VMEM((q_cols, rows), jnp.float32),
        pltpu.VMEM((q_cols, rows), jnp.float32),
        pltpu.VMEM((kv_heads, slot_len, 2 * HD), jnp.float32),
        pltpu.VMEM((kv_heads, rows, 2 * HD), jnp.float32),
        pltpu.VMEM((rows, pack_cols), jnp.bfloat16),
        pltpu.VMEM((rows, width), jnp.bfloat16),
        pltpu.VMEM((steps, width), jnp.float32),
    ]
    scratch += [pltpu.VMEM(item.shape, item.dtype) for item in later]
    scratch += [pltpu.VMEM((1, 128), jnp.float32)] * 3
    scratch += line_scratch(steps, rows, width) + total_scratch(pool_width)
    for item in owned:
        scratch += scatter_scratch(*item.shape)
    return pl.pallas_call(
        functools.partial(back_body, steps, group, BACK_ORDER),
        out_shape=owned
        + [full((1, pool_width))]
        + [jax.ShapeDtypeStruct((rows, width), jnp.bfloat16)] * 2,
        in_specs=[in_vmem] * len(near) + [anywhere] * (len(later) + 1),
        out_specs=[in_vmem] * 4 + [anywhere] * 2,
        scratch_shapes=scratch + [pltpu.SemaphoreType.DMA((12,))],
        compiler_params=pltpu.CompilerParams(
            collective_id=which, has_side_effects=True, vmem_limit_bytes=62 << 20
        ),
        cost_estimate=busy(110),
    )(*near, *later, half_low)


def on_device(
    tokens,
    teacher,
    lengths,
    loss_mask,
    stretch_order,
    attn_gain,
    w_query,
    w_key,
    w_value,
    w_out,
    mlp_gain,
    w_gate,
    w_up,
    w_down,
    first_moment,
    second_moment,
    gain_first,
    gain_second,
):
    slot_count, stretch_len, model_width = tokens.shape
    token_rows = slot_count * stretch_len
    half_len = stretch_len // 2
    slot_len = stretch_len * lax.axis_size("context")
    all_rows = slot_count * lax.axis_size("dp") * slot_len
    steps = 4
    share_rows = token_rows // 2
    local_index = stretch_len * lax.axis_index("context") + jnp.arange(stretch_len, dtype=jnp.int32)
    query_pos = positions_of(stretch_order, local_index, half_len)
    valid = ((loss_mask == 1) & (query_pos < lengths[:, None])).astype(jnp.float32)
    valid_here = jnp.sum(valid)
    shard_rows = attn_gain.shape[0]
    q_cols, k_cols = w_query.shape[1], w_key.shape[1]
    square = lax.axis_size("dp") == 4 and lax.axis_size("context") == 2
    head_count = q_cols // HD
    kv_count = k_cols // HD
    group_size = head_count // kv_count
    angles = frequencies()[:, None] * query_pos.reshape(1, token_rows).astype(jnp.float32)
    cosine, sine_table = jnp.cos(angles), jnp.sin(angles)
    token_rows_low = tokens.reshape(token_rows, model_width)
    low = functools.partial(jax.ShapeDtypeStruct, dtype=jnp.bfloat16)
    full = functools.partial(jax.ShapeDtypeStruct, dtype=jnp.float32)
    shard_f32 = full((share_rows, model_width))
    shard_low = low((share_rows, model_width))
    gain_parts = full((steps, model_width))
    line = functools.partial(line_sum, steps=steps)
    key_pos = positions_of(stretch_order, jnp.arange(slot_len, dtype=jnp.int32), half_len)
    key_pos = jnp.where(key_pos < lengths[:, None], key_pos, slot_len).reshape(slot_len, 1)
    query_row = query_pos.reshape(1, token_rows)
    if square:
        both_gains = jnp.stack([attn_gain, mlp_gain])
        gain_tiles = jnp.broadcast_to(both_gains[:, None, :], (2, 16, shard_rows))
        count_high = jnp.floor(valid_here / 64.0)
        count_low = valid_here - 64.0 * count_high
        count_tile = jnp.broadcast_to(
            jnp.where(jnp.arange(256)[None, :] < 128, count_high, count_low), (16, 256)
        ).astype(jnp.bfloat16)
        (
            normed, query_t, pairs, mixed_t, mixed_low, stats, gains, state, normed_two,
            first_pack, full_out, full_gate, full_up, full_down, count_whole,
        ) = front(
            token_rows_low,
            (cosine, sine_table, query_row, key_pos),
            (
                w_query, w_key, w_value, w_out, gain_tiles.reshape(32, shard_rows),
                w_gate, w_up, w_down, count_tile,
            ),
            group_size,
            steps,
            0,
        )
        gain_one, gain_two = gains[:1], gains[1:]
        counts = count_whole.reshape(8, 16, 256)[:, 0].astype(jnp.float32)
        valid_count = jnp.sum(64.0 * counts[:, 0] + counts[:, 128])
    else:
        whole = functools.partial(
            lax.all_gather, axis_name=("dp", "context"), axis=0, tiled=True
        )
        first_pack = whole(jnp.concatenate([w_query, w_key, w_value], axis=1))
        full_out, full_gate, full_up, full_down = (
            whole(item) for item in (w_out, w_gate, w_up, w_down)
        )
        gain_one, gain_two = (
            whole(item)[None, :].astype(jnp.float32) for item in (attn_gain, mlp_gain)
        )
        valid_count = lax.psum(valid_here, ("dp", "context"))
        normed, query_t, pairs_here = local_call(
            project_body,
            8,
            [
                low((token_rows, model_width)),
                low((q_cols, token_rows)),
                low((token_rows, 2 * k_cols)),
            ],
            [token_rows_low, gain_one, first_pack, cosine, sine_table],
        )
        pairs = lax.all_gather(pairs_here, "context", axis=0, tiled=True)
        mixed_t, mixed_low, stats, branch_part = local_call(
            functools.partial(attend_body, group_size),
            20,
            [
                full((q_cols, token_rows)),
                low((token_rows, q_cols)),
                full((head_count, 2, token_rows)),
                low((token_rows, model_width)),
            ],
            [query_t, pairs, query_row, key_pos, full_out],
            [
                pltpu.VMEM((kv_count, slot_len, HD), jnp.bfloat16),
                pltpu.VMEM((kv_count, HD, slot_len), jnp.bfloat16),
                pltpu.VMEM((slot_len, token_rows), jnp.float32),
                pltpu.VMEM((q_cols, token_rows), jnp.float32),
            ],
        )
        normed_two, state = line(
            finish_branch, branch_part, (token_rows_low, gain_two), [shard_f32], 0
        )
    factor = jnp.float32(all_rows) / valid_count * valid.reshape(token_rows, 1)
    teacher_rows = teacher.reshape(token_rows, model_width)
    if square:
        (
            output_low, grad_up, grad_state, gain_two_parts, owned_down, owned_gate,
            squares_down, squares_gate, _, grad_branch, _,
        ) = middle(
            state, factor, gains, normed_two, teacher_rows, (full_gate, full_up, full_down),
            steps, 1,
        )
        owned_up, owned_out, owned_qkv, totals, grad_tokens, block_out = back(
            (cosine, sine_table, query_row, key_pos),
            (grad_branch, full_out, query_t, pairs, mixed_t, stats, gains),
            (normed_two, grad_up, mixed_low),
            (gain_two_parts, squares_down, squares_gate),
            (first_pack, token_rows_low, grad_state, normed),
            output_low,
            group_size,
            steps,
            3,
        )
    else:
        gate, up, product, output_part = by_units(
            ffn_body,
            normed_two,
            [full_gate, full_up, full_down],
            [],
            [jnp.float32, jnp.float32, jnp.bfloat16],
            18,
        )
        grad_ffn, output_low, grad_output = line(
            finish_output, output_part, (state, teacher_rows, factor), [shard_low, shard_f32], 1
        )
        outward = [(1, 0), (2, 3)]
        own_half = lax.ppermute(output_low, "tensor", outward)
        crossed_half = lax.ppermute(output_low, "tensor", [(1, 2), (2, 1)])
        other_half = lax.ppermute(crossed_half, "tensor", outward)
        block_out = join_halves(output_low, own_half, crossed_half, other_half)
        grad_gate, grad_up, normed_part = by_units(
            ffn_back_body,
            grad_ffn,
            [full_gate, full_up, full_down],
            [gate, up],
            [jnp.bfloat16, jnp.bfloat16],
            18,
        )

        def owned(left, right):
            return lax.psum_scatter(
                column_term(left, right).astype(jnp.bfloat16),
                ("dp", "context"),
                scatter_dimension=0,
                tiled=True,
            ).astype(jnp.float32)

        owned_down = owned(grad_ffn, product)
        owned_gate = owned(normed_two, grad_gate)
        owned_up = owned(normed_two, grad_up)
        grad_branch, grad_state, gain_two_parts = line(
            finish_ffn_back, normed_part, (state, grad_output, gain_two), [shard_f32, gain_parts], 2
        )
        owned_out = owned(grad_branch, mixed_low)
        grad_query, grad_pairs = local_call(
            functools.partial(attend_back_body, group_size),
            24,
            [low((token_rows, q_cols)), full((kv_count, slot_len, 2 * HD))],
            [
                grad_branch, full_out, query_t, pairs, mixed_t, stats, query_row, key_pos,
                cosine, sine_table,
            ],
            [
                pltpu.VMEM((kv_count, slot_len, HD), jnp.bfloat16),
                pltpu.VMEM((kv_count, HD, slot_len), jnp.bfloat16),
                pltpu.VMEM((kv_count, slot_len, HD), jnp.bfloat16),
                pltpu.VMEM((head_count, token_rows, HD), jnp.bfloat16),
                pltpu.VMEM((q_cols, token_rows), jnp.float32),
                pltpu.VMEM((q_cols, token_rows), jnp.float32),
            ],
        )
        grad_pairs_own = lax.psum_scatter(
            grad_pairs, "context", scatter_dimension=1, tiled=True
        )
        grad_lin, inputs_part = local_call(
            join_body,
            6,
            [low((token_rows, q_cols + 2 * k_cols)), low((token_rows, model_width))],
            [grad_query, grad_pairs_own, cosine, sine_table, first_pack],
        )
        owned_qkv = owned(normed, grad_lin)
        grad_tokens, gain_one_parts = line(
            finish_attn_back, inputs_part, (token_rows_low, grad_state, gain_one), [gain_parts], 3
        )
    owned_all = [owned_qkv, owned_out, owned_gate, owned_up, owned_down]
    gain_cols = 2 * model_width
    if not square:
        square_local = sum(jnp.sum(part * part) for part in owned_all)
        totals = lax.psum(
            jnp.concatenate(
                [
                    jnp.sum(gain_one_parts, axis=0),
                    jnp.sum(gain_two_parts, axis=0),
                    jnp.full((128,), square_local / 128.0),
                ]
            )[None, :],
            ("dp", "context", "tensor"),
        )
    gains_owned = lax.dynamic_slice_in_dim(
        totals[0, :gain_cols].reshape(2, model_width),
        lax.axis_index(("dp", "context")) * shard_rows,
        shard_rows,
        1,
    )
    widths = (q_cols, k_cols, k_cols) + tuple(item.shape[1] for item in owned_all[1:])
    *matrices, adam_step = update_rows(
        owned_all, first_moment, second_moment, totals, gain_cols, widths
    )
    gain_step = adam_direction(
        gains_owned, gain_first, gain_second, clip_of(totals, gain_cols)
    )
    return (
        block_out.reshape(slot_count, stretch_len, model_width),
        grad_tokens.reshape(slot_count, stretch_len, model_width),
        gains_owned[0],
        matrices[0],
        matrices[1],
        matrices[2],
        matrices[3],
        gains_owned[1],
        matrices[4],
        matrices[5],
        matrices[6],
        adam_step,
        gain_step,
    )


def solution(mesh):
    in_specs = (
        P("dp", "context", None),
        P("dp", "context", None),
        P("dp"),
        P("dp", "context"),
        P("dp", None),
        P(("dp", "context")),
        P(("dp", "context"), "tensor"),
        P(("dp", "context"), "tensor"),
        P(("dp", "context"), "tensor"),
        P(("dp", "context"), "tensor"),
        P(("dp", "context")),
        P(("dp", "context"), "tensor"),
        P(("dp", "context"), "tensor"),
        P(("dp", "context"), "tensor"),
        P(("dp", "context"), "tensor"),
        P(("dp", "context"), "tensor"),
        P(None, ("dp", "context")),
        P(None, ("dp", "context")),
    )
    out_specs = (
        P("dp", "context", None),
        P("dp", "context", None),
        P(("dp", "context")),
        P(("dp", "context"), "tensor"),
        P(("dp", "context"), "tensor"),
        P(("dp", "context"), "tensor"),
        P(("dp", "context"), "tensor"),
        P(("dp", "context")),
        P(("dp", "context"), "tensor"),
        P(("dp", "context"), "tensor"),
        P(("dp", "context"), "tensor"),
        P(("dp", "context"), "tensor"),
        P(None, ("dp", "context")),
    )
    return jax.shard_map(
        on_device, mesh=mesh, in_specs=in_specs, out_specs=out_specs, check_vma=False
    )
```

```python
import functools
import math

import jax
import jax.numpy as jnp
from jax import lax
from jax.experimental import pallas as pl
from jax.experimental.pallas import tpu as pltpu
from jax.sharding import PartitionSpec as P

HD = 64
STEP = 10


EPS_NORM = 1e-05
ROPE_BASE = 500000.0
OLD_CONTEXT = 8192.0
SCALE_FACTOR = 32.0
LOW_FACTOR = 1.0
HIGH_FACTOR = 4.0
LOG2E = 1.4426950408889634
NEG_FILL = -1e30
BETA_ONE = 0.9
BETA_TWO = 0.95
ADAM_EPS = 1e-08
CLIP_NORM = 1.0


def frequencies():
    channel = jnp.arange(HD // 2, dtype=jnp.float32)
    base_freq = jnp.power(jnp.float32(ROPE_BASE), -2.0 * channel / HD)
    wavelength = 2.0 * math.pi / base_freq
    smooth = (OLD_CONTEXT / wavelength - LOW_FACTOR) / (HIGH_FACTOR - LOW_FACTOR)
    blended = (1.0 - smooth) * base_freq / SCALE_FACTOR + smooth * base_freq
    slow_freq = jnp.where(wavelength > OLD_CONTEXT / LOW_FACTOR, base_freq / SCALE_FACTOR, blended)
    return jnp.where(wavelength < OLD_CONTEXT / HIGH_FACTOR, base_freq, slow_freq)


def normalize(values, gain):
    factor = lax.rsqrt(jnp.mean(values * values, axis=-1, keepdims=True) + EPS_NORM)
    return values * factor * gain.astype(jnp.float32)


def normalize_back(values, gain, upstream):
    factor = lax.rsqrt(jnp.mean(values * values, axis=-1, keepdims=True) + EPS_NORM)
    unit_rows = values * factor
    gain_grad = jnp.sum(upstream * unit_rows, axis=0)
    scaled_up = upstream * gain.astype(jnp.float32)
    input_grad = factor * (
        scaled_up - unit_rows * jnp.mean(scaled_up * unit_rows, axis=-1, keepdims=True)
    )
    return (input_grad, gain_grad)


def positions_of(order_table, row_index, half_len):
    stretch_slot = row_index // half_len
    matches = stretch_slot[:, None] == jnp.arange(order_table.shape[1], dtype=jnp.int32)[None, :]
    stretch_ids = jnp.sum(jnp.where(matches[None, :, :], order_table[:, None, :], 0), axis=-1)
    return stretch_ids * half_len + row_index % half_len


def times_transpose(left, right):
    return lax.dot_general(
        left, right, (((1,), (1,)), ((), ())), preferred_element_type=jnp.float32
    )


def column_term(left, right):
    return lax.dot_general(
        left, right, (((0,), (0,)), ((), ())), preferred_element_type=jnp.float32
    )


def adam_direction(gradient, first, second, clip_factor):
    clipped = gradient * clip_factor
    first_new = BETA_ONE * first + (1.0 - BETA_ONE) * clipped
    second_new = BETA_TWO * second + (1.0 - BETA_TWO) * clipped * clipped
    return (
        first_new
        / (1.0 - BETA_ONE**STEP)
        / (jnp.sqrt(second_new / (1.0 - BETA_TWO**STEP)) + ADAM_EPS)
    )


MESH_ID = pl.DeviceIdType.MESH


def row_mean(values):
    return jnp.mean(values, axis=-1, keepdims=True)


def line_place():
    place = lax.axis_index("tensor")
    side = place // 2
    inner = place + 1 - 2 * side
    outer = jnp.clip(place - 1 + 2 * side, 0, 3)
    return (place == 0) | (place == 3), side, {"tensor": inner}, {"tensor": outer}


def square_peers():
    ring, core = lax.axis_index("dp"), lax.axis_index("context")
    across = ring + 1 - 2 * (ring % 2)
    along = (ring + 2) % 4
    first = across * (1 - core) + along * core
    second = along * (1 - core) + across * core
    return ring, core, first, second, 3 - ring


def meet(with_line, with_square, with_all=False):
    barrier = pltpu.get_barrier_semaphore()
    expected = jnp.int32(0)
    if with_all:
        place = lax.axis_index("tensor")
        for hop in (1, 2, 3):
            pl.semaphore_signal(
                barrier,
                inc=1,
                device_id={"tensor": (place + hop) % 4},
                device_id_type=MESH_ID,
            )
        expected = expected + 3
    elif with_line:
        at_end, side, inner, outer = line_place()
        pl.semaphore_signal(barrier, inc=1, device_id=inner, device_id_type=MESH_ID)

        @pl.when(jnp.logical_not(at_end))
        def _():
            pl.semaphore_signal(barrier, inc=1, device_id=outer, device_id_type=MESH_ID)

        expected = expected + 2 - at_end.astype(jnp.int32)
    if with_square:
        ring, core, first, second, far = square_peers()
        for target in ({"dp": first}, {"dp": second}, {"context": 1 - core}):
            pl.semaphore_signal(barrier, inc=1, device_id=target, device_id_type=MESH_ID)
        expected = expected + 3
    pl.semaphore_wait(barrier, expected)


def line_scratch(steps, total_rows, width):
    rows = total_rows // 2 // steps
    return [
        pltpu.VMEM((2, steps, rows, width), jnp.bfloat16),
        pltpu.VMEM((steps, rows, width), jnp.bfloat16),
        pltpu.VMEM((steps, rows, width), jnp.bfloat16),
        pltpu.SemaphoreType.DMA((12, steps)),
    ]


def line_events(steps, finish, part, extra, out, kept, scratch, watch=False):
    outer_in, cross_in, done, sems = scratch
    at_end, side, inner, outer = line_place()
    in_middle = jnp.logical_not(at_end)
    half = part.shape[0] // 2
    rows = half // steps

    def near(step):
        return pl.ds(pl.multiple_of(side * half + step * rows, rows), rows)

    def far(step):
        return pl.ds(pl.multiple_of((1 - side) * half + step * rows, rows), rows)

    def remote(src, dst, send, recv, step, target):
        return pltpu.make_async_remote_copy(
            src_ref=src,
            dst_ref=dst,
            send_sem=sems.at[send, step],
            recv_sem=sems.at[recv, step],
            device_id=target,
            device_id_type=MESH_ID,
        )

    def inward(kind, step):
        span = near(step) if kind else far(step)
        return remote(part.at[span], outer_in.at[kind, step], kind, 2 + kind, step, inner)

    def across(step):
        return remote(outer_in.at[0, step], cross_in.at[step], 4, 5, step, inner)

    def hand_outer(step):
        return remote(done.at[step], out.at[near(step)], 6, 9, step, outer)

    def hand_inner(step):
        return remote(done.at[step], out.at[near(step)], 7, 10, step, inner)

    def hand_on(step):
        return remote(out.at[far(step)], out.at[far(step)], 8, 10, step, outer)

    def keep(step):
        return pltpu.make_async_copy(done.at[step], out.at[near(step)], sems.at[11, step])

    def feed(index):
        step, kind = divmod(index, 2)
        if index >= 2:
            inward(kind, step - 1).wait_send()
        inward(kind, step).start()

    def pass_on(step):
        hand_inner(step).wait_recv()
        hand_on(step).start()

    def arrive(step):
        @pl.when(in_middle)
        def _():
            keep(step).wait()

        @pl.when(at_end)
        def _():
            hand_outer(step).wait_recv()
            hand_on(step).wait_recv()

    @pl.when(at_end)
    def _():
        feed(0)
        feed(1)

    for item in kept:
        if item.shape[0] == steps:
            item[...] = jnp.zeros_like(item)
    yield
    for step in range(steps):

        @pl.when(at_end)
        def _():
            if step + 1 < steps:
                feed(2 * step + 2)

        @pl.when(in_middle)
        def _():
            inward(0, step).wait_recv()
            outer_in[0, step] = (
                outer_in[0, step].astype(jnp.float32) + part[far(step), :].astype(jnp.float32)
            ).astype(jnp.bfloat16)
            across(step).start()

        yield

        @pl.when(at_end)
        def _():
            if step + 1 < steps:
                feed(2 * step + 3)

        @pl.when(in_middle)
        def _():
            inward(1, step).wait_recv()
            across(step).wait_recv()
            total = (
                part[near(step), :].astype(jnp.float32)
                + outer_in[1, step].astype(jnp.float32)
                + cross_in[step].astype(jnp.float32)
            )
            finish(total, near(step), pl.ds(step * rows, rows), step, done, extra, kept)
            hand_outer(step).start()
            hand_inner(step).start()
            keep(step).start()
            if step > 0:
                pass_on(step - 1)

        yield
        if watch and step >= 2:
            arrive(step - 2)
            yield

    @pl.when(in_middle)
    def _():
        pass_on(steps - 1)

    @pl.when(at_end)
    def _():
        for kind in range(2):
            inward(kind, steps - 1).wait_send()

    if watch:
        yield
    for step in range(steps - 2 if watch else 0, steps):
        arrive(step)
        if watch:
            yield

    @pl.when(in_middle)
    def _():
        for step in range(steps):
            across(step).wait_send()
            hand_outer(step).wait_send()
            hand_inner(step).wait_send()
            hand_on(step).wait_send()

    yield


def gather_events(src, dst, sems):
    rows = src.shape[0]
    ring, core, first, second, far = square_peers()
    to_first, to_second, to_twin = {"dp": first}, {"dp": second}, {"context": 1 - core}

    def span(owner_ring, owner_core):
        return pl.ds(pl.multiple_of((owner_ring * 2 + owner_core) * rows, rows), rows)

    def copy(source, owner_ring, owner_core, slot, target):
        return pltpu.make_async_remote_copy(
            src_ref=source,
            dst_ref=dst.at[span(owner_ring, owner_core)],
            send_sem=sems.at[slot],
            recv_sem=sems.at[8 + owner_ring * 2 + owner_core],
            device_id=target,
            device_id_type=MESH_ID,
        )

    own = pltpu.make_async_copy(src, dst.at[span(ring, core)], sems.at[7])
    copy(src, ring, core, 0, to_first).start()
    copy(src, ring, core, 1, to_second).start()
    copy(src, ring, core, 2, to_twin).start()
    own.start()
    yield
    block = dst.at[span(first, core)]
    copy(block, first, core, 3, to_second).wait_recv()
    copy(block, first, core, 3, to_second).start()
    copy(block, first, core, 4, to_twin).start()
    yield
    block = dst.at[span(second, core)]
    copy(block, second, core, 5, to_twin).wait_recv()
    copy(block, second, core, 5, to_twin).start()
    yield
    block = dst.at[span(far, core)]
    copy(block, far, core, 6, to_twin).wait_recv()
    copy(block, far, core, 6, to_twin).start()
    yield
    for owner_ring in (ring, first, second, far):
        block = dst.at[span(owner_ring, 1 - core)]
        copy(block, owner_ring, 1 - core, 2, to_twin).wait_recv()
    for slot in range(7):
        copy(src, ring, core, slot, to_twin).wait_send()
    own.wait()
    yield


def lane_sums(item):
    sums = jnp.sum(item[...] * item[...], axis=0, keepdims=True)
    return sum(sums[:, first : first + 128] for first in range(0, sums.shape[1], 128))


def scatter_scratch(rows, cols):
    return [
        pltpu.VMEM((2, rows, cols), jnp.bfloat16),
        pltpu.VMEM((4, rows, cols), jnp.bfloat16),
        pltpu.VMEM((2, rows, cols), jnp.bfloat16),
        pltpu.VMEM((1, rows, cols), jnp.bfloat16),
        pltpu.SemaphoreType.DMA((14,)),
    ]


def scatter_events(left, right, out, square, scratch):
    twin_out, twin_in, first_in, second_in, sems = scratch
    rows = out.shape[0]
    ring, core, first, second, far = square_peers()
    to_first, to_second, to_twin = {"dp": first}, {"dp": second}, {"context": 1 - core}
    own_order = (far, first, second, ring)
    twin_order = (far, second, first, ring)

    def block(owner_ring, owner_core):
        span = pl.ds(pl.multiple_of((owner_ring * 2 + owner_core) * rows, rows), rows)
        return column_term(left[:, span], right[...])

    def remote(src, dst, slot, target):
        return pltpu.make_async_remote_copy(
            src_ref=src,
            dst_ref=dst,
            send_sem=sems.at[slot],
            recv_sem=sems.at[7 + slot],
            device_id=target,
            device_id_type=MESH_ID,
        )

    def swap(role):
        return remote(twin_out.at[role % 2], twin_in.at[role], role, to_twin)

    def over_first(role):
        return remote(twin_in.at[role], first_in.at[role], 4 + role, to_first)

    over_second = remote(twin_in.at[2], second_in.at[0], 6, to_second)

    def for_twin(role):
        if role >= 2:
            swap(role - 2).wait_send()
        twin_out[role % 2] = block(twin_order[role], 1 - core).astype(jnp.bfloat16)
        swap(role).start()

    for role in range(2):
        for_twin(role)
        yield
    for role in range(2):
        term = block(own_order[role], core)
        swap(role).wait_recv()
        twin_in[role] = (term + twin_in[role].astype(jnp.float32)).astype(jnp.bfloat16)
        over_first(role).start()
        yield
    for_twin(2)
    yield
    for_twin(3)
    yield
    term = block(second, core)
    swap(2).wait_recv()
    over_first(0).wait_recv()
    twin_in[2] = (
        term + twin_in[2].astype(jnp.float32) + first_in[0].astype(jnp.float32)
    ).astype(jnp.bfloat16)
    over_second.start()
    yield
    term = block(ring, core)
    swap(3).wait_recv()
    over_first(1).wait_recv()
    out[...] = term + twin_in[3].astype(jnp.float32) + first_in[1].astype(jnp.float32)
    yield
    over_second.wait_recv()
    out[...] += second_in[0].astype(jnp.float32)
    square[...] = lane_sums(out)
    swap(2).wait_send()
    swap(3).wait_send()
    over_first(0).wait_send()
    over_first(1).wait_send()
    over_second.wait_send()
    yield


def total_scratch(width):
    return [
        pltpu.VMEM((7, 1, width), jnp.float32),
        pltpu.VMEM((4, 1, width), jnp.float32),
        pltpu.SemaphoreType.DMA((13,)),
    ]


def total_everywhere(out, taken, line_in, sems):
    ring, core, first, second, far = square_peers()
    place = lax.axis_index("tensor")
    across = ring + 1 - 2 * (ring % 2)
    along = (ring + 2) % 4
    others = [{"tensor": (place + hop) % 4} for hop in (1, 2, 3)]
    for stage, target in enumerate(({"context": 1 - core}, {"dp": across}, {"dp": along})):
        copy = pltpu.make_async_remote_copy(
            src_ref=taken.at[2 * stage],
            dst_ref=taken.at[2 * stage + 1],
            send_sem=sems.at[stage],
            recv_sem=sems.at[3 + stage],
            device_id=target,
            device_id_type=MESH_ID,
        )
        copy.start()
        copy.wait()
        taken[2 * stage + 2] = taken[2 * stage] + taken[2 * stage + 1]

    def along_line(hop, owner):
        return pltpu.make_async_remote_copy(
            src_ref=taken.at[6],
            dst_ref=line_in.at[owner],
            send_sem=sems.at[6 + hop],
            recv_sem=sems.at[9 + owner],
            device_id=others[hop],
            device_id_type=MESH_ID,
        )

    for hop in range(3):
        along_line(hop, place).start()
    line_in[place] = taken[6]
    for hop in range(3):
        along_line(hop, (place + hop + 1) % 4).wait_recv()
    out[...] = (line_in[0] + line_in[1]) + (line_in[2] + line_in[3])
    for hop in range(3):
        along_line(hop, place).wait_send()


def clip_of(totals, gain_cols):
    gains, squares = totals[:, :gain_cols], totals[:, gain_cols:]
    square_all = jnp.sum(squares) + jnp.sum(gains * gains)
    return CLIP_NORM / jnp.maximum(jnp.sqrt(square_all), CLIP_NORM)


def update_body(widths, gain_cols, totals, *refs):
    gains, gain_first, gain_second = refs[:3]
    owned, (first, second), outs = refs[3:8], refs[8:10], refs[10:]
    clip_factor = clip_of(totals[...], gain_cols)

    @pl.when(pl.program_id(0) == 0)
    def _():
        outs[8][...] = gains[0:1, :]
        outs[9][...] = gains[1:2, :]
        outs[10][...] = adam_direction(
            gains[...], gain_first[...], gain_second[...], clip_factor
        )

    bounds = [0, widths[0], widths[0] + widths[1], sum(widths[:3])]
    grads = [owned[0][:, bounds[place] : bounds[place + 1]] for place in range(3)]
    grads += [item[...] for item in owned[1:]]
    start = 0
    for grad, grad_out in zip(grads, outs[:7]):
        grad_out[...] = grad
        span = slice(start, start + grad.shape[1])
        outs[7][:, span] = adam_direction(grad, first[:, span], second[:, span], clip_factor)
        start = start + grad.shape[1]


def update_rows(owned, first, second, totals, gains, gain_cols, widths):
    shard_rows, pack_cols = first.shape
    rows = min(32, shard_rows)

    def block(width):
        return pl.BlockSpec((rows, width), lambda row: (row, 0))

    def same(depth, width):
        return pl.BlockSpec((depth, width), lambda row: (0, 0))

    return pl.pallas_call(
        functools.partial(update_body, widths, gain_cols),
        grid=(shard_rows // rows,),
        out_shape=[jax.ShapeDtypeStruct((shard_rows, width), jnp.float32) for width in widths]
        + [jax.ShapeDtypeStruct((shard_rows, pack_cols), jnp.float32)]
        + [jax.ShapeDtypeStruct((depth, shard_rows), jnp.float32) for depth in (1, 1, 2)],
        in_specs=[same(*totals.shape)]
        + [same(2, shard_rows)] * 3
        + [block(item.shape[1]) for item in owned]
        + [block(pack_cols)] * 2,
        out_specs=[block(width) for width in widths]
        + [block(pack_cols)]
        + [same(depth, shard_rows) for depth in (1, 1, 2)],
        compiler_params=pltpu.CompilerParams(vmem_limit_bytes=62 << 20),
        cost_estimate=busy(15),
    )(totals, *gains, *owned, first, second)


def busy(microseconds):
    return pl.CostEstimate(
        flops=microseconds * 10**9, bytes_accessed=1 << 20, transcendentals=0
    )


def weave(order):
    for events in order:
        next(events, None)
    for events in order:
        for _ in events:
            pass


def line_body(steps, finish, extra_count, kept_count, *refs):
    part, extra, out = refs[0], refs[1 : 1 + extra_count], refs[1 + extra_count]
    kept, scratch = refs[2 + extra_count : 2 + extra_count + kept_count], refs[-4:]
    meet(True, False)
    weave([line_events(steps, finish, part, extra, out, kept, scratch)])


def line_sum(finish, part, extra, kept, which, steps):
    total_rows, width = part.shape
    in_vmem = pl.BlockSpec(memory_space=pltpu.VMEM)
    return pl.pallas_call(
        functools.partial(line_body, steps, finish, len(extra), len(kept)),
        out_shape=[jax.ShapeDtypeStruct((total_rows, width), jnp.bfloat16)] + kept,
        in_specs=[in_vmem] * (1 + len(extra)),
        out_specs=[pl.BlockSpec(memory_space=pl.ANY)] + [in_vmem] * len(kept),
        scratch_shapes=line_scratch(steps, total_rows, width),
        compiler_params=pltpu.CompilerParams(
            collective_id=which, has_side_effects=True, vmem_limit_bytes=60 << 20
        ),
        cost_estimate=busy(70),
    )(part, *extra)


def join_halves(held, own, crossed, other):
    place = lax.axis_index("tensor")
    at_end = (place == 0) | (place == 3)
    own = jnp.where(at_end, own, held)
    other = jnp.where(at_end, other, crossed)
    low_side = place < 2
    return jnp.concatenate(
        [jnp.where(low_side, own, other), jnp.where(low_side, other, own)], axis=0
    )


def finish_branch(total, own, local, step, done, extra, kept):
    tokens, gain = extra
    (state,) = kept
    rows_now = tokens[own, :].astype(jnp.float32) + total
    state[local, :] = rows_now
    done[step] = normalize(rows_now, gain[...]).astype(jnp.bfloat16)


def finish_output(total, own, local, step, done, extra, kept):
    state, teacher, factor = extra
    output_low, grad_output = kept
    output = state[local, :] + total
    output_low[local, :] = output.astype(jnp.bfloat16)
    grad_now = factor[own, :] * (output - teacher[own, :].astype(jnp.float32))
    grad_output[local, :] = grad_now
    done[step] = grad_now.astype(jnp.bfloat16)


def finish_ffn_back(total, own, local, step, done, extra, kept):
    state, grad_output, gain = extra
    grad_state, gain_grad = kept
    input_grad, gain_now = normalize_back(state[local, :], gain[...], total)
    grad_now = grad_output[local, :] + input_grad
    grad_state[local, :] = grad_now
    gain_grad[step : step + 1, :] = gain_now[None, :]
    done[step] = grad_now.astype(jnp.bfloat16)


def finish_attn_back(total, own, local, step, done, extra, kept):
    tokens, grad_state, gain = extra
    (gain_grad,) = kept
    input_grad, gain_now = normalize_back(tokens[own, :].astype(jnp.float32), gain[...], total)
    gain_grad[step : step + 1, :] = gain_now[None, :]
    done[step] = (grad_state[local, :] + input_grad).astype(jnp.bfloat16)


def local_call(body, time, outs, operands, scratch=(), vmem=60):
    in_vmem = pl.BlockSpec(memory_space=pltpu.VMEM)
    return pl.pallas_call(
        body,
        out_shape=outs,
        in_specs=[in_vmem] * len(operands),
        out_specs=[in_vmem] * len(outs),
        scratch_shapes=list(scratch),
        compiler_params=pltpu.CompilerParams(vmem_limit_bytes=vmem << 20),
        cost_estimate=busy(time),
    )(*operands)


def ffn_body(normed, w_gate, w_up, w_down, gate, up, product, part, total):
    step = pl.program_id(0)
    gate_now = jnp.dot(normed[...], w_gate[...], preferred_element_type=jnp.float32)
    up_now = jnp.dot(normed[...], w_up[...], preferred_element_type=jnp.float32)
    gate[...] = gate_now
    up[...] = up_now
    product_now = (gate_now * jax.nn.sigmoid(gate_now) * up_now).astype(jnp.bfloat16)
    product[...] = product_now
    accumulate(step, total, part, times_transpose(product_now, w_down[...]))


def ffn_back_body(
    grad_rows, w_gate, w_up, w_down, gate, up, grad_gate, grad_up, part, total
):
    step = pl.program_id(0)
    grad_product = jnp.dot(grad_rows[...], w_down[...], preferred_element_type=jnp.float32)
    gate_now = gate[...]
    sigmoid_gate = jax.nn.sigmoid(gate_now)
    gate_low = (
        grad_product * up[...] * sigmoid_gate * (1.0 + gate_now * (1.0 - sigmoid_gate))
    ).astype(jnp.bfloat16)
    up_low = (grad_product * (gate_now * sigmoid_gate)).astype(jnp.bfloat16)
    grad_gate[...] = gate_low
    grad_up[...] = up_low
    accumulate(
        step,
        total,
        part,
        times_transpose(gate_low, w_gate[...]) + times_transpose(up_low, w_up[...]),
    )


def accumulate(step, total, part, term):
    last = pl.num_programs(0) - 1

    @pl.when(step == 0)
    def _():
        total[...] = term

    @pl.when((step > 0) & (step < last))
    def _():
        total[...] += term

    @pl.when(step == last)
    def _():
        part[...] = (total[...] + term).astype(jnp.bfloat16)


def by_units(body, rows_in, weights, by_columns, outs, time):
    rows, width = rows_in.shape
    units = weights[0].shape[1]
    block = min(UNIT_BLOCK, units)

    def columns(depth):
        return pl.BlockSpec((depth, block), lambda step: (0, step))

    whole = pl.BlockSpec((rows, width), lambda step: (0, 0))
    return pl.pallas_call(
        body,
        grid=(units // block,),
        out_shape=[jax.ShapeDtypeStruct((rows, units), kind) for kind in outs]
        + [jax.ShapeDtypeStruct((rows, width), jnp.bfloat16)],
        in_specs=[whole]
        + [columns(item.shape[0]) for item in weights]
        + [columns(rows) for _ in by_columns],
        out_specs=[columns(rows) for _ in outs] + [whole],
        scratch_shapes=[pltpu.VMEM((rows, width), jnp.float32)],
        compiler_params=pltpu.CompilerParams(vmem_limit_bytes=56 << 20),
        cost_estimate=busy(time),
    )(rows_in, *weights, *by_columns)


UNIT_BLOCK = 512


MIDDLE_BLOCK = 256


def finish_output_near(total, own, local, step, done, extra, kept):
    state, teacher, factor = extra
    output_low, grad_output = kept
    output = state[local, :] + total
    output_low[local, :] = output.astype(jnp.bfloat16)
    grad_now = factor[own, :] * (output - teacher[local, :].astype(jnp.float32))
    grad_output[local, :] = grad_now
    done[step] = grad_now.astype(jnp.bfloat16)


MIDDLE_ORDER = (
    "c", "c", "l1", "c", "l1", "c", "l1", "l1", "l1", "l1",
    "l1", "l1", "l1", "l1", "l1", "c", "c", "l1", "c", "l1",
    "l2", "l1", "c", "s0", "s0", "s0", "s0", "c", "l2", "c",
    "l1", "l2", "s1", "s1", "s1", "s1", "l2", "s0", "s0", "l2",
    "s1", "s1", "l2", "s0", "s0", "l2", "l2", "l2", "s1", "s1",
    "l2",
)


def middle_body(steps, order, *refs):
    refs = list(refs)

    def take(count):
        taken = refs[:count]
        del refs[:count]
        return taken

    state, factor, gains = take(3)
    normed_two, teacher, *weights = take(5)
    output_low, grad_up, grad_state, gain_parts = take(4)
    owned, squares = take(2), take(2)
    grad_ffn, grad_branch, inner_store = take(3)
    normed, product, grads_in, grad_gate, part, total, teacher_near = take(7)
    slots, kept_out, kept_in = take(3), *take(2)
    first_line, second_line = take(4), take(4)
    scatter_refs = [take(5), take(5)]
    weight_sems, store_sems, load_sems, row_sems = take(4)
    at_end, side, inner, outer = line_place()
    rows, width = normed.shape
    half, quarter = rows // 2, rows // 4
    units = weights[0].shape[1]
    block = MIDDLE_BLOCK
    blocks = units // block
    meet(True, True)

    def chunk_copy(source, target, chunk, sem):
        return [
            pltpu.make_async_copy(
                source.at[pl.ds(part_of * half + chunk * quarter, quarter)],
                target.at[pl.ds(chunk * half + part_of * quarter, quarter)],
                row_sems.at[sem + part_of],
            )
            for part_of in range(2)
        ]

    near_rows = pl.ds(pl.multiple_of(side * half, half), half)
    load_teacher = pltpu.make_async_copy(teacher.at[near_rows], teacher_near, row_sems.at[8])
    load_teacher.start()
    loads = chunk_copy(normed_two, normed, 0, 0) + chunk_copy(normed_two, normed, 1, 2)
    for load in loads:
        load.start()

    def columns(index):
        return pl.ds(pl.multiple_of(lax.rem(index, blocks) * block, block), block)

    def weight_copies(index):
        slot = lax.rem(index, 2)
        return [
            pltpu.make_async_copy(
                weight.at[:, columns(index)], item.at[slot], weight_sems.at[place, slot]
            )
            for place, (weight, item) in enumerate(zip(weights, slots))
        ]

    def store(index):
        slot = lax.rem(index, 2)
        return pltpu.make_async_copy(kept_out.at[slot], inner_store.at[index], store_sems.at[slot])

    def restore(index):
        slot = lax.rem(index, 2)
        return pltpu.make_async_copy(
            inner_store.at[index - 2 * blocks], kept_in.at[slot], load_sems.at[slot]
        )

    def fetch(index):
        for copy in weight_copies(index):
            copy.start()

        @pl.when(index >= 2 * blocks)
        def _():
            restore(index).start()

    def add_term(index, term):
        @pl.when(lax.rem(index, blocks) == 0)
        def _():
            total[...] = term

        @pl.when(lax.rem(index, blocks) > 0)
        def _():
            total[...] += term

    def put_part(chunk):
        for part_of in range(2):
            part[pl.ds(part_of * half + chunk * quarter, quarter), :] = total[
                pl.ds(part_of * quarter, quarter), :
            ].astype(jnp.bfloat16)

    def chunk_rows(chunk):
        return pl.ds(chunk * half, half)

    def forward(chunk, index):
        slot = lax.rem(index, 2)
        fetch(index + 1)
        for copy in weight_copies(index):
            copy.wait()
        gate = jnp.dot(
            normed[chunk_rows(chunk), :], slots[0][slot], preferred_element_type=jnp.float32
        )
        up = jnp.dot(
            normed[chunk_rows(chunk), :], slots[1][slot], preferred_element_type=jnp.float32
        )

        @pl.when(index >= 2)
        def _():
            store(index - 2).wait()

        kept_out[slot, 0] = gate
        kept_out[slot, 1] = up
        store(index).start()
        product_now = (gate * jax.nn.sigmoid(gate) * up).astype(jnp.bfloat16)
        product[chunk_rows(chunk), columns(index)] = product_now
        add_term(index, times_transpose(product_now, slots[2][slot]))

    def backward(chunk, index):
        slot = lax.rem(index, 2)

        @pl.when(index + 1 < 4 * blocks)
        def _():
            fetch(index + 1)

        for copy in weight_copies(index):
            copy.wait()
        restore(index).wait()
        grad_product = jnp.dot(
            grads_in[chunk_rows(chunk), :], slots[2][slot], preferred_element_type=jnp.float32
        )
        gate, up = kept_in[slot, 0], kept_in[slot, 1]
        sigmoid_gate = jax.nn.sigmoid(gate)
        gate_low = (
            grad_product * up * sigmoid_gate * (1.0 + gate * (1.0 - sigmoid_gate))
        ).astype(jnp.bfloat16)
        up_low = (grad_product * (gate * sigmoid_gate)).astype(jnp.bfloat16)
        grad_gate[chunk_rows(chunk), columns(index)] = gate_low
        for part_of in range(2):
            grad_up[pl.ds(part_of * half + chunk * quarter, quarter), columns(index)] = up_low[
                part_of * quarter : (part_of + 1) * quarter
            ]
        add_term(
            index,
            times_transpose(gate_low, slots[0][slot]) + times_transpose(up_low, slots[1][slot]),
        )

    def compute():
        fetch(jnp.int32(0))
        for load in loads:
            load.wait()
        for chunk in range(2):
            for piece in range(2):
                first = chunk * blocks + piece * blocks // 2

                @pl.loop(first, first + blocks // 2)
                def _(index):
                    forward(chunk, index)

                if piece == 1:
                    put_part(chunk)
                    if chunk == 0:
                        load_teacher.wait()
                yield
        store(jnp.int32(2 * blocks - 2)).wait()
        store(jnp.int32(2 * blocks - 1)).wait()
        for chunk in range(2):
            copies = chunk_copy(grad_ffn, grads_in, chunk, 4 + 2 * chunk)
            for copy in copies:
                copy.start()
            for copy in copies:
                copy.wait()
            yield
            for piece in range(2):
                first = (2 + chunk) * blocks + piece * blocks // 2

                @pl.loop(first, first + blocks // 2)
                def _(index):
                    backward(chunk, index)

                if piece == 1:
                    put_part(chunk)
                yield

    lists = {
        "c": compute(),
        "l1": line_events(
            steps, finish_output_near, part, (state, teacher_near, factor), grad_ffn,
            (output_low, grad_state), first_line, watch=True,
        ),
        "l2": line_events(
            steps, finish_ffn_back, part, (state, grad_state, gains.at[1:2]), grad_branch,
            (grad_state, gain_parts), second_line,
        ),
    }
    for place, (left, right) in enumerate(((grads_in, product), (normed, grad_gate))):
        lists[f"s{place}"] = scatter_events(
            left, right, owned[place], squares[place], scatter_refs[place]
        )
    weave([lists[name] for name in order + tuple(sorted(lists))])


def middle(state, factor, gains, normed_two, teacher, weights, steps, which):
    rows, width = normed_two.shape
    units = weights[0].shape[1]
    low = functools.partial(jax.ShapeDtypeStruct, dtype=jnp.bfloat16)
    full = functools.partial(jax.ShapeDtypeStruct, dtype=jnp.float32)
    in_vmem = pl.BlockSpec(memory_space=pltpu.VMEM)
    anywhere = pl.BlockSpec(memory_space=pl.ANY)
    held = [
        low((rows // 2, width)),
        low((rows, units)),
        full((rows // 2, width)),
        full((steps, width)),
    ]
    owned = [full((width // 8, units))] * 2 + [full((1, 128))] * 2
    blocks = units // MIDDLE_BLOCK
    inner = (2, rows // 2, MIDDLE_BLOCK)
    far = [low((rows, width)), low((rows, width)), full((2 * blocks,) + inner)]
    scratch = [
        pltpu.VMEM((rows, width), jnp.bfloat16),
        pltpu.VMEM((rows, units), jnp.bfloat16),
        pltpu.VMEM((rows, width), jnp.bfloat16),
        pltpu.VMEM((rows, units), jnp.bfloat16),
        pltpu.VMEM((rows, width), jnp.bfloat16),
        pltpu.VMEM((rows // 2, width), jnp.float32),
        pltpu.VMEM((rows // 2, width), jnp.bfloat16),
    ]
    scratch += [pltpu.VMEM((2, width, MIDDLE_BLOCK), jnp.bfloat16)] * 3
    scratch += [pltpu.VMEM((2,) + inner, jnp.float32)] * 2
    scratch += line_scratch(steps, rows, width) * 2
    scratch += scatter_scratch(width // 8, units) * 2
    scratch += [
        pltpu.SemaphoreType.DMA((3, 2)),
        pltpu.SemaphoreType.DMA((2,)),
        pltpu.SemaphoreType.DMA((2,)),
        pltpu.SemaphoreType.DMA((9,)),
    ]
    return pl.pallas_call(
        functools.partial(middle_body, steps, MIDDLE_ORDER),
        out_shape=held + owned + far,
        in_specs=[in_vmem] * 3 + [anywhere] * 5,
        out_specs=[in_vmem] * 8 + [anywhere] * 3,
        scratch_shapes=scratch,
        compiler_params=pltpu.CompilerParams(
            collective_id=which, has_side_effects=True, vmem_limit_bytes=63 << 20
        ),
        cost_estimate=busy(150),
    )(state, factor, gains, normed_two, teacher, *weights)


def turn(head_rows, cosine, sine_table):
    middle = head_rows.shape[0] // 2
    upper, lower = head_rows[:middle], head_rows[middle:]
    return jnp.concatenate(
        [upper * cosine - lower * sine_table, lower * cosine + upper * sine_table], axis=0
    )


def normalize_rows(tokens, gain, normed):
    @pl.loop(0, tokens.shape[0] // 64)
    def _(block):
        span = pl.ds(pl.multiple_of(block * 64, 64), 64)
        normed[span, :] = normalize(tokens[span, :].astype(jnp.float32), gain[...]).astype(
            jnp.bfloat16
        )


def project_rows(normed, weights, cosine, sine_table, query_t, pairs):
    q_cols = query_t.shape[0]
    k_cols = pairs.shape[1] // 2
    lin_t = jnp.dot(
        normed[...], weights[:, : q_cols + k_cols], preferred_element_type=jnp.float32
    ).T
    for first in range(0, q_cols, HD):
        query_t[first : first + HD, :] = turn(
            lin_t[first : first + HD], cosine[...], sine_table[...]
        ).astype(jnp.bfloat16)
    keys = [
        turn(lin_t[first : first + HD], cosine[...], sine_table[...])
        for first in range(q_cols, q_cols + k_cols, HD)
    ]
    pairs[:, :k_cols] = jnp.concatenate(keys, axis=0).T.astype(jnp.bfloat16)
    pairs[:, k_cols:] = jnp.dot(
        normed[...],
        weights[:, q_cols + k_cols : q_cols + 2 * k_cols],
        preferred_element_type=jnp.float32,
    ).astype(jnp.bfloat16)


def project_body(tokens, gain, weights, cosine, sine_table, normed, query_t, pairs):
    normalize_rows(tokens, gain, normed)
    project_rows(normed, weights, cosine, sine_table, query_t, pairs)


def split_pairs(pairs, keys, keys_t, values, values_t):
    heads = pairs.shape[1] // (2 * HD)
    for head in range(heads):
        part = pairs[:, head * HD : (head + 1) * HD]
        if keys is not None:
            keys[head] = part
        if keys_t is not None:
            keys_t[head] = part.astype(jnp.float32).T.astype(jnp.bfloat16)
        part = pairs[:, (heads + head) * HD : (heads + head + 1) * HD]
        if values is not None:
            values[head] = part
        if values_t is not None:
            values_t[head] = part.astype(jnp.float32).T.astype(jnp.bfloat16)


SCORE_FACTOR = float(HD) ** (-0.5) * LOG2E
KEY_BLOCK = 256


def lifted_scores(key_block, query_head, query_pos, key_pos):
    scores = jnp.dot(key_block, query_head, preferred_element_type=jnp.float32)
    return jnp.where(key_pos <= query_pos, scores * SCORE_FACTOR, NEG_FILL)


def attend_heads(
    heads, group, query_t, query_pos, key_pos, keys, values_t, lifted, mixed_t, low_t, stats
):
    rows = query_t.shape[1]
    blocks = keys.shape[1] // KEY_BLOCK

    @pl.loop(*heads)
    def _(head):
        span = pl.ds(pl.multiple_of(head * HD, HD), HD)
        shared = head // group
        query_head = query_t[span, :]

        def scan_scores(block, highest):
            keys_now = pl.ds(pl.multiple_of(block * KEY_BLOCK, KEY_BLOCK), KEY_BLOCK)
            scores = lifted_scores(
                keys[shared, keys_now, :], query_head, query_pos[...], key_pos[keys_now, :]
            )
            lifted[keys_now, :] = scores
            return jnp.maximum(highest, jnp.max(scores, axis=0, keepdims=True))

        highest = lax.fori_loop(
            0, blocks, scan_scores, jnp.full((1, rows), NEG_FILL, jnp.float32)
        )
        ceiling = jnp.floor(highest)

        def scan_values(block, state):
            weight_sum, mixed = state
            keys_now = pl.ds(pl.multiple_of(block * KEY_BLOCK, KEY_BLOCK), KEY_BLOCK)
            expo = jnp.exp2(lifted[keys_now, :] - ceiling)
            mixed = mixed + jnp.dot(
                values_t[shared, :, keys_now],
                expo.astype(jnp.bfloat16),
                preferred_element_type=jnp.float32,
            )
            return weight_sum + jnp.sum(expo, axis=0, keepdims=True), mixed

        weight_sum, mixed = lax.fori_loop(
            0,
            blocks,
            scan_values,
            (jnp.zeros((1, rows), jnp.float32), jnp.zeros((HD, rows), jnp.float32)),
        )
        mixed = mixed / weight_sum
        mixed_t[span, :] = mixed
        low_t[span, :] = mixed.astype(jnp.bfloat16).astype(jnp.float32)
        stats[head] = jnp.concatenate([ceiling, weight_sum], axis=0)


def branch_rows(low_t, w_out, mixed_low, part):
    mixed_low[...] = low_t[...].T.astype(jnp.bfloat16)

    @pl.loop(0, part.shape[1] // 512)
    def _(block):
        span = pl.ds(pl.multiple_of(block * 512, 512), 512)
        part[:, span] = times_transpose(mixed_low[...], w_out[span, :]).astype(jnp.bfloat16)


def attend_body(
    group, query_t, pairs, query_pos, key_pos, w_out, mixed_t, mixed_low, stats, part,
    keys, values_t, lifted, low_t,
):
    split_pairs(pairs, keys, None, None, values_t)
    attend_heads(
        (0, query_t.shape[0] // HD), group, query_t, query_pos, key_pos, keys, values_t,
        lifted, mixed_t, low_t, stats,
    )
    branch_rows(low_t, w_out, mixed_low, part)


FRONT_ORDER = (
    "gs", "gq", "gk", "gv", "c", "gs", "gs", "gs", "gs", "c",
    "gq", "gk", "gv", "go", "gq", "gk", "gv", "gz", "gq", "gk",
    "gv", "gq", "gk", "gv", "c", "go", "c", "ga", "go", "c",
    "go", "c", "c", "gu", "go", "c", "line", "line", "line", "line",
    "gz", "gz", "line", "gd", "line", "ga", "gu", "ga", "gu", "line",
    "line", "line", "gz", "line", "gd", "gz", "gd", "ga", "gu", "gd",
)


def front_body(steps, group, all_rows, order, *refs):
    refs = list(refs)

    def take(count):
        taken = refs[:count]
        del refs[:count]
        return taken

    stretch_order, lengths = take(2)
    tokens, cosine_all, sine_all, loss_mask, attn_gain, mlp_gain = take(6)
    shards = take(7)
    normed, query_t, pairs_out, mixed_t, mixed_low, stats, gains, state = take(8)
    cosine, sine_table, query_pos, key_pos, factor = take(5)
    normed_two, pack_out, out_whole, gate, up, down = take(6)
    pack, w_out, gain_tiles, pairs, keys, values_t, lifted, low_t, part = take(9)
    counts, gain_shard, count_shard = take(3)
    line_refs = take(4)
    gather_sems = take(9)
    (own_sems,) = take(1)
    ring, core, first, second, far = square_peers()
    rows, width = tokens.shape
    q_cols, k_cols = query_t.shape[0], pairs.shape[1] // 2
    heads = q_cols // HD
    half = rows // 2
    slot_len = key_pos.shape[0]

    def wide(row, depth):
        return jnp.broadcast_to(row.astype(jnp.float32), (depth, row.shape[1]))

    places = [stretch_order[0, 2 * core + piece] for piece in range(2)]
    row_index = lax.broadcasted_iota(jnp.int32, (1, rows), 1)
    query_pos[...] = row_index + jnp.where(
        row_index < half, places[0] * half, (places[1] - 1) * half
    )
    valid = jnp.where((loss_mask[...] == 1) & (query_pos[...] < lengths[0]), 1.0, 0.0)
    count = jnp.sum(valid)
    count_high = jnp.floor(count / 64.0)
    lane = lax.broadcasted_iota(jnp.int32, count_shard.shape, 1)
    count_shard[...] = jnp.where(lane < 128, count_high, count - 64.0 * count_high).astype(
        jnp.bfloat16
    )
    gain_shard[:16, :] = wide(attn_gain[...], 16).astype(jnp.bfloat16)
    gain_shard[16:, :] = wide(mlp_gain[...], 16).astype(jnp.bfloat16)
    shards = shards[:4] + [gain_shard] + shards[4:] + [count_shard]
    meet(True, True)

    def place_rows():
        key_index = lax.broadcasted_iota(jnp.int32, (slot_len, 1), 0)
        position = key_index
        for stretch in range(slot_len // half):
            inside = (key_index >= stretch * half) & (key_index < (stretch + 1) * half)
            moved = key_index + (stretch_order[0, stretch] - stretch) * half
            position = jnp.where(inside, moved, position)
        key_pos[...] = jnp.where(position < lengths[0], position, slot_len)
        for source, target in ((cosine_all, cosine), (sine_all, sine_table)):
            for piece in range(2):
                span = slice(piece * half, (piece + 1) * half)
                row = query_pos[:, span]
                table = source[:, :half]
                for stretch in range(1, slot_len // half):
                    first_place = stretch * half
                    table = jnp.where(
                        row >= first_place, source[:, first_place : first_place + half], table
                    )
                target[:, span] = table

    def pair_rows(which):
        return pl.ds(pl.multiple_of(which * rows, rows), rows)

    def swap_pairs(which):
        return pltpu.make_async_remote_copy(
            src_ref=pairs.at[pair_rows(which)],
            dst_ref=pairs.at[pair_rows(which)],
            send_sem=own_sems.at[0],
            recv_sem=own_sems.at[1],
            device_id={"context": 1 - core},
            device_id_type=MESH_ID,
        )

    keep_pack = pltpu.make_async_copy(pack, pack_out, own_sems.at[2])
    keep_out = pltpu.make_async_copy(w_out, out_whole, own_sems.at[3])

    def compute():
        place_rows()
        yield
        for row in range(2):
            gains[row : row + 1, :] = jnp.concatenate(
                [
                    gain_tiles[32 * owner + 16 * row : 32 * owner + 16 * row + 16, :].astype(
                        jnp.float32
                    )[:1]
                    for owner in range(8)
                ],
                axis=1,
            )
        normalize_rows(tokens, gains.at[0:1], normed)
        yield
        project_rows(normed, pack, cosine, sine_table, query_t, pairs.at[pair_rows(core)])
        swap_pairs(core).start()
        keep_pack.start()
        yield
        swap_pairs(1 - core).wait_recv()
        split_pairs(pairs, keys, None, None, values_t)
        pairs_out[...] = pairs[...]
        for chunk in range(4):
            attend_heads(
                (chunk * heads // 4, (chunk + 1) * heads // 4), group, query_t, query_pos,
                key_pos, keys, values_t, lifted, mixed_t, low_t, stats,
            )
            yield
        keep_out.start()
        branch_rows(low_t, w_out, mixed_low, part)
        yield
        swap_pairs(core).wait_send()
        keep_pack.wait()
        keep_out.wait()
        yield
        count_rows = sum(
            counts[16 * owner : 16 * owner + 16, :].astype(jnp.float32)[:1] for owner in range(8)
        )
        valid_count = 64.0 * jnp.max(count_rows[:, :128]) + jnp.max(count_rows[:, 128:])
        factor[...] = (all_rows / valid_count * wide(valid, 8)).T[:, :1]
        yield

    targets = [
        pack.at[:, pl.ds(0, q_cols)],
        pack.at[:, pl.ds(q_cols, k_cols)],
        pack.at[:, pl.ds(q_cols + k_cols, k_cols)],
        w_out,
        gain_tiles,
        gate,
        up,
        down,
        counts,
    ]
    lists = {
        name: gather_events(source, target, sems)
        for name, source, target, sems in zip(
            ("gq", "gk", "gv", "go", "gs", "ga", "gu", "gd", "gz"), shards, targets, gather_sems
        )
    }
    lists["c"] = compute()
    lists["line"] = line_events(
        steps, finish_branch, part, (tokens, gains.at[1:2]), normed_two, (state,), line_refs
    )
    weave([lists[name] for name in order + tuple(sorted(lists))])


def front(scalars, tokens, rows_in, shards, group, all_rows, steps, which):
    rows, width = tokens.shape
    slot_len = rows_in[0].shape[1]
    q_cols, k_cols = shards[0].shape[1], shards[1].shape[1]
    heads, kv_heads = q_cols // HD, k_cols // HD
    low = functools.partial(jax.ShapeDtypeStruct, dtype=jnp.bfloat16)
    full = functools.partial(jax.ShapeDtypeStruct, dtype=jnp.float32)
    in_vmem = pl.BlockSpec(memory_space=pltpu.VMEM)
    anywhere = pl.BlockSpec(memory_space=pl.ANY)
    pack_cols = q_cols + 2 * k_cols
    held = [
        low((rows, width)),
        low((q_cols, rows)),
        low((slot_len, 2 * k_cols)),
        full((q_cols, rows)),
        low((rows, q_cols)),
        full((heads, 2, rows)),
        full((2, width)),
        full((rows // 2, width)),
        full((HD // 2, rows)),
        full((HD // 2, rows)),
        jax.ShapeDtypeStruct((1, rows), jnp.int32),
        jax.ShapeDtypeStruct((slot_len, 1), jnp.int32),
        full((rows, 1)),
    ]
    far = [low((rows, width)), low((width, pack_cols)), low((width, q_cols))]
    far += [low((8 * item.shape[0], item.shape[1])) for item in shards[4:]]
    return pl.pallas_call(
        functools.partial(front_body, steps, group, all_rows, FRONT_ORDER),
        out_shape=held + far,
        in_specs=[pl.BlockSpec(memory_space=pltpu.SMEM)] * 2
        + [in_vmem] * 6
        + [anywhere] * len(shards),
        out_specs=[in_vmem] * len(held) + [anywhere] * len(far),
        scratch_shapes=[
            pltpu.VMEM((width, pack_cols), jnp.bfloat16),
            pltpu.VMEM((width, q_cols), jnp.bfloat16),
            pltpu.VMEM((8 * 32, width // 8), jnp.bfloat16),
            pltpu.VMEM((slot_len, 2 * k_cols), jnp.bfloat16),
            pltpu.VMEM((kv_heads, slot_len, HD), jnp.bfloat16),
            pltpu.VMEM((kv_heads, HD, slot_len), jnp.bfloat16),
            pltpu.VMEM((slot_len, rows), jnp.float32),
            pltpu.VMEM((q_cols, rows), jnp.float32),
            pltpu.VMEM((rows, width), jnp.bfloat16),
            pltpu.VMEM((8 * 16, 256), jnp.bfloat16),
            pltpu.VMEM((32, width // 8), jnp.bfloat16),
            pltpu.VMEM((16, 256), jnp.bfloat16),
        ]
        + line_scratch(steps, rows, width)
        + [pltpu.SemaphoreType.DMA((16,))] * 9
        + [pltpu.SemaphoreType.DMA((4,))],
        compiler_params=pltpu.CompilerParams(
            collective_id=which, has_side_effects=True, vmem_limit_bytes=60 << 20
        ),
        cost_estimate=busy(130),
    )(*scalars, tokens, *rows_in, *shards)


def prepare_back(grad_branch, w_out, query_t, queries, grad_t):
    queries_f = query_t[...].astype(jnp.float32).T
    for head in range(queries.shape[0]):
        queries[head] = queries_f[:, head * HD : (head + 1) * HD].astype(jnp.bfloat16)
    grad_t[...] = (
        jnp.dot(grad_branch[...], w_out[...], preferred_element_type=jnp.float32)
        .astype(jnp.bfloat16)
        .astype(jnp.float32)
        .T
    )


def attend_back_heads(
    heads, group, query_t, mixed_t, stats, query_pos, key_pos, cosine, sine_table, grad_pairs,
    keys, keys_t, values, queries, grad_t, turned,
):
    rows = query_t.shape[1]
    blocks = keys.shape[1] // KEY_BLOCK
    score_scale = float(HD) ** (-0.5)

    @pl.loop(*heads)
    def _(head):
        span = pl.ds(pl.multiple_of(head * HD, HD), HD)
        shared = head // group
        query_head = query_t[span, :]
        query_rows = queries[head]
        ceiling = stats[head, 0:1, :]
        inverse = 1.0 / stats[head, 1:2, :]
        grad_head = grad_t[span, :]
        delta = jnp.sum(grad_head * mixed_t[span, :], axis=0, keepdims=True)
        scaled = grad_head * inverse
        scaled_high = scaled.astype(jnp.bfloat16)
        scaled_low = (scaled - scaled_high.astype(jnp.float32)).astype(jnp.bfloat16)
        scaled_both = jnp.concatenate([scaled_high, scaled_low], axis=0)
        grad_head_low = grad_head.astype(jnp.bfloat16)

        def scan_keys(block, grad_query_t):
            keys_now = pl.ds(pl.multiple_of(block * KEY_BLOCK, KEY_BLOCK), KEY_BLOCK)
            scores = lifted_scores(
                keys[shared, keys_now, :], query_head, query_pos[...], key_pos[keys_now, :]
            )
            expo = jnp.exp2(scores - ceiling)
            value_term = times_transpose(expo.astype(jnp.bfloat16), scaled_both)
            grad_probs = jnp.dot(
                values[shared, keys_now, :], grad_head_low, preferred_element_type=jnp.float32
            )
            grad_scores = (expo * inverse * (grad_probs - delta)).astype(jnp.bfloat16)
            key_term = jnp.dot(grad_scores, query_rows, preferred_element_type=jnp.float32)
            grad_pairs[shared, keys_now, :] += jnp.concatenate(
                [key_term * score_scale, value_term[:, :HD] + value_term[:, HD:]], axis=1
            )
            return grad_query_t + jnp.dot(
                keys_t[shared, :, keys_now], grad_scores, preferred_element_type=jnp.float32
            )

        grad_query_t = lax.fori_loop(
            0, blocks, scan_keys, jnp.zeros((HD, rows), jnp.float32)
        )
        turned[span, :] = turn(grad_query_t * score_scale, cosine[...], -sine_table[...])


def attend_back_body(
    group, grad_branch, w_out, query_t, pairs, mixed_t, stats, query_pos, key_pos, cosine,
    sine_table, grad_query, grad_pairs, keys, keys_t, values, queries, grad_t, turned,
):
    split_pairs(pairs, keys, keys_t, values, None)
    prepare_back(grad_branch, w_out, query_t, queries, grad_t)
    grad_pairs[...] = jnp.zeros_like(grad_pairs)
    attend_back_heads(
        (0, queries.shape[0]), group, query_t, mixed_t, stats, query_pos, key_pos, cosine,
        sine_table, grad_pairs, keys, keys_t, values, queries, grad_t, turned,
    )
    grad_query[...] = turned[...].T.astype(jnp.bfloat16)


def join_rows(grad_query, pair_grads, cosine, sine_table, weights, grad_lin, part):
    q_cols = grad_query.shape[1]
    k_cols = HD * len(pair_grads)
    grad_lin[:, :q_cols] = grad_query
    keys = [turn(item.T[:HD], cosine[...], -sine_table[...]) for item in pair_grads]
    grad_lin[:, q_cols : q_cols + k_cols] = jnp.concatenate(keys, axis=0).T.astype(jnp.bfloat16)
    grad_lin[:, q_cols + k_cols :] = jnp.concatenate(
        [item[:, HD:] for item in pair_grads], axis=1
    ).astype(jnp.bfloat16)

    @pl.loop(0, part.shape[1] // 512)
    def _(block):
        span = pl.ds(pl.multiple_of(block * 512, 512), 512)
        part[:, span] = times_transpose(
            grad_lin[...], weights[span, : q_cols + 2 * k_cols]
        ).astype(jnp.bfloat16)


def join_body(grad_query, grad_pairs, cosine, sine_table, weights, grad_lin, part):
    pair_grads = [grad_pairs[head] for head in range(grad_pairs.shape[0])]
    join_rows(grad_query[...], pair_grads, cosine, sine_table, weights, grad_lin, part)


BACK_ORDER = (
    "y", "s0", "s0", "s0", "s0", "s0", "s0", "c", "s1", "s1",
    "s1", "s1", "s1", "s1", "c", "c", "c", "y", "c", "c",
    "s0", "s0", "s1", "s1", "line", "s2", "s2", "s2", "s2", "line",
    "s2", "s2", "line", "line", "s2", "s2", "line", "line", "line", "line",
    "y", "line",
)


def back_body(steps, group, order, *refs):
    refs = list(refs)

    def take(count):
        taken = refs[:count]
        del refs[:count]
        return taken

    cosine, sine_table, query_pos, key_pos = take(4)
    grad_branch, w_out, query_t, pairs, mixed_t, stats, gains = take(7)
    normed_two, grad_up, mixed_low = take(3)
    pooled = take(3)
    later = take(4)
    (half_low,) = take(1)
    owned = take(3)
    (totals,) = take(1)
    out, block_out = take(2)
    keys, keys_t, values, queries, grad_t, turned, grad_pairs, pairs_in, grad_lin, part = take(10)
    gain_parts = take(1)
    loaded = take(4)
    squares = take(3)
    line_refs = take(4)
    total_refs = take(3)
    scatter_refs = [take(5) for _ in range(3)]
    (own_sems,) = take(1)
    weights, tokens, grad_state, normed = loaded
    ring, core, first, second, far = square_peers()
    rows = query_t.shape[1]
    heads = queries.shape[0]
    meet(True, True, True)
    loads = [
        pltpu.make_async_copy(source, target, own_sems.at[2 + place])
        for place, (source, target) in enumerate(zip(later, loaded))
    ]
    for load in loads:
        load.start()

    def own_rows(which):
        return pl.ds(pl.multiple_of(which * rows, rows), rows)

    swap = pltpu.make_async_remote_copy(
        src_ref=grad_pairs.at[:, own_rows(1 - core)],
        dst_ref=pairs_in,
        send_sem=own_sems.at[0],
        recv_sem=own_sems.at[1],
        device_id={"context": 1 - core},
        device_id_type=MESH_ID,
    )

    def compute():
        split_pairs(pairs, keys, keys_t, values, None)
        prepare_back(grad_branch, w_out, query_t, queries, grad_t)
        grad_pairs[...] = jnp.zeros_like(grad_pairs)
        yield
        for chunk in range(4):
            attend_back_heads(
                (chunk * heads // 4, (chunk + 1) * heads // 4), group, query_t, mixed_t, stats,
                query_pos, key_pos, cosine, sine_table, grad_pairs, keys, keys_t, values,
                queries, grad_t, turned,
            )
            yield
        swap.start()
        for load in loads:
            load.wait()
        grad_query = turned[...].T.astype(jnp.bfloat16)
        swap.wait_recv()
        pair_grads = [
            grad_pairs[head, own_rows(core), :] + pairs_in[head] for head in range(keys.shape[0])
        ]
        join_rows(grad_query, pair_grads, cosine, sine_table, weights, grad_lin, part)
        yield
        swap.wait_send()
        yield

    at_end, side, inner, outer = line_place()
    in_middle = jnp.logical_not(at_end)

    def spread():
        half = half_low.shape[0]
        near = block_out.at[pl.ds(pl.multiple_of(side * half, half), half)]
        far = block_out.at[pl.ds(pl.multiple_of((1 - side) * half, half), half)]

        def hand(source, target, send, recv, device):
            return pltpu.make_async_remote_copy(
                src_ref=source,
                dst_ref=target,
                send_sem=own_sems.at[send],
                recv_sem=own_sems.at[recv],
                device_id=device,
                device_id_type=MESH_ID,
            )

        to_outer = hand(half_low, near, 6, 7, outer)
        to_inner = hand(half_low, near, 8, 9, inner)
        onward = hand(far, far, 10, 9, outer)
        keep = pltpu.make_async_copy(half_low, near, own_sems.at[11])

        @pl.when(in_middle)
        def _():
            to_outer.start()
            to_inner.start()
            keep.start()

        yield

        @pl.when(in_middle)
        def _():
            to_inner.wait_recv()
            onward.start()

        yield

        @pl.when(in_middle)
        def _():
            to_outer.wait_send()
            to_inner.wait_send()
            onward.wait_send()
            keep.wait()

        @pl.when(at_end)
        def _():
            to_outer.wait_recv()
            onward.wait_recv()

        yield

    pairs_of = ((normed_two, grad_up), (grad_branch, mixed_low), (normed, grad_lin))
    lists = {
        f"s{place}": scatter_events(left, right, owned[place], squares[place], scatter_refs[place])
        for place, (left, right) in enumerate(pairs_of)
    }
    lists["c"] = compute()
    lists["y"] = spread()
    lists["line"] = line_events(
        steps, finish_attn_back, part, (tokens, grad_state, gains.at[0:1]), out, gain_parts,
        line_refs,
    )
    weave([lists[name] for name in order + tuple(sorted(lists))])
    own_row = total_refs[0].at[0]
    width = gains.shape[1]
    own_row[:, :width] = jnp.sum(gain_parts[0][...], axis=0, keepdims=True)
    own_row[:, width : 2 * width] = jnp.sum(pooled[0][...], axis=0, keepdims=True)
    own_row[:, 2 * width :] = sum(item[...] for item in (*pooled[1:], *squares))
    total_everywhere(totals, *total_refs)


def back(tables, held, factors, pooled, later, half_low, group, steps, which):
    query_t, pairs = held[2], held[3]
    q_cols, rows = query_t.shape
    slot_len, k_cols = pairs.shape[0], pairs.shape[1] // 2
    kv_heads, heads = k_cols // HD, q_cols // HD
    width = held[0].shape[1]
    pack_cols = q_cols + 2 * k_cols
    full = functools.partial(jax.ShapeDtypeStruct, dtype=jnp.float32)
    in_vmem = pl.BlockSpec(memory_space=pltpu.VMEM)
    anywhere = pl.BlockSpec(memory_space=pl.ANY)
    shard_rows = width // 8
    owned = [full((shard_rows, cols)) for cols in (factors[1].shape[1], q_cols, pack_cols)]
    pool_width = 2 * width + 128
    near = (*tables, *held, *factors, *pooled)
    scratch = [
        pltpu.VMEM((kv_heads, slot_len, HD), jnp.bfloat16),
        pltpu.VMEM((kv_heads, HD, slot_len), jnp.bfloat16),
        pltpu.VMEM((kv_heads, slot_len, HD), jnp.bfloat16),
        pltpu.VMEM((heads, rows, HD), jnp.bfloat16),
        pltpu.VMEM((q_cols, rows), jnp.float32),
        pltpu.VMEM((q_cols, rows), jnp.float32),
        pltpu.VMEM((kv_heads, slot_len, 2 * HD), jnp.float32),
        pltpu.VMEM((kv_heads, rows, 2 * HD), jnp.float32),
        pltpu.VMEM((rows, pack_cols), jnp.bfloat16),
        pltpu.VMEM((rows, width), jnp.bfloat16),
        pltpu.VMEM((steps, width), jnp.float32),
    ]
    scratch += [pltpu.VMEM(item.shape, item.dtype) for item in later]
    scratch += [pltpu.VMEM((1, 128), jnp.float32)] * 3
    scratch += line_scratch(steps, rows, width) + total_scratch(pool_width)
    for item in owned:
        scratch += scatter_scratch(*item.shape)
    return pl.pallas_call(
        functools.partial(back_body, steps, group, BACK_ORDER),
        out_shape=owned
        + [full((1, pool_width))]
        + [jax.ShapeDtypeStruct((rows, width), jnp.bfloat16)] * 2,
        in_specs=[in_vmem] * len(near) + [anywhere] * (len(later) + 1),
        out_specs=[in_vmem] * 4 + [anywhere] * 2,
        scratch_shapes=scratch + [pltpu.SemaphoreType.DMA((12,))],
        compiler_params=pltpu.CompilerParams(
            collective_id=which, has_side_effects=True, vmem_limit_bytes=62 << 20
        ),
        cost_estimate=busy(110),
    )(*near, *later, half_low)


def on_device(
    tokens,
    teacher,
    lengths,
    loss_mask,
    stretch_order,
    attn_gain,
    w_query,
    w_key,
    w_value,
    w_out,
    mlp_gain,
    w_gate,
    w_up,
    w_down,
    first_moment,
    second_moment,
    gain_first,
    gain_second,
):
    slot_count, stretch_len, model_width = tokens.shape
    token_rows = slot_count * stretch_len
    half_len = stretch_len // 2
    slot_len = stretch_len * lax.axis_size("context")
    all_rows = slot_count * lax.axis_size("dp") * slot_len
    steps = 4
    share_rows = token_rows // 2
    shard_rows = attn_gain.shape[0]
    q_cols, k_cols = w_query.shape[1], w_key.shape[1]
    square = lax.axis_size("dp") == 4 and lax.axis_size("context") == 2
    head_count = q_cols // HD
    kv_count = k_cols // HD
    group_size = head_count // kv_count
    token_rows_low = tokens.reshape(token_rows, model_width)
    low = functools.partial(jax.ShapeDtypeStruct, dtype=jnp.bfloat16)
    full = functools.partial(jax.ShapeDtypeStruct, dtype=jnp.float32)
    shard_f32 = full((share_rows, model_width))
    shard_low = low((share_rows, model_width))
    gain_parts = full((steps, model_width))
    line = functools.partial(line_sum, steps=steps)
    teacher_rows = teacher.reshape(token_rows, model_width)
    if square:
        angles = frequencies()[:, None] * jnp.arange(slot_len, dtype=jnp.float32)[None, :]
        (
            normed, query_t, pairs, mixed_t, mixed_low, stats, gains, state, cosine, sine_table,
            query_row, key_pos, factor, normed_two, first_pack, full_out, full_gate, full_up,
            full_down,
        ) = front(
            (stretch_order, lengths),
            token_rows_low,
            (
                jnp.cos(angles), jnp.sin(angles), loss_mask, attn_gain[None, :],
                mlp_gain[None, :],
            ),
            (w_query, w_key, w_value, w_out, w_gate, w_up, w_down),
            group_size,
            float(all_rows),
            steps,
            0,
        )
    else:
        local_index = stretch_len * lax.axis_index("context") + jnp.arange(
            stretch_len, dtype=jnp.int32
        )
        query_pos = positions_of(stretch_order, local_index, half_len)
        valid = ((loss_mask == 1) & (query_pos < lengths[:, None])).astype(jnp.float32)
        valid_count = lax.psum(jnp.sum(valid), ("dp", "context"))
        factor = jnp.float32(all_rows) / valid_count * valid.reshape(token_rows, 1)
        angles = frequencies()[:, None] * query_pos.reshape(1, token_rows).astype(jnp.float32)
        cosine, sine_table = jnp.cos(angles), jnp.sin(angles)
        key_pos = positions_of(stretch_order, jnp.arange(slot_len, dtype=jnp.int32), half_len)
        key_pos = jnp.where(key_pos < lengths[:, None], key_pos, slot_len).reshape(slot_len, 1)
        query_row = query_pos.reshape(1, token_rows)
        whole = functools.partial(
            lax.all_gather, axis_name=("dp", "context"), axis=0, tiled=True
        )
        first_pack = whole(jnp.concatenate([w_query, w_key, w_value], axis=1))
        full_out, full_gate, full_up, full_down = (
            whole(item) for item in (w_out, w_gate, w_up, w_down)
        )
        gain_one, gain_two = (
            whole(item)[None, :].astype(jnp.float32) for item in (attn_gain, mlp_gain)
        )
        normed, query_t, pairs_here = local_call(
            project_body,
            8,
            [
                low((token_rows, model_width)),
                low((q_cols, token_rows)),
                low((token_rows, 2 * k_cols)),
            ],
            [token_rows_low, gain_one, first_pack, cosine, sine_table],
        )
        pairs = lax.all_gather(pairs_here, "context", axis=0, tiled=True)
        mixed_t, mixed_low, stats, branch_part = local_call(
            functools.partial(attend_body, group_size),
            20,
            [
                full((q_cols, token_rows)),
                low((token_rows, q_cols)),
                full((head_count, 2, token_rows)),
                low((token_rows, model_width)),
            ],
            [query_t, pairs, query_row, key_pos, full_out],
            [
                pltpu.VMEM((kv_count, slot_len, HD), jnp.bfloat16),
                pltpu.VMEM((kv_count, HD, slot_len), jnp.bfloat16),
                pltpu.VMEM((slot_len, token_rows), jnp.float32),
                pltpu.VMEM((q_cols, token_rows), jnp.float32),
            ],
        )
        normed_two, state = line(
            finish_branch, branch_part, (token_rows_low, gain_two), [shard_f32], 0
        )
    if square:
        (
            output_low, grad_up, grad_state, gain_two_parts, owned_down, owned_gate,
            squares_down, squares_gate, _, grad_branch, _,
        ) = middle(
            state, factor, gains, normed_two, teacher_rows, (full_gate, full_up, full_down),
            steps, 1,
        )
        owned_up, owned_out, owned_qkv, totals, grad_tokens, block_out = back(
            (cosine, sine_table, query_row, key_pos),
            (grad_branch, full_out, query_t, pairs, mixed_t, stats, gains),
            (normed_two, grad_up, mixed_low),
            (gain_two_parts, squares_down, squares_gate),
            (first_pack, token_rows_low, grad_state, normed),
            output_low,
            group_size,
            steps,
            3,
        )
    else:
        gate, up, product, output_part = by_units(
            ffn_body,
            normed_two,
            [full_gate, full_up, full_down],
            [],
            [jnp.float32, jnp.float32, jnp.bfloat16],
            18,
        )
        grad_ffn, output_low, grad_output = line(
            finish_output, output_part, (state, teacher_rows, factor), [shard_low, shard_f32], 1
        )
        outward = [(1, 0), (2, 3)]
        own_half = lax.ppermute(output_low, "tensor", outward)
        crossed_half = lax.ppermute(output_low, "tensor", [(1, 2), (2, 1)])
        other_half = lax.ppermute(crossed_half, "tensor", outward)
        block_out = join_halves(output_low, own_half, crossed_half, other_half)
        grad_gate, grad_up, normed_part = by_units(
            ffn_back_body,
            grad_ffn,
            [full_gate, full_up, full_down],
            [gate, up],
            [jnp.bfloat16, jnp.bfloat16],
            18,
        )

        def owned(left, right):
            return lax.psum_scatter(
                column_term(left, right).astype(jnp.bfloat16),
                ("dp", "context"),
                scatter_dimension=0,
                tiled=True,
            ).astype(jnp.float32)

        owned_down = owned(grad_ffn, product)
        owned_gate = owned(normed_two, grad_gate)
        owned_up = owned(normed_two, grad_up)
        grad_branch, grad_state, gain_two_parts = line(
            finish_ffn_back, normed_part, (state, grad_output, gain_two), [shard_f32, gain_parts], 2
        )
        owned_out = owned(grad_branch, mixed_low)
        grad_query, grad_pairs = local_call(
            functools.partial(attend_back_body, group_size),
            24,
            [low((token_rows, q_cols)), full((kv_count, slot_len, 2 * HD))],
            [
                grad_branch, full_out, query_t, pairs, mixed_t, stats, query_row, key_pos,
                cosine, sine_table,
            ],
            [
                pltpu.VMEM((kv_count, slot_len, HD), jnp.bfloat16),
                pltpu.VMEM((kv_count, HD, slot_len), jnp.bfloat16),
                pltpu.VMEM((kv_count, slot_len, HD), jnp.bfloat16),
                pltpu.VMEM((head_count, token_rows, HD), jnp.bfloat16),
                pltpu.VMEM((q_cols, token_rows), jnp.float32),
                pltpu.VMEM((q_cols, token_rows), jnp.float32),
            ],
        )
        grad_pairs_own = lax.psum_scatter(
            grad_pairs, "context", scatter_dimension=1, tiled=True
        )
        grad_lin, inputs_part = local_call(
            join_body,
            6,
            [low((token_rows, q_cols + 2 * k_cols)), low((token_rows, model_width))],
            [grad_query, grad_pairs_own, cosine, sine_table, first_pack],
        )
        owned_qkv = owned(normed, grad_lin)
        grad_tokens, gain_one_parts = line(
            finish_attn_back, inputs_part, (token_rows_low, grad_state, gain_one), [gain_parts], 3
        )
    owned_all = [owned_qkv, owned_out, owned_gate, owned_up, owned_down]
    gain_cols = 2 * model_width
    if not square:
        square_local = sum(jnp.sum(part * part) for part in owned_all)
        totals = lax.psum(
            jnp.concatenate(
                [
                    jnp.sum(gain_one_parts, axis=0),
                    jnp.sum(gain_two_parts, axis=0),
                    jnp.full((128,), square_local / 128.0),
                ]
            )[None, :],
            ("dp", "context", "tensor"),
        )
    gains_owned = lax.dynamic_slice_in_dim(
        totals[0, :gain_cols].reshape(2, model_width),
        lax.axis_index(("dp", "context")) * shard_rows,
        shard_rows,
        1,
    )
    widths = (q_cols, k_cols, k_cols) + tuple(item.shape[1] for item in owned_all[1:])
    *matrices, adam_step, gain_one_grad, gain_two_grad, gain_step = update_rows(
        owned_all,
        first_moment,
        second_moment,
        totals,
        (gains_owned, gain_first, gain_second),
        gain_cols,
        widths,
    )
    return (
        block_out.reshape(slot_count, stretch_len, model_width),
        grad_tokens.reshape(slot_count, stretch_len, model_width),
        gain_one_grad[0],
        matrices[0],
        matrices[1],
        matrices[2],
        matrices[3],
        gain_two_grad[0],
        matrices[4],
        matrices[5],
        matrices[6],
        adam_step,
        gain_step,
    )


def solution(mesh):
    in_specs = (
        P("dp", "context", None),
        P("dp", "context", None),
        P("dp"),
        P("dp", "context"),
        P("dp", None),
        P(("dp", "context")),
        P(("dp", "context"), "tensor"),
        P(("dp", "context"), "tensor"),
        P(("dp", "context"), "tensor"),
        P(("dp", "context"), "tensor"),
        P(("dp", "context")),
        P(("dp", "context"), "tensor"),
        P(("dp", "context"), "tensor"),
        P(("dp", "context"), "tensor"),
        P(("dp", "context"), "tensor"),
        P(("dp", "context"), "tensor"),
        P(None, ("dp", "context")),
        P(None, ("dp", "context")),
    )
    out_specs = (
        P("dp", "context", None),
        P("dp", "context", None),
        P(("dp", "context")),
        P(("dp", "context"), "tensor"),
        P(("dp", "context"), "tensor"),
        P(("dp", "context"), "tensor"),
        P(("dp", "context"), "tensor"),
        P(("dp", "context")),
        P(("dp", "context"), "tensor"),
        P(("dp", "context"), "tensor"),
        P(("dp", "context"), "tensor"),
        P(("dp", "context"), "tensor"),
        P(None, ("dp", "context")),
    )
    return jax.shard_map(
        on_device, mesh=mesh, in_specs=in_specs, out_specs=out_specs, check_vma=False
    )
```

```python
import functools
import math

import jax
import jax.numpy as jnp
from jax import lax
from jax.experimental import pallas as pl
from jax.experimental.pallas import tpu as pltpu
from jax.sharding import PartitionSpec as P

HD = 64
STEP = 10


EPS_NORM = 1e-05
ROPE_BASE = 500000.0
OLD_CONTEXT = 8192.0
SCALE_FACTOR = 32.0
LOW_FACTOR = 1.0
HIGH_FACTOR = 4.0
LOG2E = 1.4426950408889634
NEG_FILL = -1e30
BETA_ONE = 0.9
BETA_TWO = 0.95
ADAM_EPS = 1e-08
CLIP_NORM = 1.0


def frequencies():
    channel = jnp.arange(HD // 2, dtype=jnp.float32)
    base_freq = jnp.power(jnp.float32(ROPE_BASE), -2.0 * channel / HD)
    wavelength = 2.0 * math.pi / base_freq
    smooth = (OLD_CONTEXT / wavelength - LOW_FACTOR) / (HIGH_FACTOR - LOW_FACTOR)
    blended = (1.0 - smooth) * base_freq / SCALE_FACTOR + smooth * base_freq
    slow_freq = jnp.where(wavelength > OLD_CONTEXT / LOW_FACTOR, base_freq / SCALE_FACTOR, blended)
    return jnp.where(wavelength < OLD_CONTEXT / HIGH_FACTOR, base_freq, slow_freq)


def normalize(values, gain):
    factor = lax.rsqrt(jnp.mean(values * values, axis=-1, keepdims=True) + EPS_NORM)
    return values * factor * gain.astype(jnp.float32)


def normalize_back(values, gain, upstream):
    factor = lax.rsqrt(jnp.mean(values * values, axis=-1, keepdims=True) + EPS_NORM)
    unit_rows = values * factor
    gain_grad = jnp.sum(upstream * unit_rows, axis=0)
    scaled_up = upstream * gain.astype(jnp.float32)
    input_grad = factor * (
        scaled_up - unit_rows * jnp.mean(scaled_up * unit_rows, axis=-1, keepdims=True)
    )
    return (input_grad, gain_grad)


def positions_of(order_table, row_index, half_len):
    stretch_slot = row_index // half_len
    matches = stretch_slot[:, None] == jnp.arange(order_table.shape[1], dtype=jnp.int32)[None, :]
    stretch_ids = jnp.sum(jnp.where(matches[None, :, :], order_table[:, None, :], 0), axis=-1)
    return stretch_ids * half_len + row_index % half_len


def times_transpose(left, right):
    return lax.dot_general(
        left, right, (((1,), (1,)), ((), ())), preferred_element_type=jnp.float32
    )


def column_term(left, right):
    return lax.dot_general(
        left, right, (((0,), (0,)), ((), ())), preferred_element_type=jnp.float32
    )


def adam_direction(gradient, first, second, clip_factor):
    clipped = gradient * clip_factor
    first_new = BETA_ONE * first + (1.0 - BETA_ONE) * clipped
    second_new = BETA_TWO * second + (1.0 - BETA_TWO) * clipped * clipped
    return (
        first_new
        / (1.0 - BETA_ONE**STEP)
        / (jnp.sqrt(second_new / (1.0 - BETA_TWO**STEP)) + ADAM_EPS)
    )


MESH_ID = pl.DeviceIdType.MESH


def row_mean(values):
    return jnp.mean(values, axis=-1, keepdims=True)


def line_place():
    place = lax.axis_index("tensor")
    side = place // 2
    inner = place + 1 - 2 * side
    outer = jnp.clip(place - 1 + 2 * side, 0, 3)
    return (place == 0) | (place == 3), side, {"tensor": inner}, {"tensor": outer}


def square_peers():
    ring, core = lax.axis_index("dp"), lax.axis_index("context")
    across = ring + 1 - 2 * (ring % 2)
    along = (ring + 2) % 4
    first = across * (1 - core) + along * core
    second = along * (1 - core) + across * core
    return ring, core, first, second, 3 - ring


def meet(with_line, with_square, with_all=False):
    barrier = pltpu.get_barrier_semaphore()
    expected = jnp.int32(0)
    if with_all:
        place = lax.axis_index("tensor")
        for hop in (1, 2, 3):
            pl.semaphore_signal(
                barrier,
                inc=1,
                device_id={"tensor": (place + hop) % 4},
                device_id_type=MESH_ID,
            )
        expected = expected + 3
    elif with_line:
        at_end, side, inner, outer = line_place()
        pl.semaphore_signal(barrier, inc=1, device_id=inner, device_id_type=MESH_ID)

        @pl.when(jnp.logical_not(at_end))
        def _():
            pl.semaphore_signal(barrier, inc=1, device_id=outer, device_id_type=MESH_ID)

        expected = expected + 2 - at_end.astype(jnp.int32)
    if with_square:
        ring, core, first, second, far = square_peers()
        for target in ({"dp": first}, {"dp": second}, {"context": 1 - core}):
            pl.semaphore_signal(barrier, inc=1, device_id=target, device_id_type=MESH_ID)
        expected = expected + 3
    pl.semaphore_wait(barrier, expected)


def line_scratch(steps, total_rows, width):
    rows = total_rows // 2 // steps
    return [
        pltpu.VMEM((2, steps, rows, width), jnp.bfloat16),
        pltpu.VMEM((steps, rows, width), jnp.bfloat16),
        pltpu.VMEM((steps, rows, width), jnp.bfloat16),
        pltpu.SemaphoreType.DMA((12, steps)),
    ]


def line_events(steps, finish, part, extra, out, kept, scratch, watch=False):
    outer_in, cross_in, done, sems = scratch
    at_end, side, inner, outer = line_place()
    in_middle = jnp.logical_not(at_end)
    half = part.shape[0] // 2
    rows = half // steps

    def near(step):
        return pl.ds(pl.multiple_of(side * half + step * rows, rows), rows)

    def far(step):
        return pl.ds(pl.multiple_of((1 - side) * half + step * rows, rows), rows)

    def remote(src, dst, send, recv, step, target):
        return pltpu.make_async_remote_copy(
            src_ref=src,
            dst_ref=dst,
            send_sem=sems.at[send, step],
            recv_sem=sems.at[recv, step],
            device_id=target,
            device_id_type=MESH_ID,
        )

    def inward(kind, step):
        span = near(step) if kind else far(step)
        return remote(part.at[span], outer_in.at[kind, step], kind, 2 + kind, step, inner)

    def across(step):
        return remote(outer_in.at[0, step], cross_in.at[step], 4, 5, step, inner)

    def hand_outer(step):
        return remote(done.at[step], out.at[near(step)], 6, 9, step, outer)

    def hand_inner(step):
        return remote(done.at[step], out.at[near(step)], 7, 10, step, inner)

    def hand_on(step):
        return remote(out.at[far(step)], out.at[far(step)], 8, 10, step, outer)

    def keep(step):
        return pltpu.make_async_copy(done.at[step], out.at[near(step)], sems.at[11, step])

    def feed(index):
        step, kind = divmod(index, 2)
        if index >= 2:
            inward(kind, step - 1).wait_send()
        inward(kind, step).start()

    def pass_on(step):
        hand_inner(step).wait_recv()
        hand_on(step).start()

    def arrive(step):
        @pl.when(in_middle)
        def _():
            keep(step).wait()

        @pl.when(at_end)
        def _():
            hand_outer(step).wait_recv()
            hand_on(step).wait_recv()

    @pl.when(at_end)
    def _():
        feed(0)
        feed(1)

    for item in kept:
        if item.shape[0] == steps:
            item[...] = jnp.zeros_like(item)
    yield
    for step in range(steps):

        @pl.when(at_end)
        def _():
            if step + 1 < steps:
                feed(2 * step + 2)

        @pl.when(in_middle)
        def _():
            inward(0, step).wait_recv()
            outer_in[0, step] = (
                outer_in[0, step].astype(jnp.float32) + part[far(step), :].astype(jnp.float32)
            ).astype(jnp.bfloat16)
            across(step).start()

        yield

        @pl.when(at_end)
        def _():
            if step + 1 < steps:
                feed(2 * step + 3)

        @pl.when(in_middle)
        def _():
            inward(1, step).wait_recv()
            across(step).wait_recv()
            total = (
                part[near(step), :].astype(jnp.float32)
                + outer_in[1, step].astype(jnp.float32)
                + cross_in[step].astype(jnp.float32)
            )
            finish(total, near(step), pl.ds(step * rows, rows), step, done, extra, kept)
            hand_outer(step).start()
            hand_inner(step).start()
            keep(step).start()
            if step > 0:
                pass_on(step - 1)

        yield
        if watch and step >= 2:
            arrive(step - 2)
            yield

    @pl.when(in_middle)
    def _():
        pass_on(steps - 1)

    @pl.when(at_end)
    def _():
        for kind in range(2):
            inward(kind, steps - 1).wait_send()

    if watch:
        yield
    for step in range(steps - 2 if watch else 0, steps):
        arrive(step)
        if watch:
            yield

    @pl.when(in_middle)
    def _():
        for step in range(steps):
            across(step).wait_send()
            hand_outer(step).wait_send()
            hand_inner(step).wait_send()
            hand_on(step).wait_send()

    yield


def gather_events(src, dst, sems):
    rows = src.shape[0]
    ring, core, first, second, far = square_peers()
    to_first, to_second, to_twin = {"dp": first}, {"dp": second}, {"context": 1 - core}

    def span(owner_ring, owner_core):
        return pl.ds(pl.multiple_of((owner_ring * 2 + owner_core) * rows, rows), rows)

    def copy(source, owner_ring, owner_core, slot, target):
        return pltpu.make_async_remote_copy(
            src_ref=source,
            dst_ref=dst.at[span(owner_ring, owner_core)],
            send_sem=sems.at[slot],
            recv_sem=sems.at[8 + owner_ring * 2 + owner_core],
            device_id=target,
            device_id_type=MESH_ID,
        )

    own = pltpu.make_async_copy(src, dst.at[span(ring, core)], sems.at[7])
    copy(src, ring, core, 0, to_first).start()
    copy(src, ring, core, 1, to_second).start()
    copy(src, ring, core, 2, to_twin).start()
    own.start()
    yield
    block = dst.at[span(first, core)]
    copy(block, first, core, 3, to_second).wait_recv()
    copy(block, first, core, 3, to_second).start()
    copy(block, first, core, 4, to_twin).start()
    yield
    block = dst.at[span(second, core)]
    copy(block, second, core, 5, to_twin).wait_recv()
    copy(block, second, core, 5, to_twin).start()
    yield
    block = dst.at[span(far, core)]
    copy(block, far, core, 6, to_twin).wait_recv()
    copy(block, far, core, 6, to_twin).start()
    yield
    for owner_ring in (ring, first, second, far):
        block = dst.at[span(owner_ring, 1 - core)]
        copy(block, owner_ring, 1 - core, 2, to_twin).wait_recv()
    for slot in range(7):
        copy(src, ring, core, slot, to_twin).wait_send()
    own.wait()
    yield


def lane_sums(item):
    sums = jnp.sum(item[...] * item[...], axis=0, keepdims=True)
    return sum(sums[:, first : first + 128] for first in range(0, sums.shape[1], 128))


def scatter_scratch(rows, cols):
    return [
        pltpu.VMEM((2, rows, cols), jnp.bfloat16),
        pltpu.VMEM((4, rows, cols), jnp.bfloat16),
        pltpu.VMEM((2, rows, cols), jnp.bfloat16),
        pltpu.VMEM((1, rows, cols), jnp.bfloat16),
        pltpu.SemaphoreType.DMA((14,)),
    ]


def scatter_events(left, right, out, square, scratch):
    twin_out, twin_in, first_in, second_in, sems = scratch
    rows = out.shape[0]
    ring, core, first, second, far = square_peers()
    to_first, to_second, to_twin = {"dp": first}, {"dp": second}, {"context": 1 - core}
    own_order = (far, first, second, ring)
    twin_order = (far, second, first, ring)

    def block(owner_ring, owner_core):
        span = pl.ds(pl.multiple_of((owner_ring * 2 + owner_core) * rows, rows), rows)
        return column_term(left[:, span], right[...])

    def remote(src, dst, slot, target):
        return pltpu.make_async_remote_copy(
            src_ref=src,
            dst_ref=dst,
            send_sem=sems.at[slot],
            recv_sem=sems.at[7 + slot],
            device_id=target,
            device_id_type=MESH_ID,
        )

    def swap(role):
        return remote(twin_out.at[role % 2], twin_in.at[role], role, to_twin)

    def over_first(role):
        return remote(twin_in.at[role], first_in.at[role], 4 + role, to_first)

    over_second = remote(twin_in.at[2], second_in.at[0], 6, to_second)

    def for_twin(role):
        if role >= 2:
            swap(role - 2).wait_send()
        twin_out[role % 2] = block(twin_order[role], 1 - core).astype(jnp.bfloat16)
        swap(role).start()

    for role in range(2):
        for_twin(role)
        yield
    for role in range(2):
        term = block(own_order[role], core)
        swap(role).wait_recv()
        twin_in[role] = (term + twin_in[role].astype(jnp.float32)).astype(jnp.bfloat16)
        over_first(role).start()
        yield
    for_twin(2)
    yield
    for_twin(3)
    yield
    term = block(second, core)
    swap(2).wait_recv()
    over_first(0).wait_recv()
    twin_in[2] = (
        term + twin_in[2].astype(jnp.float32) + first_in[0].astype(jnp.float32)
    ).astype(jnp.bfloat16)
    over_second.start()
    yield
    term = block(ring, core)
    swap(3).wait_recv()
    over_first(1).wait_recv()
    out[...] = term + twin_in[3].astype(jnp.float32) + first_in[1].astype(jnp.float32)
    yield
    over_second.wait_recv()
    out[...] += second_in[0].astype(jnp.float32)
    square[...] = lane_sums(out)
    swap(2).wait_send()
    swap(3).wait_send()
    over_first(0).wait_send()
    over_first(1).wait_send()
    over_second.wait_send()
    yield


def total_scratch(width):
    return [
        pltpu.VMEM((7, 1, width), jnp.float32),
        pltpu.VMEM((4, 1, width), jnp.float32),
        pltpu.SemaphoreType.DMA((13,)),
    ]


def total_everywhere(out, taken, line_in, sems):
    ring, core, first, second, far = square_peers()
    place = lax.axis_index("tensor")
    across = ring + 1 - 2 * (ring % 2)
    along = (ring + 2) % 4
    others = [{"tensor": (place + hop) % 4} for hop in (1, 2, 3)]
    for stage, target in enumerate(({"context": 1 - core}, {"dp": across}, {"dp": along})):
        copy = pltpu.make_async_remote_copy(
            src_ref=taken.at[2 * stage],
            dst_ref=taken.at[2 * stage + 1],
            send_sem=sems.at[stage],
            recv_sem=sems.at[3 + stage],
            device_id=target,
            device_id_type=MESH_ID,
        )
        copy.start()
        copy.wait()
        taken[2 * stage + 2] = taken[2 * stage] + taken[2 * stage + 1]

    def along_line(hop, owner):
        return pltpu.make_async_remote_copy(
            src_ref=taken.at[6],
            dst_ref=line_in.at[owner],
            send_sem=sems.at[6 + hop],
            recv_sem=sems.at[9 + owner],
            device_id=others[hop],
            device_id_type=MESH_ID,
        )

    for hop in range(3):
        along_line(hop, place).start()
    line_in[place] = taken[6]
    for hop in range(3):
        along_line(hop, (place + hop + 1) % 4).wait_recv()
    out[...] = (line_in[0] + line_in[1]) + (line_in[2] + line_in[3])
    for hop in range(3):
        along_line(hop, place).wait_send()


def clip_of(totals, gain_cols):
    gains, squares = totals[:, :gain_cols], totals[:, gain_cols:]
    square_all = jnp.sum(squares) + jnp.sum(gains * gains)
    return CLIP_NORM / jnp.maximum(jnp.sqrt(square_all), CLIP_NORM)


def update_body(widths, gain_cols, totals, *refs):
    gains, gain_first, gain_second = refs[:3]
    owned, (first, second), outs = refs[3:8], refs[8:10], refs[10:]
    clip_factor = clip_of(totals[...], gain_cols)

    @pl.when(pl.program_id(0) == 0)
    def _():
        outs[8][...] = gains[0:1, :]
        outs[9][...] = gains[1:2, :]
        outs[10][...] = adam_direction(
            gains[...], gain_first[...], gain_second[...], clip_factor
        )

    bounds = [0, widths[0], widths[0] + widths[1], sum(widths[:3])]
    grads = [owned[0][:, bounds[place] : bounds[place + 1]] for place in range(3)]
    grads += [item[...] for item in owned[1:]]
    start = 0
    for grad, grad_out in zip(grads, outs[:7]):
        grad_out[...] = grad
        span = slice(start, start + grad.shape[1])
        outs[7][:, span] = adam_direction(grad, first[:, span], second[:, span], clip_factor)
        start = start + grad.shape[1]


def update_rows(owned, first, second, totals, gains, gain_cols, widths):
    shard_rows, pack_cols = first.shape
    rows = min(128, shard_rows)

    def block(width):
        return pl.BlockSpec((rows, width), lambda row: (row, 0))

    def same(depth, width):
        return pl.BlockSpec((depth, width), lambda row: (0, 0))

    return pl.pallas_call(
        functools.partial(update_body, widths, gain_cols),
        grid=(shard_rows // rows,),
        out_shape=[jax.ShapeDtypeStruct((shard_rows, width), jnp.float32) for width in widths]
        + [jax.ShapeDtypeStruct((shard_rows, pack_cols), jnp.float32)]
        + [jax.ShapeDtypeStruct((depth, shard_rows), jnp.float32) for depth in (1, 1, 2)],
        in_specs=[same(*totals.shape)]
        + [same(2, shard_rows)] * 3
        + [block(item.shape[1]) for item in owned]
        + [block(pack_cols)] * 2,
        out_specs=[block(width) for width in widths]
        + [block(pack_cols)]
        + [same(depth, shard_rows) for depth in (1, 1, 2)],
        compiler_params=pltpu.CompilerParams(vmem_limit_bytes=62 << 20),
        cost_estimate=busy(15),
    )(totals, *gains, *owned, first, second)


def busy(microseconds):
    return pl.CostEstimate(
        flops=microseconds * 10**9, bytes_accessed=1 << 20, transcendentals=0
    )


def weave(order):
    for events in order:
        next(events, None)
    for events in order:
        for _ in events:
            pass


def line_body(steps, finish, extra_count, kept_count, *refs):
    part, extra, out = refs[0], refs[1 : 1 + extra_count], refs[1 + extra_count]
    kept, scratch = refs[2 + extra_count : 2 + extra_count + kept_count], refs[-4:]
    meet(True, False)
    weave([line_events(steps, finish, part, extra, out, kept, scratch)])


def line_sum(finish, part, extra, kept, which, steps):
    total_rows, width = part.shape
    in_vmem = pl.BlockSpec(memory_space=pltpu.VMEM)
    return pl.pallas_call(
        functools.partial(line_body, steps, finish, len(extra), len(kept)),
        out_shape=[jax.ShapeDtypeStruct((total_rows, width), jnp.bfloat16)] + kept,
        in_specs=[in_vmem] * (1 + len(extra)),
        out_specs=[pl.BlockSpec(memory_space=pl.ANY)] + [in_vmem] * len(kept),
        scratch_shapes=line_scratch(steps, total_rows, width),
        compiler_params=pltpu.CompilerParams(
            collective_id=which, has_side_effects=True, vmem_limit_bytes=60 << 20
        ),
        cost_estimate=busy(70),
    )(part, *extra)


def join_halves(held, own, crossed, other):
    place = lax.axis_index("tensor")
    at_end = (place == 0) | (place == 3)
    own = jnp.where(at_end, own, held)
    other = jnp.where(at_end, other, crossed)
    low_side = place < 2
    return jnp.concatenate(
        [jnp.where(low_side, own, other), jnp.where(low_side, other, own)], axis=0
    )


def finish_branch(total, own, local, step, done, extra, kept):
    tokens, gain = extra
    (state,) = kept
    rows_now = tokens[own, :].astype(jnp.float32) + total
    state[local, :] = rows_now
    done[step] = normalize(rows_now, gain[...]).astype(jnp.bfloat16)


def finish_output(total, own, local, step, done, extra, kept):
    state, teacher, factor = extra
    output_low, grad_output = kept
    output = state[local, :] + total
    output_low[local, :] = output.astype(jnp.bfloat16)
    grad_now = factor[own, :] * (output - teacher[own, :].astype(jnp.float32))
    grad_output[local, :] = grad_now
    done[step] = grad_now.astype(jnp.bfloat16)


def finish_ffn_back(total, own, local, step, done, extra, kept):
    state, grad_output, gain = extra
    grad_state, gain_grad = kept
    input_grad, gain_now = normalize_back(state[local, :], gain[...], total)
    grad_now = grad_output[local, :] + input_grad
    grad_state[local, :] = grad_now
    gain_grad[step : step + 1, :] = gain_now[None, :]
    done[step] = grad_now.astype(jnp.bfloat16)


def finish_attn_back(total, own, local, step, done, extra, kept):
    tokens, grad_state, gain = extra
    (gain_grad,) = kept
    input_grad, gain_now = normalize_back(tokens[own, :].astype(jnp.float32), gain[...], total)
    gain_grad[step : step + 1, :] = gain_now[None, :]
    done[step] = (grad_state[local, :] + input_grad).astype(jnp.bfloat16)


def local_call(body, time, outs, operands, scratch=(), vmem=60):
    in_vmem = pl.BlockSpec(memory_space=pltpu.VMEM)
    return pl.pallas_call(
        body,
        out_shape=outs,
        in_specs=[in_vmem] * len(operands),
        out_specs=[in_vmem] * len(outs),
        scratch_shapes=list(scratch),
        compiler_params=pltpu.CompilerParams(vmem_limit_bytes=vmem << 20),
        cost_estimate=busy(time),
    )(*operands)


def ffn_body(normed, w_gate, w_up, w_down, gate, up, product, part, total):
    step = pl.program_id(0)
    gate_now = jnp.dot(normed[...], w_gate[...], preferred_element_type=jnp.float32)
    up_now = jnp.dot(normed[...], w_up[...], preferred_element_type=jnp.float32)
    gate[...] = gate_now
    up[...] = up_now
    product_now = (gate_now * jax.nn.sigmoid(gate_now) * up_now).astype(jnp.bfloat16)
    product[...] = product_now
    accumulate(step, total, part, times_transpose(product_now, w_down[...]))


def ffn_back_body(
    grad_rows, w_gate, w_up, w_down, gate, up, grad_gate, grad_up, part, total
):
    step = pl.program_id(0)
    grad_product = jnp.dot(grad_rows[...], w_down[...], preferred_element_type=jnp.float32)
    gate_now = gate[...]
    sigmoid_gate = jax.nn.sigmoid(gate_now)
    gate_low = (
        grad_product * up[...] * sigmoid_gate * (1.0 + gate_now * (1.0 - sigmoid_gate))
    ).astype(jnp.bfloat16)
    up_low = (grad_product * (gate_now * sigmoid_gate)).astype(jnp.bfloat16)
    grad_gate[...] = gate_low
    grad_up[...] = up_low
    accumulate(
        step,
        total,
        part,
        times_transpose(gate_low, w_gate[...]) + times_transpose(up_low, w_up[...]),
    )


def accumulate(step, total, part, term):
    last = pl.num_programs(0) - 1

    @pl.when(step == 0)
    def _():
        total[...] = term

    @pl.when((step > 0) & (step < last))
    def _():
        total[...] += term

    @pl.when(step == last)
    def _():
        part[...] = (total[...] + term).astype(jnp.bfloat16)


def by_units(body, rows_in, weights, by_columns, outs, time):
    rows, width = rows_in.shape
    units = weights[0].shape[1]
    block = min(UNIT_BLOCK, units)

    def columns(depth):
        return pl.BlockSpec((depth, block), lambda step: (0, step))

    whole = pl.BlockSpec((rows, width), lambda step: (0, 0))
    return pl.pallas_call(
        body,
        grid=(units // block,),
        out_shape=[jax.ShapeDtypeStruct((rows, units), kind) for kind in outs]
        + [jax.ShapeDtypeStruct((rows, width), jnp.bfloat16)],
        in_specs=[whole]
        + [columns(item.shape[0]) for item in weights]
        + [columns(rows) for _ in by_columns],
        out_specs=[columns(rows) for _ in outs] + [whole],
        scratch_shapes=[pltpu.VMEM((rows, width), jnp.float32)],
        compiler_params=pltpu.CompilerParams(vmem_limit_bytes=56 << 20),
        cost_estimate=busy(time),
    )(rows_in, *weights, *by_columns)


UNIT_BLOCK = 512


MIDDLE_BLOCK = 256


def finish_output_near(total, own, local, step, done, extra, kept):
    state, teacher, factor = extra
    output_low, grad_output = kept
    output = state[local, :] + total
    output_low[local, :] = output.astype(jnp.bfloat16)
    grad_now = factor[own, :] * (output - teacher[local, :].astype(jnp.float32))
    grad_output[local, :] = grad_now
    done[step] = grad_now.astype(jnp.bfloat16)


MIDDLE_ORDER = (
    "c", "c", "l1", "c", "l1", "c", "l1", "l1", "l1", "l1",
    "l1", "l1", "l1", "l1", "l1", "c", "c", "l1", "c", "l1",
    "l2", "l1", "c", "s0", "s0", "s0", "s0", "c", "l2", "c",
    "l1", "l2", "s1", "s1", "s1", "s1", "l2", "s0", "s0", "l2",
    "s1", "s1", "l2", "s0", "s0", "l2", "l2", "l2", "s1", "s1",
    "l2",
)


def middle_body(steps, order, *refs):
    refs = list(refs)

    def take(count):
        taken = refs[:count]
        del refs[:count]
        return taken

    state, factor, gains = take(3)
    normed_two, teacher, *weights = take(5)
    output_low, grad_up, grad_state, gain_parts = take(4)
    owned, squares = take(2), take(2)
    grad_ffn, grad_branch, inner_store = take(3)
    normed, product, grads_in, grad_gate, part, total, teacher_near = take(7)
    slots, kept_out, kept_in = take(3), *take(2)
    first_line, second_line = take(4), take(4)
    scatter_refs = [take(5), take(5)]
    weight_sems, store_sems, load_sems, row_sems = take(4)
    at_end, side, inner, outer = line_place()
    rows, width = normed.shape
    half, quarter = rows // 2, rows // 4
    units = weights[0].shape[1]
    block = MIDDLE_BLOCK
    blocks = units // block
    meet(True, True)

    def chunk_copy(source, target, chunk, sem):
        return [
            pltpu.make_async_copy(
                source.at[pl.ds(part_of * half + chunk * quarter, quarter)],
                target.at[pl.ds(chunk * half + part_of * quarter, quarter)],
                row_sems.at[sem + part_of],
            )
            for part_of in range(2)
        ]

    near_rows = pl.ds(pl.multiple_of(side * half, half), half)
    load_teacher = pltpu.make_async_copy(teacher.at[near_rows], teacher_near, row_sems.at[8])
    load_teacher.start()
    loads = chunk_copy(normed_two, normed, 0, 0) + chunk_copy(normed_two, normed, 1, 2)
    for load in loads:
        load.start()

    def columns(index):
        return pl.ds(pl.multiple_of(lax.rem(index, blocks) * block, block), block)

    def weight_copies(index):
        slot = lax.rem(index, 2)
        return [
            pltpu.make_async_copy(
                weight.at[:, columns(index)], item.at[slot], weight_sems.at[place, slot]
            )
            for place, (weight, item) in enumerate(zip(weights, slots))
        ]

    def store(index):
        slot = lax.rem(index, 2)
        return pltpu.make_async_copy(kept_out.at[slot], inner_store.at[index], store_sems.at[slot])

    def restore(index):
        slot = lax.rem(index, 2)
        return pltpu.make_async_copy(
            inner_store.at[index - 2 * blocks], kept_in.at[slot], load_sems.at[slot]
        )

    def fetch(index):
        for copy in weight_copies(index):
            copy.start()

        @pl.when(index >= 2 * blocks)
        def _():
            restore(index).start()

    def add_term(index, term):
        @pl.when(lax.rem(index, blocks) == 0)
        def _():
            total[...] = term

        @pl.when(lax.rem(index, blocks) > 0)
        def _():
            total[...] += term

    def put_part(chunk):
        for part_of in range(2):
            part[pl.ds(part_of * half + chunk * quarter, quarter), :] = total[
                pl.ds(part_of * quarter, quarter), :
            ].astype(jnp.bfloat16)

    def chunk_rows(chunk):
        return pl.ds(chunk * half, half)

    def forward(chunk, index):
        slot = lax.rem(index, 2)
        fetch(index + 1)
        for copy in weight_copies(index):
            copy.wait()
        gate = jnp.dot(
            normed[chunk_rows(chunk), :], slots[0][slot], preferred_element_type=jnp.float32
        )
        up = jnp.dot(
            normed[chunk_rows(chunk), :], slots[1][slot], preferred_element_type=jnp.float32
        )

        @pl.when(index >= 2)
        def _():
            store(index - 2).wait()

        kept_out[slot, 0] = gate
        kept_out[slot, 1] = up
        store(index).start()
        product_now = (gate * jax.nn.sigmoid(gate) * up).astype(jnp.bfloat16)
        product[chunk_rows(chunk), columns(index)] = product_now
        add_term(index, times_transpose(product_now, slots[2][slot]))

    def backward(chunk, index):
        slot = lax.rem(index, 2)

        @pl.when(index + 1 < 4 * blocks)
        def _():
            fetch(index + 1)

        for copy in weight_copies(index):
            copy.wait()
        restore(index).wait()
        grad_product = jnp.dot(
            grads_in[chunk_rows(chunk), :], slots[2][slot], preferred_element_type=jnp.float32
        )
        gate, up = kept_in[slot, 0], kept_in[slot, 1]
        sigmoid_gate = jax.nn.sigmoid(gate)
        gate_low = (
            grad_product * up * sigmoid_gate * (1.0 + gate * (1.0 - sigmoid_gate))
        ).astype(jnp.bfloat16)
        up_low = (grad_product * (gate * sigmoid_gate)).astype(jnp.bfloat16)
        grad_gate[chunk_rows(chunk), columns(index)] = gate_low
        for part_of in range(2):
            grad_up[pl.ds(part_of * half + chunk * quarter, quarter), columns(index)] = up_low[
                part_of * quarter : (part_of + 1) * quarter
            ]
        add_term(
            index,
            times_transpose(gate_low, slots[0][slot]) + times_transpose(up_low, slots[1][slot]),
        )

    def compute():
        fetch(jnp.int32(0))
        for load in loads:
            load.wait()
        for chunk in range(2):
            for piece in range(2):
                first = chunk * blocks + piece * blocks // 2

                @pl.loop(first, first + blocks // 2)
                def _(index):
                    forward(chunk, index)

                if piece == 1:
                    put_part(chunk)
                    if chunk == 0:
                        load_teacher.wait()
                yield
        store(jnp.int32(2 * blocks - 2)).wait()
        store(jnp.int32(2 * blocks - 1)).wait()
        for chunk in range(2):
            copies = chunk_copy(grad_ffn, grads_in, chunk, 4 + 2 * chunk)
            for copy in copies:
                copy.start()
            for copy in copies:
                copy.wait()
            yield
            for piece in range(2):
                first = (2 + chunk) * blocks + piece * blocks // 2

                @pl.loop(first, first + blocks // 2)
                def _(index):
                    backward(chunk, index)

                if piece == 1:
                    put_part(chunk)
                yield

    lists = {
        "c": compute(),
        "l1": line_events(
            steps, finish_output_near, part, (state, teacher_near, factor), grad_ffn,
            (output_low, grad_state), first_line, watch=True,
        ),
        "l2": line_events(
            steps, finish_ffn_back, part, (state, grad_state, gains.at[1:2]), grad_branch,
            (grad_state, gain_parts), second_line,
        ),
    }
    for place, (left, right) in enumerate(((grads_in, product), (normed, grad_gate))):
        lists[f"s{place}"] = scatter_events(
            left, right, owned[place], squares[place], scatter_refs[place]
        )
    weave([lists[name] for name in order + tuple(sorted(lists))])


def middle(state, factor, gains, normed_two, teacher, weights, steps, which):
    rows, width = normed_two.shape
    units = weights[0].shape[1]
    low = functools.partial(jax.ShapeDtypeStruct, dtype=jnp.bfloat16)
    full = functools.partial(jax.ShapeDtypeStruct, dtype=jnp.float32)
    in_vmem = pl.BlockSpec(memory_space=pltpu.VMEM)
    anywhere = pl.BlockSpec(memory_space=pl.ANY)
    held = [
        low((rows // 2, width)),
        low((rows, units)),
        full((rows // 2, width)),
        full((steps, width)),
    ]
    owned = [full((width // 8, units))] * 2 + [full((1, 128))] * 2
    blocks = units // MIDDLE_BLOCK
    inner = (2, rows // 2, MIDDLE_BLOCK)
    far = [low((rows, width)), low((rows, width)), full((2 * blocks,) + inner)]
    scratch = [
        pltpu.VMEM((rows, width), jnp.bfloat16),
        pltpu.VMEM((rows, units), jnp.bfloat16),
        pltpu.VMEM((rows, width), jnp.bfloat16),
        pltpu.VMEM((rows, units), jnp.bfloat16),
        pltpu.VMEM((rows, width), jnp.bfloat16),
        pltpu.VMEM((rows // 2, width), jnp.float32),
        pltpu.VMEM((rows // 2, width), jnp.bfloat16),
    ]
    scratch += [pltpu.VMEM((2, width, MIDDLE_BLOCK), jnp.bfloat16)] * 3
    scratch += [pltpu.VMEM((2,) + inner, jnp.float32)] * 2
    scratch += line_scratch(steps, rows, width) * 2
    scratch += scatter_scratch(width // 8, units) * 2
    scratch += [
        pltpu.SemaphoreType.DMA((3, 2)),
        pltpu.SemaphoreType.DMA((2,)),
        pltpu.SemaphoreType.DMA((2,)),
        pltpu.SemaphoreType.DMA((9,)),
    ]
    return pl.pallas_call(
        functools.partial(middle_body, steps, MIDDLE_ORDER),
        out_shape=held + owned + far,
        in_specs=[in_vmem] * 3 + [anywhere] * 5,
        out_specs=[in_vmem] * 8 + [anywhere] * 3,
        scratch_shapes=scratch,
        compiler_params=pltpu.CompilerParams(
            collective_id=which, has_side_effects=True, vmem_limit_bytes=63 << 20
        ),
        cost_estimate=busy(150),
    )(state, factor, gains, normed_two, teacher, *weights)


def turn(head_rows, cosine, sine_table):
    middle = head_rows.shape[0] // 2
    upper, lower = head_rows[:middle], head_rows[middle:]
    return jnp.concatenate(
        [upper * cosine - lower * sine_table, lower * cosine + upper * sine_table], axis=0
    )


def normalize_rows(tokens, gain, normed):
    @pl.loop(0, tokens.shape[0] // 64)
    def _(block):
        span = pl.ds(pl.multiple_of(block * 64, 64), 64)
        normed[span, :] = normalize(tokens[span, :].astype(jnp.float32), gain[...]).astype(
            jnp.bfloat16
        )


def project_rows(normed, weights, cosine, sine_table, query_t, pairs):
    q_cols = query_t.shape[0]
    k_cols = pairs.shape[1] // 2
    lin_t = jnp.dot(
        normed[...], weights[:, : q_cols + k_cols], preferred_element_type=jnp.float32
    ).T
    for first in range(0, q_cols, HD):
        query_t[first : first + HD, :] = turn(
            lin_t[first : first + HD], cosine[...], sine_table[...]
        ).astype(jnp.bfloat16)
    keys = [
        turn(lin_t[first : first + HD], cosine[...], sine_table[...])
        for first in range(q_cols, q_cols + k_cols, HD)
    ]
    pairs[:, :k_cols] = jnp.concatenate(keys, axis=0).T.astype(jnp.bfloat16)
    pairs[:, k_cols:] = jnp.dot(
        normed[...],
        weights[:, q_cols + k_cols : q_cols + 2 * k_cols],
        preferred_element_type=jnp.float32,
    ).astype(jnp.bfloat16)


def project_body(tokens, gain, weights, cosine, sine_table, normed, query_t, pairs):
    normalize_rows(tokens, gain, normed)
    project_rows(normed, weights, cosine, sine_table, query_t, pairs)


def split_pairs(pairs, keys, keys_t, values, values_t):
    heads = pairs.shape[1] // (2 * HD)
    for head in range(heads):
        part = pairs[:, head * HD : (head + 1) * HD]
        if keys is not None:
            keys[head] = part
        if keys_t is not None:
            keys_t[head] = part.astype(jnp.float32).T.astype(jnp.bfloat16)
        part = pairs[:, (heads + head) * HD : (heads + head + 1) * HD]
        if values is not None:
            values[head] = part
        if values_t is not None:
            values_t[head] = part.astype(jnp.float32).T.astype(jnp.bfloat16)


SCORE_FACTOR = float(HD) ** (-0.5) * LOG2E
KEY_BLOCK = 256


def lifted_scores(key_block, query_head, query_pos, key_pos):
    scores = jnp.dot(key_block, query_head, preferred_element_type=jnp.float32)
    return jnp.where(key_pos <= query_pos, scores * SCORE_FACTOR, NEG_FILL)


def attend_heads(
    heads, group, query_t, query_pos, key_pos, keys, values_t, lifted, mixed_t, low_t, stats
):
    rows = query_t.shape[1]
    blocks = keys.shape[1] // KEY_BLOCK

    @pl.loop(*heads)
    def _(head):
        span = pl.ds(pl.multiple_of(head * HD, HD), HD)
        shared = head // group
        query_head = query_t[span, :]

        def scan_scores(block, highest):
            keys_now = pl.ds(pl.multiple_of(block * KEY_BLOCK, KEY_BLOCK), KEY_BLOCK)
            scores = lifted_scores(
                keys[shared, keys_now, :], query_head, query_pos[...], key_pos[keys_now, :]
            )
            lifted[keys_now, :] = scores
            return jnp.maximum(highest, jnp.max(scores, axis=0, keepdims=True))

        highest = lax.fori_loop(
            0, blocks, scan_scores, jnp.full((1, rows), NEG_FILL, jnp.float32)
        )
        ceiling = jnp.floor(highest)

        def scan_values(block, state):
            weight_sum, mixed = state
            keys_now = pl.ds(pl.multiple_of(block * KEY_BLOCK, KEY_BLOCK), KEY_BLOCK)
            expo = jnp.exp2(lifted[keys_now, :] - ceiling)
            mixed = mixed + jnp.dot(
                values_t[shared, :, keys_now],
                expo.astype(jnp.bfloat16),
                preferred_element_type=jnp.float32,
            )
            return weight_sum + jnp.sum(expo, axis=0, keepdims=True), mixed

        weight_sum, mixed = lax.fori_loop(
            0,
            blocks,
            scan_values,
            (jnp.zeros((1, rows), jnp.float32), jnp.zeros((HD, rows), jnp.float32)),
        )
        mixed = mixed / weight_sum
        mixed_t[span, :] = mixed
        low_t[span, :] = mixed.astype(jnp.bfloat16).astype(jnp.float32)
        stats[head] = jnp.concatenate([ceiling, weight_sum], axis=0)


def branch_rows(low_t, w_out, mixed_low, part):
    mixed_low[...] = low_t[...].T.astype(jnp.bfloat16)

    @pl.loop(0, part.shape[1] // 512)
    def _(block):
        span = pl.ds(pl.multiple_of(block * 512, 512), 512)
        part[:, span] = times_transpose(mixed_low[...], w_out[span, :]).astype(jnp.bfloat16)


def attend_body(
    group, query_t, pairs, query_pos, key_pos, w_out, mixed_t, mixed_low, stats, part,
    keys, values_t, lifted, low_t,
):
    split_pairs(pairs, keys, None, None, values_t)
    attend_heads(
        (0, query_t.shape[0] // HD), group, query_t, query_pos, key_pos, keys, values_t,
        lifted, mixed_t, low_t, stats,
    )
    branch_rows(low_t, w_out, mixed_low, part)


FRONT_ORDER = (
    "gs", "gq", "gk", "gv", "c", "gs", "gs", "gs", "gs", "c",
    "gq", "gk", "gv", "go", "gq", "gk", "gv", "gz", "gq", "gk",
    "gv", "gq", "gk", "gv", "c", "go", "c", "ga", "go", "c",
    "go", "c", "c", "gu", "go", "c", "line", "line", "line", "line",
    "gz", "gz", "line", "gd", "line", "ga", "gu", "ga", "gu", "line",
    "line", "line", "gz", "line", "gd", "gz", "gd", "ga", "gu", "gd",
)


def front_body(steps, group, all_rows, order, *refs):
    refs = list(refs)

    def take(count):
        taken = refs[:count]
        del refs[:count]
        return taken

    stretch_order, lengths = take(2)
    tokens, cosine_all, sine_all, loss_mask, attn_gain, mlp_gain = take(6)
    shards = take(7)
    normed, query_t, pairs_out, mixed_t, mixed_low, stats, gains, state = take(8)
    cosine, sine_table, query_pos, key_pos, factor = take(5)
    normed_two, pack_out, out_whole, gate, up, down = take(6)
    pack, w_out, gain_tiles, pairs, keys, values_t, lifted, low_t, part = take(9)
    counts, gain_shard, count_shard = take(3)
    line_refs = take(4)
    gather_sems = take(9)
    (own_sems,) = take(1)
    ring, core, first, second, far = square_peers()
    rows, width = tokens.shape
    q_cols, k_cols = query_t.shape[0], pairs.shape[1] // 2
    heads = q_cols // HD
    half = rows // 2
    slot_len = key_pos.shape[0]

    def wide(row, depth):
        return jnp.broadcast_to(row.astype(jnp.float32), (depth, row.shape[1]))

    places = [stretch_order[0, 2 * core + piece] for piece in range(2)]
    row_index = lax.broadcasted_iota(jnp.int32, (1, rows), 1)
    query_pos[...] = row_index + jnp.where(
        row_index < half, places[0] * half, (places[1] - 1) * half
    )
    valid = jnp.where((loss_mask[...] == 1) & (query_pos[...] < lengths[0]), 1.0, 0.0)
    count = jnp.sum(valid)
    count_high = jnp.floor(count / 64.0)
    lane = lax.broadcasted_iota(jnp.int32, count_shard.shape, 1)
    count_shard[...] = jnp.where(lane < 128, count_high, count - 64.0 * count_high).astype(
        jnp.bfloat16
    )
    gain_shard[:16, :] = wide(attn_gain[...], 16).astype(jnp.bfloat16)
    gain_shard[16:, :] = wide(mlp_gain[...], 16).astype(jnp.bfloat16)
    shards = shards[:4] + [gain_shard] + shards[4:] + [count_shard]
    meet(True, True)

    def place_rows():
        key_index = lax.broadcasted_iota(jnp.int32, (slot_len, 1), 0)
        position = key_index
        for stretch in range(slot_len // half):
            inside = (key_index >= stretch * half) & (key_index < (stretch + 1) * half)
            moved = key_index + (stretch_order[0, stretch] - stretch) * half
            position = jnp.where(inside, moved, position)
        key_pos[...] = jnp.where(position < lengths[0], position, slot_len)
        for source, target in ((cosine_all, cosine), (sine_all, sine_table)):
            for piece in range(2):
                span = slice(piece * half, (piece + 1) * half)
                row = query_pos[:, span]
                table = source[:, :half]
                for stretch in range(1, slot_len // half):
                    first_place = stretch * half
                    table = jnp.where(
                        row >= first_place, source[:, first_place : first_place + half], table
                    )
                target[:, span] = table

    def pair_rows(which):
        return pl.ds(pl.multiple_of(which * rows, rows), rows)

    def swap_pairs(which):
        return pltpu.make_async_remote_copy(
            src_ref=pairs.at[pair_rows(which)],
            dst_ref=pairs.at[pair_rows(which)],
            send_sem=own_sems.at[0],
            recv_sem=own_sems.at[1],
            device_id={"context": 1 - core},
            device_id_type=MESH_ID,
        )

    keep_pack = pltpu.make_async_copy(pack, pack_out, own_sems.at[2])
    keep_out = pltpu.make_async_copy(w_out, out_whole, own_sems.at[3])

    def compute():
        place_rows()
        yield
        for row in range(2):
            gains[row : row + 1, :] = jnp.concatenate(
                [
                    gain_tiles[32 * owner + 16 * row : 32 * owner + 16 * row + 16, :].astype(
                        jnp.float32
                    )[:1]
                    for owner in range(8)
                ],
                axis=1,
            )
        normalize_rows(tokens, gains.at[0:1], normed)
        yield
        project_rows(normed, pack, cosine, sine_table, query_t, pairs.at[pair_rows(core)])
        swap_pairs(core).start()
        keep_pack.start()
        yield
        swap_pairs(1 - core).wait_recv()
        split_pairs(pairs, keys, None, None, values_t)
        pairs_out[...] = pairs[...]
        for chunk in range(4):
            attend_heads(
                (chunk * heads // 4, (chunk + 1) * heads // 4), group, query_t, query_pos,
                key_pos, keys, values_t, lifted, mixed_t, low_t, stats,
            )
            yield
        keep_out.start()
        branch_rows(low_t, w_out, mixed_low, part)
        yield
        swap_pairs(core).wait_send()
        keep_pack.wait()
        keep_out.wait()
        yield
        count_rows = sum(
            counts[16 * owner : 16 * owner + 16, :].astype(jnp.float32)[:1] for owner in range(8)
        )
        valid_count = 64.0 * jnp.max(count_rows[:, :128]) + jnp.max(count_rows[:, 128:])
        factor[...] = (all_rows / valid_count * wide(valid, 8)).T[:, :1]
        yield

    targets = [
        pack.at[:, pl.ds(0, q_cols)],
        pack.at[:, pl.ds(q_cols, k_cols)],
        pack.at[:, pl.ds(q_cols + k_cols, k_cols)],
        w_out,
        gain_tiles,
        gate,
        up,
        down,
        counts,
    ]
    lists = {
        name: gather_events(source, target, sems)
        for name, source, target, sems in zip(
            ("gq", "gk", "gv", "go", "gs", "ga", "gu", "gd", "gz"), shards, targets, gather_sems
        )
    }
    lists["c"] = compute()
    lists["line"] = line_events(
        steps, finish_branch, part, (tokens, gains.at[1:2]), normed_two, (state,), line_refs
    )
    weave([lists[name] for name in order + tuple(sorted(lists))])


def front(scalars, tokens, rows_in, shards, group, all_rows, steps, which):
    rows, width = tokens.shape
    slot_len = rows_in[0].shape[1]
    q_cols, k_cols = shards[0].shape[1], shards[1].shape[1]
    heads, kv_heads = q_cols // HD, k_cols // HD
    low = functools.partial(jax.ShapeDtypeStruct, dtype=jnp.bfloat16)
    full = functools.partial(jax.ShapeDtypeStruct, dtype=jnp.float32)
    in_vmem = pl.BlockSpec(memory_space=pltpu.VMEM)
    anywhere = pl.BlockSpec(memory_space=pl.ANY)
    pack_cols = q_cols + 2 * k_cols
    held = [
        low((rows, width)),
        low((q_cols, rows)),
        low((slot_len, 2 * k_cols)),
        full((q_cols, rows)),
        low((rows, q_cols)),
        full((heads, 2, rows)),
        full((2, width)),
        full((rows // 2, width)),
        full((HD // 2, rows)),
        full((HD // 2, rows)),
        jax.ShapeDtypeStruct((1, rows), jnp.int32),
        jax.ShapeDtypeStruct((slot_len, 1), jnp.int32),
        full((rows, 1)),
    ]
    far = [low((rows, width)), low((width, pack_cols)), low((width, q_cols))]
    far += [low((8 * item.shape[0], item.shape[1])) for item in shards[4:]]
    return pl.pallas_call(
        functools.partial(front_body, steps, group, all_rows, FRONT_ORDER),
        out_shape=held + far,
        in_specs=[pl.BlockSpec(memory_space=pltpu.SMEM)] * 2
        + [in_vmem] * 6
        + [anywhere] * len(shards),
        out_specs=[in_vmem] * len(held) + [anywhere] * len(far),
        scratch_shapes=[
            pltpu.VMEM((width, pack_cols), jnp.bfloat16),
            pltpu.VMEM((width, q_cols), jnp.bfloat16),
            pltpu.VMEM((8 * 32, width // 8), jnp.bfloat16),
            pltpu.VMEM((slot_len, 2 * k_cols), jnp.bfloat16),
            pltpu.VMEM((kv_heads, slot_len, HD), jnp.bfloat16),
            pltpu.VMEM((kv_heads, HD, slot_len), jnp.bfloat16),
            pltpu.VMEM((slot_len, rows), jnp.float32),
            pltpu.VMEM((q_cols, rows), jnp.float32),
            pltpu.VMEM((rows, width), jnp.bfloat16),
            pltpu.VMEM((8 * 16, 256), jnp.bfloat16),
            pltpu.VMEM((32, width // 8), jnp.bfloat16),
            pltpu.VMEM((16, 256), jnp.bfloat16),
        ]
        + line_scratch(steps, rows, width)
        + [pltpu.SemaphoreType.DMA((16,))] * 9
        + [pltpu.SemaphoreType.DMA((4,))],
        compiler_params=pltpu.CompilerParams(
            collective_id=which, has_side_effects=True, vmem_limit_bytes=60 << 20
        ),
        cost_estimate=busy(130),
    )(*scalars, tokens, *rows_in, *shards)


def prepare_back(grad_branch, w_out, query_t, queries, grad_t):
    queries_f = query_t[...].astype(jnp.float32).T
    for head in range(queries.shape[0]):
        queries[head] = queries_f[:, head * HD : (head + 1) * HD].astype(jnp.bfloat16)
    grad_t[...] = (
        jnp.dot(grad_branch[...], w_out[...], preferred_element_type=jnp.float32)
        .astype(jnp.bfloat16)
        .astype(jnp.float32)
        .T
    )


def attend_back_heads(
    heads, group, query_t, mixed_t, stats, query_pos, key_pos, cosine, sine_table, grad_pairs,
    keys, keys_t, values, queries, grad_t, turned,
):
    rows = query_t.shape[1]
    blocks = keys.shape[1] // KEY_BLOCK
    score_scale = float(HD) ** (-0.5)

    @pl.loop(*heads)
    def _(head):
        span = pl.ds(pl.multiple_of(head * HD, HD), HD)
        shared = head // group
        query_head = query_t[span, :]
        query_rows = queries[head]
        ceiling = stats[head, 0:1, :]
        inverse = 1.0 / stats[head, 1:2, :]
        grad_head = grad_t[span, :]
        delta = jnp.sum(grad_head * mixed_t[span, :], axis=0, keepdims=True)
        scaled = grad_head * inverse
        scaled_high = scaled.astype(jnp.bfloat16)
        scaled_low = (scaled - scaled_high.astype(jnp.float32)).astype(jnp.bfloat16)
        scaled_both = jnp.concatenate([scaled_high, scaled_low], axis=0)
        grad_head_low = grad_head.astype(jnp.bfloat16)

        def scan_keys(block, grad_query_t):
            keys_now = pl.ds(pl.multiple_of(block * KEY_BLOCK, KEY_BLOCK), KEY_BLOCK)
            scores = lifted_scores(
                keys[shared, keys_now, :], query_head, query_pos[...], key_pos[keys_now, :]
            )
            expo = jnp.exp2(scores - ceiling)
            value_term = times_transpose(expo.astype(jnp.bfloat16), scaled_both)
            grad_probs = jnp.dot(
                values[shared, keys_now, :], grad_head_low, preferred_element_type=jnp.float32
            )
            grad_scores = (expo * inverse * (grad_probs - delta)).astype(jnp.bfloat16)
            key_term = jnp.dot(grad_scores, query_rows, preferred_element_type=jnp.float32)
            grad_pairs[shared, keys_now, :] += jnp.concatenate(
                [key_term * score_scale, value_term[:, :HD] + value_term[:, HD:]], axis=1
            )
            return grad_query_t + jnp.dot(
                keys_t[shared, :, keys_now], grad_scores, preferred_element_type=jnp.float32
            )

        grad_query_t = lax.fori_loop(
            0, blocks, scan_keys, jnp.zeros((HD, rows), jnp.float32)
        )
        turned[span, :] = turn(grad_query_t * score_scale, cosine[...], -sine_table[...])


def attend_back_body(
    group, grad_branch, w_out, query_t, pairs, mixed_t, stats, query_pos, key_pos, cosine,
    sine_table, grad_query, grad_pairs, keys, keys_t, values, queries, grad_t, turned,
):
    split_pairs(pairs, keys, keys_t, values, None)
    prepare_back(grad_branch, w_out, query_t, queries, grad_t)
    grad_pairs[...] = jnp.zeros_like(grad_pairs)
    attend_back_heads(
        (0, queries.shape[0]), group, query_t, mixed_t, stats, query_pos, key_pos, cosine,
        sine_table, grad_pairs, keys, keys_t, values, queries, grad_t, turned,
    )
    grad_query[...] = turned[...].T.astype(jnp.bfloat16)


def join_rows(grad_query, pair_grads, cosine, sine_table, weights, grad_lin, part):
    q_cols = grad_query.shape[1]
    k_cols = HD * len(pair_grads)
    grad_lin[:, :q_cols] = grad_query
    keys = [turn(item.T[:HD], cosine[...], -sine_table[...]) for item in pair_grads]
    grad_lin[:, q_cols : q_cols + k_cols] = jnp.concatenate(keys, axis=0).T.astype(jnp.bfloat16)
    grad_lin[:, q_cols + k_cols :] = jnp.concatenate(
        [item[:, HD:] for item in pair_grads], axis=1
    ).astype(jnp.bfloat16)

    @pl.loop(0, part.shape[1] // 512)
    def _(block):
        span = pl.ds(pl.multiple_of(block * 512, 512), 512)
        part[:, span] = times_transpose(
            grad_lin[...], weights[span, : q_cols + 2 * k_cols]
        ).astype(jnp.bfloat16)


def join_body(grad_query, grad_pairs, cosine, sine_table, weights, grad_lin, part):
    pair_grads = [grad_pairs[head] for head in range(grad_pairs.shape[0])]
    join_rows(grad_query[...], pair_grads, cosine, sine_table, weights, grad_lin, part)


BACK_ORDER = (
    "y", "s0", "s0", "s0", "s0", "s0", "s0", "c", "s1", "s1",
    "s1", "s1", "s1", "s1", "c", "c", "c", "y", "c", "c",
    "s0", "s0", "s1", "s1", "line", "s2", "s2", "s2", "s2", "line",
    "s2", "s2", "line", "line", "s2", "s2", "line", "line", "line", "line",
    "y", "line",
)


def back_body(steps, group, order, *refs):
    refs = list(refs)

    def take(count):
        taken = refs[:count]
        del refs[:count]
        return taken

    cosine, sine_table, query_pos, key_pos = take(4)
    grad_branch, w_out, query_t, pairs, mixed_t, stats, gains = take(7)
    normed_two, grad_up, mixed_low = take(3)
    pooled = take(3)
    later = take(4)
    (half_low,) = take(1)
    owned = take(3)
    (totals,) = take(1)
    out, block_out = take(2)
    keys, keys_t, values, queries, grad_t, turned, grad_pairs, pairs_in, grad_lin, part = take(10)
    gain_parts = take(1)
    loaded = take(4)
    squares = take(3)
    line_refs = take(4)
    total_refs = take(3)
    scatter_refs = [take(5) for _ in range(3)]
    (own_sems,) = take(1)
    weights, tokens, grad_state, normed = loaded
    ring, core, first, second, far = square_peers()
    rows = query_t.shape[1]
    heads = queries.shape[0]
    meet(True, True, True)
    loads = [
        pltpu.make_async_copy(source, target, own_sems.at[2 + place])
        for place, (source, target) in enumerate(zip(later, loaded))
    ]
    for load in loads:
        load.start()

    def own_rows(which):
        return pl.ds(pl.multiple_of(which * rows, rows), rows)

    swap = pltpu.make_async_remote_copy(
        src_ref=grad_pairs.at[:, own_rows(1 - core)],
        dst_ref=pairs_in,
        send_sem=own_sems.at[0],
        recv_sem=own_sems.at[1],
        device_id={"context": 1 - core},
        device_id_type=MESH_ID,
    )

    def compute():
        split_pairs(pairs, keys, keys_t, values, None)
        prepare_back(grad_branch, w_out, query_t, queries, grad_t)
        grad_pairs[...] = jnp.zeros_like(grad_pairs)
        yield
        for chunk in range(4):
            attend_back_heads(
                (chunk * heads // 4, (chunk + 1) * heads // 4), group, query_t, mixed_t, stats,
                query_pos, key_pos, cosine, sine_table, grad_pairs, keys, keys_t, values,
                queries, grad_t, turned,
            )
            yield
        swap.start()
        for load in loads:
            load.wait()
        grad_query = turned[...].T.astype(jnp.bfloat16)
        swap.wait_recv()
        pair_grads = [
            grad_pairs[head, own_rows(core), :] + pairs_in[head] for head in range(keys.shape[0])
        ]
        join_rows(grad_query, pair_grads, cosine, sine_table, weights, grad_lin, part)
        yield
        swap.wait_send()
        yield

    at_end, side, inner, outer = line_place()
    in_middle = jnp.logical_not(at_end)

    def spread():
        half = half_low.shape[0]
        near = block_out.at[pl.ds(pl.multiple_of(side * half, half), half)]
        far = block_out.at[pl.ds(pl.multiple_of((1 - side) * half, half), half)]

        def hand(source, target, send, recv, device):
            return pltpu.make_async_remote_copy(
                src_ref=source,
                dst_ref=target,
                send_sem=own_sems.at[send],
                recv_sem=own_sems.at[recv],
                device_id=device,
                device_id_type=MESH_ID,
            )

        to_outer = hand(half_low, near, 6, 7, outer)
        to_inner = hand(half_low, near, 8, 9, inner)
        onward = hand(far, far, 10, 9, outer)
        keep = pltpu.make_async_copy(half_low, near, own_sems.at[11])

        @pl.when(in_middle)
        def _():
            to_outer.start()
            to_inner.start()
            keep.start()

        yield

        @pl.when(in_middle)
        def _():
            to_inner.wait_recv()
            onward.start()

        yield

        @pl.when(in_middle)
        def _():
            to_outer.wait_send()
            to_inner.wait_send()
            onward.wait_send()
            keep.wait()

        @pl.when(at_end)
        def _():
            to_outer.wait_recv()
            onward.wait_recv()

        yield

    pairs_of = ((normed_two, grad_up), (grad_branch, mixed_low), (normed, grad_lin))
    lists = {
        f"s{place}": scatter_events(left, right, owned[place], squares[place], scatter_refs[place])
        for place, (left, right) in enumerate(pairs_of)
    }
    lists["c"] = compute()
    lists["y"] = spread()
    lists["line"] = line_events(
        steps, finish_attn_back, part, (tokens, grad_state, gains.at[0:1]), out, gain_parts,
        line_refs,
    )
    weave([lists[name] for name in order + tuple(sorted(lists))])
    own_row = total_refs[0].at[0]
    width = gains.shape[1]
    own_row[:, :width] = jnp.sum(gain_parts[0][...], axis=0, keepdims=True)
    own_row[:, width : 2 * width] = jnp.sum(pooled[0][...], axis=0, keepdims=True)
    own_row[:, 2 * width :] = sum(item[...] for item in (*pooled[1:], *squares))
    total_everywhere(totals, *total_refs)


def back(tables, held, factors, pooled, later, half_low, group, steps, which):
    query_t, pairs = held[2], held[3]
    q_cols, rows = query_t.shape
    slot_len, k_cols = pairs.shape[0], pairs.shape[1] // 2
    kv_heads, heads = k_cols // HD, q_cols // HD
    width = held[0].shape[1]
    pack_cols = q_cols + 2 * k_cols
    full = functools.partial(jax.ShapeDtypeStruct, dtype=jnp.float32)
    in_vmem = pl.BlockSpec(memory_space=pltpu.VMEM)
    anywhere = pl.BlockSpec(memory_space=pl.ANY)
    shard_rows = width // 8
    owned = [full((shard_rows, cols)) for cols in (factors[1].shape[1], q_cols, pack_cols)]
    pool_width = 2 * width + 128
    near = (*tables, *held, *factors, *pooled)
    scratch = [
        pltpu.VMEM((kv_heads, slot_len, HD), jnp.bfloat16),
        pltpu.VMEM((kv_heads, HD, slot_len), jnp.bfloat16),
        pltpu.VMEM((kv_heads, slot_len, HD), jnp.bfloat16),
        pltpu.VMEM((heads, rows, HD), jnp.bfloat16),
        pltpu.VMEM((q_cols, rows), jnp.float32),
        pltpu.VMEM((q_cols, rows), jnp.float32),
        pltpu.VMEM((kv_heads, slot_len, 2 * HD), jnp.float32),
        pltpu.VMEM((kv_heads, rows, 2 * HD), jnp.float32),
        pltpu.VMEM((rows, pack_cols), jnp.bfloat16),
        pltpu.VMEM((rows, width), jnp.bfloat16),
        pltpu.VMEM((steps, width), jnp.float32),
    ]
    scratch += [pltpu.VMEM(item.shape, item.dtype) for item in later]
    scratch += [pltpu.VMEM((1, 128), jnp.float32)] * 3
    scratch += line_scratch(steps, rows, width) + total_scratch(pool_width)
    for item in owned:
        scratch += scatter_scratch(*item.shape)
    return pl.pallas_call(
        functools.partial(back_body, steps, group, BACK_ORDER),
        out_shape=owned
        + [full((1, pool_width))]
        + [jax.ShapeDtypeStruct((rows, width), jnp.bfloat16)] * 2,
        in_specs=[in_vmem] * len(near) + [anywhere] * (len(later) + 1),
        out_specs=[in_vmem] * 4 + [anywhere] * 2,
        scratch_shapes=scratch + [pltpu.SemaphoreType.DMA((12,))],
        compiler_params=pltpu.CompilerParams(
            collective_id=which, has_side_effects=True, vmem_limit_bytes=62 << 20
        ),
        cost_estimate=busy(110),
    )(*near, *later, half_low)


def on_device(
    tokens,
    teacher,
    lengths,
    loss_mask,
    stretch_order,
    attn_gain,
    w_query,
    w_key,
    w_value,
    w_out,
    mlp_gain,
    w_gate,
    w_up,
    w_down,
    first_moment,
    second_moment,
    gain_first,
    gain_second,
):
    slot_count, stretch_len, model_width = tokens.shape
    token_rows = slot_count * stretch_len
    half_len = stretch_len // 2
    slot_len = stretch_len * lax.axis_size("context")
    all_rows = slot_count * lax.axis_size("dp") * slot_len
    steps = 4
    share_rows = token_rows // 2
    shard_rows = attn_gain.shape[0]
    q_cols, k_cols = w_query.shape[1], w_key.shape[1]
    square = lax.axis_size("dp") == 4 and lax.axis_size("context") == 2
    head_count = q_cols // HD
    kv_count = k_cols // HD
    group_size = head_count // kv_count
    token_rows_low = tokens.reshape(token_rows, model_width)
    low = functools.partial(jax.ShapeDtypeStruct, dtype=jnp.bfloat16)
    full = functools.partial(jax.ShapeDtypeStruct, dtype=jnp.float32)
    shard_f32 = full((share_rows, model_width))
    shard_low = low((share_rows, model_width))
    gain_parts = full((steps, model_width))
    line = functools.partial(line_sum, steps=steps)
    teacher_rows = teacher.reshape(token_rows, model_width)
    if square:
        angles = frequencies()[:, None] * jnp.arange(slot_len, dtype=jnp.float32)[None, :]
        (
            normed, query_t, pairs, mixed_t, mixed_low, stats, gains, state, cosine, sine_table,
            query_row, key_pos, factor, normed_two, first_pack, full_out, full_gate, full_up,
            full_down,
        ) = front(
            (stretch_order, lengths),
            token_rows_low,
            (
                jnp.cos(angles), jnp.sin(angles), loss_mask, attn_gain[None, :],
                mlp_gain[None, :],
            ),
            (w_query, w_key, w_value, w_out, w_gate, w_up, w_down),
            group_size,
            float(all_rows),
            steps,
            0,
        )
    else:
        local_index = stretch_len * lax.axis_index("context") + jnp.arange(
            stretch_len, dtype=jnp.int32
        )
        query_pos = positions_of(stretch_order, local_index, half_len)
        valid = ((loss_mask == 1) & (query_pos < lengths[:, None])).astype(jnp.float32)
        valid_count = lax.psum(jnp.sum(valid), ("dp", "context"))
        factor = jnp.float32(all_rows) / valid_count * valid.reshape(token_rows, 1)
        angles = frequencies()[:, None] * query_pos.reshape(1, token_rows).astype(jnp.float32)
        cosine, sine_table = jnp.cos(angles), jnp.sin(angles)
        key_pos = positions_of(stretch_order, jnp.arange(slot_len, dtype=jnp.int32), half_len)
        key_pos = jnp.where(key_pos < lengths[:, None], key_pos, slot_len).reshape(slot_len, 1)
        query_row = query_pos.reshape(1, token_rows)
        whole = functools.partial(
            lax.all_gather, axis_name=("dp", "context"), axis=0, tiled=True
        )
        first_pack = whole(jnp.concatenate([w_query, w_key, w_value], axis=1))
        full_out, full_gate, full_up, full_down = (
            whole(item) for item in (w_out, w_gate, w_up, w_down)
        )
        gain_one, gain_two = (
            whole(item)[None, :].astype(jnp.float32) for item in (attn_gain, mlp_gain)
        )
        normed, query_t, pairs_here = local_call(
            project_body,
            8,
            [
                low((token_rows, model_width)),
                low((q_cols, token_rows)),
                low((token_rows, 2 * k_cols)),
            ],
            [token_rows_low, gain_one, first_pack, cosine, sine_table],
        )
        pairs = lax.all_gather(pairs_here, "context", axis=0, tiled=True)
        mixed_t, mixed_low, stats, branch_part = local_call(
            functools.partial(attend_body, group_size),
            20,
            [
                full((q_cols, token_rows)),
                low((token_rows, q_cols)),
                full((head_count, 2, token_rows)),
                low((token_rows, model_width)),
            ],
            [query_t, pairs, query_row, key_pos, full_out],
            [
                pltpu.VMEM((kv_count, slot_len, HD), jnp.bfloat16),
                pltpu.VMEM((kv_count, HD, slot_len), jnp.bfloat16),
                pltpu.VMEM((slot_len, token_rows), jnp.float32),
                pltpu.VMEM((q_cols, token_rows), jnp.float32),
            ],
        )
        normed_two, state = line(
            finish_branch, branch_part, (token_rows_low, gain_two), [shard_f32], 0
        )
    if square:
        (
            output_low, grad_up, grad_state, gain_two_parts, owned_down, owned_gate,
            squares_down, squares_gate, _, grad_branch, _,
        ) = middle(
            state, factor, gains, normed_two, teacher_rows, (full_gate, full_up, full_down),
            steps, 1,
        )
        owned_up, owned_out, owned_qkv, totals, grad_tokens, block_out = back(
            (cosine, sine_table, query_row, key_pos),
            (grad_branch, full_out, query_t, pairs, mixed_t, stats, gains),
            (normed_two, grad_up, mixed_low),
            (gain_two_parts, squares_down, squares_gate),
            (first_pack, token_rows_low, grad_state, normed),
            output_low,
            group_size,
            steps,
            3,
        )
    else:
        gate, up, product, output_part = by_units(
            ffn_body,
            normed_two,
            [full_gate, full_up, full_down],
            [],
            [jnp.float32, jnp.float32, jnp.bfloat16],
            18,
        )
        grad_ffn, output_low, grad_output = line(
            finish_output, output_part, (state, teacher_rows, factor), [shard_low, shard_f32], 1
        )
        outward = [(1, 0), (2, 3)]
        own_half = lax.ppermute(output_low, "tensor", outward)
        crossed_half = lax.ppermute(output_low, "tensor", [(1, 2), (2, 1)])
        other_half = lax.ppermute(crossed_half, "tensor", outward)
        block_out = join_halves(output_low, own_half, crossed_half, other_half)
        grad_gate, grad_up, normed_part = by_units(
            ffn_back_body,
            grad_ffn,
            [full_gate, full_up, full_down],
            [gate, up],
            [jnp.bfloat16, jnp.bfloat16],
            18,
        )

        def owned(left, right):
            return lax.psum_scatter(
                column_term(left, right).astype(jnp.bfloat16),
                ("dp", "context"),
                scatter_dimension=0,
                tiled=True,
            ).astype(jnp.float32)

        owned_down = owned(grad_ffn, product)
        owned_gate = owned(normed_two, grad_gate)
        owned_up = owned(normed_two, grad_up)
        grad_branch, grad_state, gain_two_parts = line(
            finish_ffn_back, normed_part, (state, grad_output, gain_two), [shard_f32, gain_parts], 2
        )
        owned_out = owned(grad_branch, mixed_low)
        grad_query, grad_pairs = local_call(
            functools.partial(attend_back_body, group_size),
            24,
            [low((token_rows, q_cols)), full((kv_count, slot_len, 2 * HD))],
            [
                grad_branch, full_out, query_t, pairs, mixed_t, stats, query_row, key_pos,
                cosine, sine_table,
            ],
            [
                pltpu.VMEM((kv_count, slot_len, HD), jnp.bfloat16),
                pltpu.VMEM((kv_count, HD, slot_len), jnp.bfloat16),
                pltpu.VMEM((kv_count, slot_len, HD), jnp.bfloat16),
                pltpu.VMEM((head_count, token_rows, HD), jnp.bfloat16),
                pltpu.VMEM((q_cols, token_rows), jnp.float32),
                pltpu.VMEM((q_cols, token_rows), jnp.float32),
            ],
        )
        grad_pairs_own = lax.psum_scatter(
            grad_pairs, "context", scatter_dimension=1, tiled=True
        )
        grad_lin, inputs_part = local_call(
            join_body,
            6,
            [low((token_rows, q_cols + 2 * k_cols)), low((token_rows, model_width))],
            [grad_query, grad_pairs_own, cosine, sine_table, first_pack],
        )
        owned_qkv = owned(normed, grad_lin)
        grad_tokens, gain_one_parts = line(
            finish_attn_back, inputs_part, (token_rows_low, grad_state, gain_one), [gain_parts], 3
        )
    owned_all = [owned_qkv, owned_out, owned_gate, owned_up, owned_down]
    gain_cols = 2 * model_width
    if not square:
        square_local = sum(jnp.sum(part * part) for part in owned_all)
        totals = lax.psum(
            jnp.concatenate(
                [
                    jnp.sum(gain_one_parts, axis=0),
                    jnp.sum(gain_two_parts, axis=0),
                    jnp.full((128,), square_local / 128.0),
                ]
            )[None, :],
            ("dp", "context", "tensor"),
        )
    gains_owned = lax.dynamic_slice_in_dim(
        totals[0, :gain_cols].reshape(2, model_width),
        lax.axis_index(("dp", "context")) * shard_rows,
        shard_rows,
        1,
    )
    widths = (q_cols, k_cols, k_cols) + tuple(item.shape[1] for item in owned_all[1:])
    *matrices, adam_step, gain_one_grad, gain_two_grad, gain_step = update_rows(
        owned_all,
        first_moment,
        second_moment,
        totals,
        (gains_owned, gain_first, gain_second),
        gain_cols,
        widths,
    )
    return (
        block_out.reshape(slot_count, stretch_len, model_width),
        grad_tokens.reshape(slot_count, stretch_len, model_width),
        gain_one_grad[0],
        matrices[0],
        matrices[1],
        matrices[2],
        matrices[3],
        gain_two_grad[0],
        matrices[4],
        matrices[5],
        matrices[6],
        adam_step,
        gain_step,
    )


def solution(mesh):
    in_specs = (
        P("dp", "context", None),
        P("dp", "context", None),
        P("dp"),
        P("dp", "context"),
        P("dp", None),
        P(("dp", "context")),
        P(("dp", "context"), "tensor"),
        P(("dp", "context"), "tensor"),
        P(("dp", "context"), "tensor"),
        P(("dp", "context"), "tensor"),
        P(("dp", "context")),
        P(("dp", "context"), "tensor"),
        P(("dp", "context"), "tensor"),
        P(("dp", "context"), "tensor"),
        P(("dp", "context"), "tensor"),
        P(("dp", "context"), "tensor"),
        P(None, ("dp", "context")),
        P(None, ("dp", "context")),
    )
    out_specs = (
        P("dp", "context", None),
        P("dp", "context", None),
        P(("dp", "context")),
        P(("dp", "context"), "tensor"),
        P(("dp", "context"), "tensor"),
        P(("dp", "context"), "tensor"),
        P(("dp", "context"), "tensor"),
        P(("dp", "context")),
        P(("dp", "context"), "tensor"),
        P(("dp", "context"), "tensor"),
        P(("dp", "context"), "tensor"),
        P(("dp", "context"), "tensor"),
        P(None, ("dp", "context")),
    )
    return jax.shard_map(
        on_device, mesh=mesh, in_specs=in_specs, out_specs=out_specs, check_vma=False
    )
```
